1024 devices in a mesh: bx: 16 (over y, x), by: 64 (over z, core).
Axes of the slice: x: 4, y: 4, z: 32, core: 2. Of those that a mesh axis runs over, the one named last changes fastest.
Arguments:
- populations: float32 [19, 128, 65536], P(None, 'bx', 'by')
- cover_codes: int32 [2, 128, 65536], P(None, 'bx', 'by'), may hold values from 0 to 9215, as said below
- sphere_cell: int32 [3, 16, 64, 4], P(None, 'bx', 'by'), may hold values from 0 to 63, as said below
- sphere_velocity: float32 [3, 16, 64, 4], P(None, 'bx', 'by'), may hold values from -0.08 to 0.08
- sphere_spin: float32 [3, 16, 64, 4], P(None, 'bx', 'by'), may hold values from -0.01 to 0.01
- relax_rates: float32 [15], replicated, may hold values from 0.7 to 1.9
Outputs:
- populations_next: float32 [19, 128, 65536], P(None, 'bx', 'by')
- sphere_load: float32 [6, 16, 64, 4], P(None, 'bx', 'by')
The draws below stay inside these ranges and needn't reach their ends.
Inputs may be any that keep to these rules, and one draw needn't show every extreme that they name: `sphere_cell`: centres lie in their block, with z in [8, 56). `cover_codes`: the slot of a layer with a nonzero level names a sphere whose centre is within 9 cells of the cell; the two layers of a cell name different slots and their levels sum to 255 or less; slot is below 36.
All inputs are finite; a program needn't handle non-finite values.
Results may differ from the reference program's by a relative error of at most 0.0003.
Values sent between devices are 32-bit elements; how exact they have to be, the bound alone decides.
A program may use at most 32 MiB of HBM per device.

```python
import math
import jax
import jax.numpy as jnp
import numpy as np
from jax import lax

Q = 19
CX = 8
CY = 16
NZ = 64
RADIUS = 8
SPB = 4
BLOCKS_X = 16
BLOCKS_Y = 64
NX = 128
NY = 1024


def sphere_positions(key):
    key_x, key_y, key_z = jax.random.split(key, 3)
    layout = (BLOCKS_X, BLOCKS_Y, SPB)
    place_x = jax.random.randint(key_x, layout, 0, CX)
    place_y = jax.random.randint(key_y, layout, 0, CY)
    place_z = jax.random.randint(key_z, layout, RADIUS, NZ - RADIUS)
    return jnp.stack([place_x, place_y, place_z]).astype(jnp.int32)


def draw_sphere_cell(key, part):
    centers = sphere_positions(key)
    return centers


def draw_cover_codes(key, part):
    centers = sphere_positions(key)
    slots = 9 * SPB
    slot_ids = jnp.arange(slots, dtype=jnp.int32)
    cell_x = jnp.arange(CX, dtype=jnp.int32)[None, :, None, None]
    cell_y = jnp.arange(CY, dtype=jnp.int32)[None, None, :, None]
    cell_z = jnp.arange(NZ, dtype=jnp.int32)[None, None, None, :]

    def one_block(block_id):
        row_x = block_id // BLOCKS_Y
        row_y = block_id % BLOCKS_Y
        gathered = []
        for off_x in range(3):
            for off_y in range(3):
                picked = centers[:, (row_x + off_x - 1) % BLOCKS_X, (row_y + off_y - 1) % BLOCKS_Y, :]
                moved = picked + jnp.array([(off_x - 1) * CX, (off_y - 1) * CY, 0], jnp.int32)[:, None]
                gathered.append(moved)
        middle = jnp.concatenate(gathered, axis=1)
        diff_x = cell_x - middle[0][:, None, None, None]
        diff_y = cell_y - middle[1][:, None, None, None]
        diff_z = cell_z - middle[2][:, None, None, None]
        distance = diff_x * diff_x + diff_y * diff_y + diff_z * diff_z
        ranked = distance * 256 + slot_ids[:, None, None, None]
        first = jnp.min(ranked, axis=0)
        second = jnp.min(jnp.where(ranked == first[None], 1073741824, ranked), axis=0)
        level_one = jnp.clip((RADIUS * RADIUS + RADIUS - first // 256) * 255 // (2 * RADIUS), 0, 255)
        level_two = jnp.clip((RADIUS * RADIUS + RADIUS - second // 256) * 255 // (2 * RADIUS), 0, 255)
        level_two = jnp.minimum(level_two, 255 - level_one)
        codes = jnp.stack([first % 256 * 256 + level_one, second % 256 * 256 + level_two])
        return codes.reshape(2, CX, CY * NZ).astype(jnp.int32)
    blocks = lax.map(one_block, jnp.arange(BLOCKS_X * BLOCKS_Y, dtype=jnp.int32))
    return blocks.reshape(BLOCKS_X, BLOCKS_Y, 2, CX, CY * NZ).transpose(2, 0, 3, 1, 4).reshape(2, NX, NY * NZ)


def draw_populations(key, part):
    key = jax.random.fold_in(key, 5)
    weights = jnp.array([1.0 / 3.0] + [1.0 / 18.0] * 6 + [1.0 / 36.0] * 12, jnp.float32)[:, None, None]
    spread = jax.random.uniform(key, (Q, NX, NY * NZ), jnp.float32, 0.7, 1.3)
    return (weights * spread).astype(jnp.float32)


def shard_levels(rng, extent, cuts, smallest, top_value):
    loudness, own = 1.0, jax.random.fold_in(rng, 6)
    for dim, blocks in cuts:
        steps = jnp.exp(jax.random.uniform(jax.random.fold_in(own, dim), (blocks,), jnp.float32, smallest / len(cuts), top_value / len(cuts)))
        loudness = loudness * jnp.repeat(steps, extent[dim] // blocks).reshape([-1 if axis == dim else 1 for axis in range(len(extent))])
    return loudness


def setup_inputs(seed: int = 0) -> dict:
    splits = jax.random.split(jax.random.key(seed), 7)
    return {
        "populations": draw_populations(jax.random.fold_in(splits[6], 71), 0),
        "cover_codes": draw_cover_codes(jax.random.fold_in(splits[6], 71), 0),
        "sphere_cell": draw_sphere_cell(jax.random.fold_in(splits[6], 71), 0),
        "sphere_velocity": jnp.clip(jax.random.uniform(splits[3], (3, BLOCKS_X, BLOCKS_Y, SPB), jnp.float32, -0.08, 0.08) * shard_levels(splits[3], (3, BLOCKS_X, BLOCKS_Y, SPB), ((1, 16), (2, 64)), -0.4, 0.0), -0.08, 0.08),
        "sphere_spin": jnp.clip(jax.random.uniform(splits[4], (3, BLOCKS_X, BLOCKS_Y, SPB), jnp.float32, -0.01, 0.01) * shard_levels(splits[4], (3, BLOCKS_X, BLOCKS_Y, SPB), ((1, 16), (2, 64)), -0.4, 0.0), -0.01, 0.01),
        "relax_rates": jnp.clip(jnp.exp(jax.random.uniform(splits[5], (15,), jnp.float32, math.log(0.7), math.log(1.9))), 0.7, 1.9),
    }


VELOCITIES = np.array([[0, 0, 0], [1, 0, 0], [-1, 0, 0], [0, 1, 0], [0, -1, 0], [0, 0, 1], [0, 0, -1], [1, 1, 0], [-1, -1, 0], [1, -1, 0], [-1, 1, 0], [1, 0, 1], [-1, 0, -1], [1, 0, -1], [-1, 0, 1], [0, 1, 1], [0, -1, -1], [0, 1, -1], [0, -1, 1]])
WEIGHTS = np.array([1.0 / 3.0] + [1.0 / 18.0] * 6 + [1.0 / 36.0] * 12)
OPPOSITE = [0, 2, 1, 4, 3, 6, 5, 8, 7, 10, 9, 12, 11, 14, 13, 16, 15, 18, 17]
FRACTION_LEVELS = 255.0

def moment_rows():
    vel_x, vel_y, vel_z = [VELOCITIES[:, component] * 1.0 for component in range(3)]
    monomials = [np.ones(19), vel_x, vel_y, vel_z, vel_x * vel_x, vel_y * vel_y, vel_z * vel_z, vel_x * vel_y, vel_x * vel_z, vel_y * vel_z, vel_x * vel_x * vel_y, vel_x * vel_x * vel_z, vel_y * vel_y * vel_x, vel_y * vel_y * vel_z, vel_z * vel_z * vel_x, vel_z * vel_z * vel_y, vel_x * vel_x * vel_y * vel_y, vel_x * vel_x * vel_z * vel_z, vel_y * vel_y * vel_z * vel_z]
    orthonormal = []
    for vector in monomials:
        vector = vector.copy()
        for earlier in orthonormal:
            vector = vector - np.dot(earlier, vector) * earlier
        orthonormal.append(vector / np.sqrt(np.dot(vector, vector)))
    return np.stack(orthonormal)

def collision_matrix(relax_rates):
    moments = jnp.asarray(moment_rows(), jnp.float32)
    rate_full = jnp.concatenate([jnp.zeros((4,), jnp.float32), relax_rates.astype(jnp.float32)])
    return jnp.dot(moments.T * rate_full[None, :], moments, precision=lax.Precision.HIGHEST)

def equilibrium(density, vel_x, vel_y, vel_z):
    square = vel_x * vel_x + vel_y * vel_y + vel_z * vel_z
    pieces = []
    for pop_index in range(19):
        aligned = float(VELOCITIES[pop_index, 0]) * vel_x + float(VELOCITIES[pop_index, 1]) * vel_y + float(VELOCITIES[pop_index, 2]) * vel_z
        pieces.append(float(WEIGHTS[pop_index]) * density * (1.0 + 3.0 * aligned + 4.5 * aligned * aligned - 1.5 * square))
    return jnp.stack(pieces)

def project_on(values, component):
    running = jnp.zeros(values.shape[1:], jnp.float32)
    for pop_index in range(19):
        factor = int(VELOCITIES[pop_index, component])
        if factor != 0:
            running = running + float(factor) * values[pop_index]
    return running

def collide_block(populations, cover_codes, slot_rows, relax_rates):
    width_x = populations.shape[1]
    flat_cells = populations.shape[2]
    width_y = flat_cells // NZ
    slots = slot_rows.shape[0]
    per_block = slots // 9
    slot_ids = jnp.arange(slots, dtype=jnp.int32)
    shift_x = (slot_ids // (3 * per_block) - 1).astype(jnp.float32) * float(width_x)
    shift_y = (slot_ids // per_block % 3 - 1).astype(jnp.float32) * float(width_y)
    columns = [slot_rows[:, 0] + shift_x, slot_rows[:, 1] + shift_y] + [slot_rows[:, component] for component in range(2, 9)]
    slot_table = jnp.stack(columns)
    flat_ids = jnp.arange(flat_cells, dtype=jnp.int32)
    cell_x = jnp.broadcast_to(jnp.arange(width_x, dtype=jnp.int32).astype(jnp.float32)[:, None], (width_x, flat_cells))
    cell_y = jnp.broadcast_to((flat_ids // NZ).astype(jnp.float32)[None, :], (width_x, flat_cells))
    cell_z = jnp.broadcast_to((flat_ids % NZ).astype(jnp.float32)[None, :], (width_x, flat_cells))
    density = lax.optimization_barrier(jnp.sum(populations, axis=0))
    flow_x = project_on(populations, 0) / density
    flow_y = project_on(populations, 1) / density
    flow_z = project_on(populations, 2) / density
    balance = equilibrium(density, flow_x, flow_y, flow_z)
    relax_matrix = collision_matrix(relax_rates)
    fluid_term = -jnp.einsum('ij,jxc->ixc', relax_matrix, populations - balance, precision=lax.Precision.HIGHEST)
    collided = populations + fluid_term
    mirror = jnp.stack([populations[other] - balance[other] for other in OPPOSITE])
    slot_loads = jnp.zeros((slots, 6), jnp.float32)
    radius_two = float(RADIUS * RADIUS)
    radius_three = float(RADIUS * RADIUS * RADIUS)
    for cover_layer in range(2):
        packed = cover_codes[cover_layer]
        slot_of = packed // 256
        fraction = (packed % 256).astype(jnp.float32) / FRACTION_LEVELS
        onehot = (slot_of[None, :, :] == slot_ids[:, None, None]).astype(jnp.float32)
        values = jnp.einsum('ks,sxc->kxc', slot_table, onehot, precision=lax.Precision.HIGHEST)
        rel_x = cell_x - values[0]
        rel_y = cell_y - values[1]
        rel_z = cell_z - values[2]
        wall_x = values[3] + values[7] * rel_z - values[8] * rel_y
        wall_y = values[4] + values[8] * rel_x - values[6] * rel_z
        wall_z = values[5] + values[6] * rel_y - values[7] * rel_x
        solid_term = mirror + equilibrium(density, wall_x, wall_y, wall_z) - populations
        collided = collided + fraction[None] * (solid_term - fluid_term)
        force_x = -fraction * project_on(solid_term, 0)
        force_y = -fraction * project_on(solid_term, 1)
        force_z = -fraction * project_on(solid_term, 2)
        torque_x = rel_y * force_z - rel_z * force_y
        torque_y = rel_z * force_x - rel_x * force_z
        torque_z = rel_x * force_y - rel_y * force_x
        contrib = jnp.stack([force_x / radius_two, force_y / radius_two, force_z / radius_two, torque_x / radius_three, torque_y / radius_three, torque_z / radius_three])
        slot_loads = slot_loads + jnp.einsum('sxc,kxc->sk', onehot, contrib, precision=lax.Precision.HIGHEST)
    return (collided, slot_loads)

def along_z(shifted, bounce, offset_z):
    if offset_z == 1:
        return jnp.concatenate([bounce[..., :1], shifted[..., :-1]], axis=-1)
    if offset_z == -1:
        return jnp.concatenate([shifted[..., 1:], bounce[..., -1:]], axis=-1)
    return shifted

def reference(populations, cover_codes, sphere_cell, sphere_velocity, sphere_spin, relax_rates):
    spheres = jnp.concatenate([sphere_cell.astype(jnp.float32), sphere_velocity, sphere_spin], axis=0)
    neighbours = jnp.stack([jnp.stack([jnp.roll(spheres, (1 - off_x, 1 - off_y), axis=(1, 2)) for off_y in range(3)]) for off_x in range(3)])
    tables = neighbours.transpose(3, 4, 0, 1, 5, 2).reshape(BLOCKS_X * BLOCKS_Y, 9 * SPB, 9)
    blocks = populations.reshape(Q, BLOCKS_X, CX, BLOCKS_Y, CY * NZ).transpose(1, 3, 0, 2, 4).reshape(BLOCKS_X * BLOCKS_Y, Q, CX, CY * NZ)
    covers = cover_codes.reshape(2, BLOCKS_X, CX, BLOCKS_Y, CY * NZ).transpose(1, 3, 0, 2, 4).reshape(BLOCKS_X * BLOCKS_Y, 2, CX, CY * NZ)

    def one_block(block_items):
        return collide_block(block_items[0], block_items[1], block_items[2], relax_rates)
    posts, loads = lax.map(one_block, (blocks, covers, tables))
    collided = posts.reshape(BLOCKS_X, BLOCKS_Y, Q, CX, CY, NZ).transpose(2, 0, 3, 1, 4, 5).reshape(Q, NX, NY, NZ)
    passed = []
    for pop_index in range(19):
        offset = VELOCITIES[pop_index]
        shifted = jnp.roll(collided[pop_index], (int(offset[0]), int(offset[1])), axis=(0, 1))
        passed.append(along_z(shifted, collided[OPPOSITE[pop_index]], int(offset[2])))
    populations_next = jnp.stack(passed).reshape(Q, NX, NY * NZ)
    slot_parts = loads.reshape(BLOCKS_X, BLOCKS_Y, 3, 3, SPB, 6)
    running = jnp.zeros((BLOCKS_X, BLOCKS_Y, SPB, 6), jnp.float32)
    for off_x in range(3):
        for off_y in range(3):
            running = running + jnp.roll(slot_parts[:, :, off_x, off_y], (off_x - 1, off_y - 1), axis=(0, 1))
    sphere_load = running.transpose(3, 0, 1, 2)
    return (populations_next, sphere_load)
```

```python
import jax
import jax.numpy as jnp
import numpy as np
from jax import lax
from jax.experimental import pallas as pl
from jax.experimental.pallas import tpu as pltpu
from jax.sharding import PartitionSpec as P

NZ = 64
RADIUS = 8
CX, CY = 8, 16
CELLS = CY * NZ
LANES = 128
CHUNKS = CELLS // LANES
MESH = pl.DeviceIdType.MESH
F32 = jnp.float32

VELOCITIES = np.array(
    [
        [0, 0, 0],
        [1, 0, 0],
        [-1, 0, 0],
        [0, 1, 0],
        [0, -1, 0],
        [0, 0, 1],
        [0, 0, -1],
        [1, 1, 0],
        [-1, -1, 0],
        [1, -1, 0],
        [-1, 1, 0],
        [1, 0, 1],
        [-1, 0, -1],
        [1, 0, -1],
        [-1, 0, 1],
        [0, 1, 1],
        [0, -1, -1],
        [0, 1, -1],
        [0, -1, 1],
    ]
)
OPPOSITE = [0, 2, 1, 4, 3, 6, 5, 8, 7, 10, 9, 12, 11, 14, 13, 16, 15, 18, 17]
X_UP, X_DOWN = (1, 7, 9, 11, 13), (2, 8, 10, 12, 14)
Y_UP, Y_DOWN = (3, 7, 10, 15, 17), (4, 8, 9, 16, 18)
DIRECTIONS = [d for d in range(9) if d != 4]


def moment_rows():
    vel_x, vel_y, vel_z = [VELOCITIES[:, component] * 1.0 for component in range(3)]
    monomials = [
        np.ones(19),
        vel_x,
        vel_y,
        vel_z,
        vel_x * vel_x,
        vel_y * vel_y,
        vel_z * vel_z,
        vel_x * vel_y,
        vel_x * vel_z,
        vel_y * vel_z,
        vel_x * vel_x * vel_y,
        vel_x * vel_x * vel_z,
        vel_y * vel_y * vel_x,
        vel_y * vel_y * vel_z,
        vel_z * vel_z * vel_x,
        vel_z * vel_z * vel_y,
        vel_x * vel_x * vel_y * vel_y,
        vel_x * vel_x * vel_z * vel_z,
        vel_y * vel_y * vel_z * vel_z,
    ]
    orthonormal = []
    for vector in monomials:
        vector = vector.copy()
        for earlier in orthonormal:
            vector = vector - np.dot(earlier, vector) * earlier
        orthonormal.append(vector / np.sqrt(np.dot(vector, vector)))
    return np.stack(orthonormal)


def coefficient_rows():
    rows = moment_rows()[4:]
    even = [1, 3, 5, 7, 11, 15]
    out = []
    for a in even:
        for b in even:
            keep = np.isin(np.arange(15), [0, 1, 2, 12, 13, 14])
            out.append(rows[:, a] * (rows[:, b] - rows[:, 0]) * keep)
    for axis, first, second, rates in ((1, 7, 11, (8, 10)), (3, 7, 15, (6, 11)), (5, 11, 15, (7, 9))):
        for a in (first, second):
            for b in (first, second):
                keep = np.isin(np.arange(15), rates)
                out.append(rows[:, a] * (rows[:, b] - rows[:, axis]) * keep)
    for rate in (3, 4, 5):
        out.append(0.25 * (np.arange(15) == rate))
    table = np.zeros((64, 16), np.float32)
    table[: len(out), :15] = np.stack(out)
    return table


def lane_shift(pop):
    return int(VELOCITIES[pop, 1]) * NZ + int(VELOCITIES[pop, 2])


def kernel(
    pops_hbm, codes_hbm, cell_ref, vel_ref, spin_ref, rates_ref, coef_in,
    out_hbm, load_ref,
    f, codes, coef, post, moments, onehot, contrib, split, out,
    state, states, table, xsend, xrecv, ysend, yrecv, loads, loads_in,
    in_sem, out_sem, state_send, state_recv, halo_send, halo_recv, load_send, load_recv,
):
    nx, ny = lax.axis_size("bx"), lax.axis_size("by")
    me_x, me_y = lax.axis_index("bx"), lax.axis_index("by")

    def neighbour(d):
        return (lax.rem(me_x + d // 3 - 1 + nx, nx), lax.rem(me_y + d % 3 - 1 + ny, ny))

    barrier = pltpu.get_barrier_semaphore()
    for d in DIRECTIONS:
        pl.semaphore_signal(barrier, inc=1, device_id=neighbour(d), device_id_type=MESH)
    get_codes = pltpu.make_async_copy(codes_hbm, codes, in_sem.at[0])
    get_codes.start()
    get_pops = pltpu.make_async_copy(pops_hbm, f, in_sem.at[1])
    get_pops.start()

    lane = lax.broadcasted_iota(jnp.int32, (1, LANES), 1)
    sphere = lane & 3
    for row in range(9):
        source = (cell_ref, vel_ref, spin_ref)[row // 3]
        picked = [source[row % 3, 0, 0, k].astype(F32) for k in range(4)]
        value = jnp.where(
            sphere < 2,
            jnp.where(sphere == 0, picked[0], picked[1]),
            jnp.where(sphere == 2, picked[2], picked[3]),
        )
        state[row : row + 1, :] = value
    pl.semaphore_wait(barrier, 8)

    state_copies = {}
    for n, d in enumerate(DIRECTIONS):
        there = 8 - d
        state_copies[there] = pltpu.make_async_remote_copy(
            src_ref=state, dst_ref=states.at[there],
            send_sem=state_send.at[n], recv_sem=state_recv.at[there],
            device_id=neighbour(d), device_id_type=MESH,
        )
        state_copies[there].start()

    which = lax.broadcasted_iota(jnp.int32, (16, LANES), 0)
    rates = jnp.zeros((16, LANES), F32)
    for r in range(15):
        rates = jnp.where(which == r, rates_ref[r], rates)
    coef[...] = jnp.dot(
        coef_in[...], rates, precision=lax.Precision.HIGHEST, preferred_element_type=F32
    )

    get_codes.wait()
    slot_rows = lax.broadcasted_iota(jnp.int32, (48, CELLS), 0)

    def fill_onehot(step, carry):
        layer, row = step // CX, lax.rem(step, CX)
        slots = codes[layer, pl.ds(row, 1), :] >> 8
        hit = jnp.where(slots == slot_rows, 1.0, 0.0)
        onehot[:, pl.ds(pl.multiple_of(step * CELLS, CELLS), CELLS)] = hit.astype(jnp.bfloat16)
        return carry

    lax.fori_loop(0, 2 * CX, fill_onehot, 0)

    get_pops.wait()

    def fluid(chunk, carry):
        at = pl.ds(pl.multiple_of(chunk * LANES, LANES), LANES)
        p = [f[i, :, at] for i in range(19)]
        s = {a: p[a] + p[a + 1] for a in range(1, 19, 2)}
        d = {a: p[a] - p[a + 1] for a in range(1, 19, 2)}
        s_xy, a_xy = s[7] + s[9], s[7] - s[9]
        s_xz, a_xz = s[11] + s[13], s[11] - s[13]
        s_yz, a_yz = s[15] + s[17], s[15] - s[17]
        x1, x2 = d[7] + d[9], d[11] + d[13]
        y1, y2 = d[7] - d[9], d[15] + d[17]
        z1, z2 = d[11] - d[13], d[15] - d[17]
        density = (p[0] + s[1]) + (s[3] + s[5]) + (s_xy + s_xz) + s_yz
        jx, jy, jz = d[1] + x1 + x2, d[3] + y1 + y2, d[5] + z1 + z2
        inverse = 1.0 / density
        ux, uy, uz = jx * inverse, jy * inverse, jz * inverse
        for n, value in enumerate((density, jx, jy, jz, ux, uy, uz)):
            moments[n, :, at] = value
        cover = ((codes[0, :, at] & 255) + (codes[1, :, at] & 255)).astype(F32) * (1.0 / 255.0)
        keep = 1.0 - cover
        hx, hy, hz = 0.5 * jx * ux, 0.5 * jy * uy, 0.5 * jz * uz
        base = density * (1.0 / 9.0) - (hx + hy + hz) * (1.0 / 3.0)
        even = [
            s[1] - base - hx,
            s[3] - base - hy,
            s[5] - base - hz,
            s_xy - base - (hx + hy),
            s_xz - base - (hx + hz),
            s_yz - base - (hy + hz),
        ]
        even = [keep * value for value in even]

        def c(n):
            return jnp.broadcast_to(coef[n : n + 1, :], (CX, LANES))

        sums = []
        for a in range(6):
            total = c(6 * a) * even[0]
            for b in range(1, 6):
                total = total + c(6 * a + b) * even[b]
            sums.append(total)
        third = 1.0 / 3.0
        odd = []
        for axis, (first, second, flow) in enumerate(((x1, x2, jx), (y1, y2, jy), (z1, z2, jz))):
            level = flow * third
            first, second = keep * (first - level), keep * (second - level)
            k = 36 + 4 * axis
            near = c(k) * first + c(k + 1) * second
            far = c(k + 2) * first + c(k + 3) * second
            odd.append((-2.0 * (near + far), near, far))
        n_xy = keep * (a_xy - jx * uy) * c(48)
        n_xz = keep * (a_xz - jx * uz) * c(49)
        n_yz = keep * (a_yz - jy * uz) * c(50)
        post[0, :, at] = p[0] + 2.0 * (sums[0] + sums[1] + sums[2]) + 4.0 * (sums[3] + sums[4] + sums[5])
        pairs = {
            1: (sums[0], odd[0][0]),
            3: (sums[1], odd[1][0]),
            5: (sums[2], odd[2][0]),
            7: (sums[3] + n_xy, odd[0][1] + odd[1][1]),
            9: (sums[3] - n_xy, odd[0][1] - odd[1][1]),
            11: (sums[4] + n_xz, odd[0][2] + odd[2][1]),
            13: (sums[4] - n_xz, odd[0][2] - odd[2][1]),
            15: (sums[5] + n_yz, odd[1][2] + odd[2][2]),
            17: (sums[5] - n_yz, odd[1][2] - odd[2][2]),
        }
        for a, (ev, od) in pairs.items():
            od = od + cover * d[a]
            post[a, :, at] = p[a] - ev - od
            post[a + 1, :, at] = p[a + 1] - ev + od
        return carry

    lax.fori_loop(0, CHUNKS, fluid, 0)
    contrib[:, 48:64, :] = jnp.zeros((2 * CHUNKS, 16, LANES), F32)

    for there in DIRECTIONS:
        state_copies[there].wait()
    lanes16 = lax.broadcasted_iota(jnp.int32, (16, LANES), 1)
    group = lanes16 >> 2
    rows16 = lax.broadcasted_iota(jnp.int32, (16, LANES), 0)
    full = jnp.where(group == 4, state[...], 0.0)
    for d in DIRECTIONS:
        full = jnp.where(group == d, states[d], full)
    off_x = jnp.where(group >= 6, CX, jnp.where(group >= 3, 0, -CX)).astype(F32)
    third_of = group - jnp.where(group >= 6, 6, jnp.where(group >= 3, 3, 0))
    off_y = ((third_of - 1) * CY).astype(F32)
    full = full + jnp.where(rows16 == 0, off_x, jnp.where(rows16 == 1, off_y, 0.0))
    table[...] = full

    def covers(chunk, carry):
        start = pl.multiple_of(chunk * LANES, LANES)
        at = pl.ds(start, LANES)
        lanes = lax.broadcasted_iota(jnp.int32, (CX, LANES), 1)
        cell_x = lax.broadcasted_iota(jnp.int32, (CX, LANES), 0).astype(F32)
        cell_y = ((lanes >> 6) + 2 * chunk).astype(F32)
        cell_z = (lanes & 63).astype(F32)
        density, jx, jy, jz, ux, uy, uz = [moments[n, :, at] for n in range(7)]
        first = second = None
        for layer in range(2):
            packed = codes[layer, :, at]
            slot = packed >> 8
            eps = (packed & 255).astype(F32) * (1.0 / 255.0)
            got = [
                jnp.take_along_axis(
                    jnp.broadcast_to(table[n : n + 1, :], (CX, LANES)), slot,
                    axis=1, mode="promise_in_bounds",
                )
                for n in range(9)
            ]
            rx, ry, rz = cell_x - got[0], cell_y - got[1], cell_z - got[2]
            wx = got[3] + got[7] * rz - got[8] * ry
            wy = got[4] + got[8] * rx - got[6] * rz
            wz = got[5] + got[6] * ry - got[7] * rx
            weight = eps * density
            bx, by, bz = weight * wx, weight * wy, weight * wz
            fx, fy, fz = eps * jx - bx, eps * jy - by, eps * jz - bz
            rows = (fx, fy, fz, ry * fz - rz * fy, rz * fx - rx * fz, rx * fy - ry * fx)
            for n, value in enumerate(rows):
                contrib[layer * CHUNKS + chunk, CX * n : CX * (n + 1), :] = value
            quad = (bx * wx, by * wy, bz * wz, bx * wy, bx * wz, by * wz)
            if layer == 0:
                first, second, cover = (bx, by, bz), quad, eps
            else:
                first = [a + b for a, b in zip(first, (bx, by, bz))]
                second = [a + b for a, b in zip(second, quad)]
                cover = cover + eps
        ex, ey, ez = cover * jx, cover * jy, cover * jz
        hx, hy, hz = first[0] + ex, first[1] + ey, first[2] + ez
        qxx, qyy, qzz = second[0] - ex * ux, second[1] - ey * uy, second[2] - ez * uz
        qxy, qxz, qyz = second[3] - ex * uy, second[4] - ex * uz, second[5] - ey * uz
        trace = qxx + qyy + qzz
        post[0, :, at] = post[0, :, at] - 0.5 * trace
        axis_base = trace * (-1.0 / 12.0)
        half_base = trace * (-1.0 / 24.0)
        hx, hy, hz = hx * (1.0 / 12.0), hy * (1.0 / 12.0), hz * (1.0 / 12.0)
        exx, eyy, ezz = 0.125 * qxx, 0.125 * qyy, 0.125 * qzz
        exy, exz, eyz = 0.25 * qxy, 0.25 * qxz, 0.25 * qyz
        b_xy, b_xz, b_yz = half_base + exx + eyy, half_base + exx + ezz, half_base + eyy + ezz
        pairs = {
            1: (axis_base + 2.0 * exx, 2.0 * hx),
            3: (axis_base + 2.0 * eyy, 2.0 * hy),
            5: (axis_base + 2.0 * ezz, 2.0 * hz),
            7: (b_xy + exy, hx + hy),
            9: (b_xy - exy, hx - hy),
            11: (b_xz + exz, hx + hz),
            13: (b_xz - exz, hx - hz),
            15: (b_yz + eyz, hy + hz),
            17: (b_yz - eyz, hy - hz),
        }
        for a, (ev, od) in pairs.items():
            post[a, :, at] = post[a, :, at] + (ev + od)
            post[a + 1, :, at] = post[a + 1, :, at] + (ev - od)
        return carry

    lax.fori_loop(0, CHUNKS, covers, 0)

    def passed(pop):
        value = post[pop]
        shift = lane_shift(pop) % CELLS
        if shift:
            value = pltpu.roll(value, shift, 1)
        step = int(VELOCITIES[pop, 0]) % CX
        if step:
            value = pltpu.roll(value, step, 0)
        return value

    z_of = lax.broadcasted_iota(jnp.int32, (CX, CELLS), 1) & (NZ - 1)
    edge = {1: z_of == 0, -1: z_of == NZ - 1}
    lower = lax.broadcasted_iota(jnp.int32, (1, LANES), 1) < NZ
    corners = {}
    for pop in range(19):
        step_x, step_y, step_z = (int(v) for v in VELOCITIES[pop])
        value = passed(pop)
        if step_x:
            row = 0 if step_x > 0 else CX - 1
            side = 0 if step_x > 0 else 1
            n = (X_UP, X_DOWN)[side].index(pop)
            for c in range(CHUNKS):
                xsend[side, n * CHUNKS + c : n * CHUNKS + c + 1, :] = value[
                    row : row + 1, c * LANES : (c + 1) * LANES
                ]
        if step_y:
            side = 0 if step_y > 0 else 1
            n = (Y_UP, Y_DOWN)[side].index(pop)
            c = 0 if step_y > 0 else CHUNKS - 1
            ysend[side, n] = value[:, c * LANES : (c + 1) * LANES]
            if step_x:
                corners[pop] = value[row : row + 1, c * LANES : (c + 1) * LANES]
        if step_z:
            value = jnp.where(edge[step_z], post[OPPOSITE[pop]], value)
        out[pop] = value
    loads[6:7, :] = jnp.where(lower, corners[7], corners[8])
    loads[7:8, :] = jnp.where(lower, corners[10], corners[9])

    halo = []
    for n, (src, dst, d) in enumerate(
        (
            (xsend.at[0], xrecv.at[0], 7),
            (xsend.at[1], xrecv.at[1], 1),
            (ysend.at[0], yrecv.at[0], 5),
            (ysend.at[1], yrecv.at[1], 3),
        )
    ):
        halo.append(
            pltpu.make_async_remote_copy(
                src_ref=src, dst_ref=dst, send_sem=halo_send.at[n], recv_sem=halo_recv.at[n],
                device_id=neighbour(d), device_id_type=MESH,
            )
        )
        halo[-1].start()

    for layer in range(2):
        for row in range(CX):
            for c in range(CHUNKS):
                value = contrib[layer * CHUNKS + c, pl.ds(row, 8, stride=CX), :]
                high = value.astype(jnp.bfloat16).astype(F32)
                both = jnp.concatenate([high, value - high], axis=0)
                at = (layer * CX + row) * CELLS + c * LANES
                split[:, at : at + LANES] = both.astype(jnp.bfloat16)
    sums = lax.dot_general(
        split[...], onehot[...], (((1,), (1,)), ((), ())), preferred_element_type=F32
    )
    sums = sums[0:8] + sums[8:16]
    row8 = lax.broadcasted_iota(jnp.int32, (8, 48), 0)
    sums = sums * jnp.where(row8 < 3, 1.0 / RADIUS**2, 1.0 / RADIUS**3)
    loads[0:6, 0:48] = sums[0:6]

    load_copies = {}
    for n, d in enumerate(DIRECTIONS):
        there = 8 - d
        load_copies[there] = pltpu.make_async_remote_copy(
            src_ref=loads, dst_ref=loads_in.at[there],
            send_sem=load_send.at[n], recv_sem=load_recv.at[there],
            device_id=neighbour(d), device_id_type=MESH,
        )
        load_copies[there].start()

    for copy in halo:
        copy.wait()
    for side, names in enumerate((X_UP, X_DOWN)):
        row = 0 if side == 0 else CX - 1
        for n, pop in enumerate(names):
            step_z = int(VELOCITIES[pop, 2])
            for c in range(CHUNKS):
                at = slice(c * LANES, (c + 1) * LANES)
                value = xrecv[side, n * CHUNKS + c : n * CHUNKS + c + 1, :]
                if step_z:
                    value = jnp.where(edge[step_z][0:1, at], out[pop, row : row + 1, at], value)
                out[pop, row : row + 1, at] = value
    lower8 = lax.broadcasted_iota(jnp.int32, (CX, LANES), 1) < NZ
    for side, names in enumerate((Y_UP, Y_DOWN)):
        c = 0 if side == 0 else CHUNKS - 1
        at = slice(c * LANES, (c + 1) * LANES)
        for n, pop in enumerate(names):
            step_z = int(VELOCITIES[pop, 2])
            mask = lower8 if side == 0 else jnp.logical_not(lower8)
            if step_z:
                mask = jnp.logical_and(mask, jnp.logical_not(edge[step_z][:, at]))
            out[pop, :, at] = jnp.where(mask, yrecv[side, n], out[pop, :, at])

    for there in DIRECTIONS:
        load_copies[there].wait()
    for pop, source, row, c, corner_row in (
        (7, 0, 0, 0, 6),
        (8, 8, CX - 1, CHUNKS - 1, 6),
        (9, 2, 0, CHUNKS - 1, 7),
        (10, 6, CX - 1, 0, 7),
    ):
        at = slice(c * LANES, (c + 1) * LANES)
        mask = lower if c == 0 else jnp.logical_not(lower)
        out[pop, row : row + 1, at] = jnp.where(
            mask, loads_in[source, corner_row : corner_row + 1, :], out[pop, row : row + 1, at]
        )
    put = pltpu.make_async_copy(out, out_hbm, out_sem.at[0])
    put.start()

    total = None
    for d in range(9):
        tile = loads[...] if d == 4 else loads_in[d]
        back = (4 * (8 - d)) % LANES
        tile = pltpu.roll(tile, (LANES - back) % LANES, 1) if back else tile
        total = tile if total is None else total + tile
    for row in range(6):
        load_ref[row, 0, :, :] = total[row : row + 1, 0:4]
    put.wait()


def per_device(populations, cover_codes, sphere_cell, sphere_velocity, sphere_spin, relax_rates):
    vmem, smem, anywhere = (
        pl.BlockSpec(memory_space=pltpu.VMEM),
        pl.BlockSpec(memory_space=pltpu.SMEM),
        pl.BlockSpec(memory_space=pl.ANY),
    )
    dma = pltpu.SemaphoreType.DMA
    return pl.pallas_call(
        kernel,
        out_shape=(
            jax.ShapeDtypeStruct((19, CX, CELLS), F32),
            jax.ShapeDtypeStruct((6, 1, 1, 4), F32),
        ),
        in_specs=[anywhere, anywhere, smem, smem, smem, smem, vmem],
        out_specs=(anywhere, vmem),
        scratch_shapes=[
            pltpu.VMEM((19, CX, CELLS), F32),
            pltpu.VMEM((2, CX, CELLS), jnp.int32),
            pltpu.VMEM((64, LANES), F32),
            pltpu.VMEM((19, CX, CELLS), F32),
            pltpu.VMEM((7, CX, CELLS), F32),
            pltpu.VMEM((48, 2 * CX * CELLS), jnp.bfloat16),
            pltpu.VMEM((2 * CHUNKS, 64, LANES), F32),
            pltpu.VMEM((16, 2 * CX * CELLS), jnp.bfloat16),
            pltpu.VMEM((19, CX, CELLS), F32),
            pltpu.VMEM((16, LANES), F32),
            pltpu.VMEM((9, 16, LANES), F32),
            pltpu.VMEM((16, LANES), F32),
            pltpu.VMEM((2, 40, LANES), F32),
            pltpu.VMEM((2, 40, LANES), F32),
            pltpu.VMEM((2, 5, CX, LANES), F32),
            pltpu.VMEM((2, 5, CX, LANES), F32),
            pltpu.VMEM((8, LANES), F32),
            pltpu.VMEM((9, 8, LANES), F32),
            dma((2,)),
            dma((1,)),
            dma((8,)),
            dma((9,)),
            dma((4,)),
            dma((4,)),
            dma((8,)),
            dma((9,)),
        ],
        compiler_params=pltpu.CompilerParams(
            collective_id=0, has_side_effects=True, vmem_limit_bytes=32 * 1024 * 1024
        ),
    )(
        populations, cover_codes, sphere_cell, sphere_velocity, sphere_spin, relax_rates,
        jnp.asarray(coefficient_rows()),
    )


def solution(mesh):
    placed = (
        P(None, "bx", "by"),
        P(None, "bx", "by"),
        P(None, "bx", "by", None),
        P(None, "bx", "by", None),
        P(None, "bx", "by", None),
        P(),
    )
    return jax.shard_map(
        per_device,
        mesh=mesh,
        in_specs=placed,
        out_specs=(P(None, "bx", "by"), P(None, "bx", "by", None)),
        check_vma=False,
    )
```

```python
import jax
import jax.numpy as jnp
import numpy as np
from jax import lax
from jax.experimental import pallas as pl
from jax.experimental.pallas import tpu as pltpu
from jax.sharding import PartitionSpec as P

NZ = 64
RADIUS = 8
CX, CY = 8, 16
CELLS = CY * NZ
LANES = 128
CHUNKS = CELLS // LANES
MESH = pl.DeviceIdType.MESH
F32 = jnp.float32

VELOCITIES = np.array(
    [
        [0, 0, 0],
        [1, 0, 0],
        [-1, 0, 0],
        [0, 1, 0],
        [0, -1, 0],
        [0, 0, 1],
        [0, 0, -1],
        [1, 1, 0],
        [-1, -1, 0],
        [1, -1, 0],
        [-1, 1, 0],
        [1, 0, 1],
        [-1, 0, -1],
        [1, 0, -1],
        [-1, 0, 1],
        [0, 1, 1],
        [0, -1, -1],
        [0, 1, -1],
        [0, -1, 1],
    ]
)
OPPOSITE = [0, 2, 1, 4, 3, 6, 5, 8, 7, 10, 9, 12, 11, 14, 13, 16, 15, 18, 17]
X_UP, X_DOWN = (1, 7, 9, 11, 13), (2, 8, 10, 12, 14)
Y_UP, Y_DOWN = (3, 7, 10, 15, 17), (4, 8, 9, 16, 18)
DIRECTIONS = [d for d in range(9) if d != 4]


def moment_rows():
    vel_x, vel_y, vel_z = [VELOCITIES[:, component] * 1.0 for component in range(3)]
    monomials = [
        np.ones(19),
        vel_x,
        vel_y,
        vel_z,
        vel_x * vel_x,
        vel_y * vel_y,
        vel_z * vel_z,
        vel_x * vel_y,
        vel_x * vel_z,
        vel_y * vel_z,
        vel_x * vel_x * vel_y,
        vel_x * vel_x * vel_z,
        vel_y * vel_y * vel_x,
        vel_y * vel_y * vel_z,
        vel_z * vel_z * vel_x,
        vel_z * vel_z * vel_y,
        vel_x * vel_x * vel_y * vel_y,
        vel_x * vel_x * vel_z * vel_z,
        vel_y * vel_y * vel_z * vel_z,
    ]
    orthonormal = []
    for vector in monomials:
        vector = vector.copy()
        for earlier in orthonormal:
            vector = vector - np.dot(earlier, vector) * earlier
        orthonormal.append(vector / np.sqrt(np.dot(vector, vector)))
    return np.stack(orthonormal)


def coefficient_rows():
    rows = moment_rows()[4:]
    even = [1, 3, 5, 7, 11, 15]
    out = []
    for a in even:
        for b in even:
            keep = np.isin(np.arange(15), [0, 1, 2, 12, 13, 14])
            out.append(rows[:, a] * (rows[:, b] - rows[:, 0]) * keep)
    for axis, first, second, rates in ((1, 7, 11, (8, 10)), (3, 7, 15, (6, 11)), (5, 11, 15, (7, 9))):
        for a in (first, second):
            for b in (first, second):
                keep = np.isin(np.arange(15), rates)
                out.append(rows[:, a] * (rows[:, b] - rows[:, axis]) * keep)
    for rate in (3, 4, 5):
        out.append(0.25 * (np.arange(15) == rate))
    table = np.zeros((64, 16), np.float32)
    table[: len(out), :15] = np.stack(out)
    return table


def lane_shift(pop):
    return int(VELOCITIES[pop, 1]) * NZ + int(VELOCITIES[pop, 2])


def kernel(
    pops_hbm, codes_hbm, cell_ref, vel_ref, spin_ref, rates_ref, coef_in,
    out, load_ref,
    f, codes, coef, post, moments, onehot, contrib, split,
    state, states, table, xsend, xrecv, ysend, yrecv, loads, loads_in,
    in_sem, out_sem, state_send, state_recv, halo_send, halo_recv, load_send, load_recv,
):
    nx, ny = lax.axis_size("bx"), lax.axis_size("by")
    me_x, me_y = lax.axis_index("bx"), lax.axis_index("by")

    def neighbour(d):
        return (lax.rem(me_x + d // 3 - 1 + nx, nx), lax.rem(me_y + d % 3 - 1 + ny, ny))

    barrier = pltpu.get_barrier_semaphore()
    for d in DIRECTIONS:
        pl.semaphore_signal(barrier, inc=1, device_id=neighbour(d), device_id_type=MESH)
    get_codes = pltpu.make_async_copy(codes_hbm, codes, in_sem.at[0])
    get_codes.start()
    get_pops = pltpu.make_async_copy(pops_hbm, f, in_sem.at[1])
    get_pops.start()

    lane = lax.broadcasted_iota(jnp.int32, (1, LANES), 1)
    sphere = lane & 3
    for row in range(9):
        source = (cell_ref, vel_ref, spin_ref)[row // 3]
        picked = [source[row % 3, 0, 0, k].astype(F32) for k in range(4)]
        value = jnp.where(
            sphere < 2,
            jnp.where(sphere == 0, picked[0], picked[1]),
            jnp.where(sphere == 2, picked[2], picked[3]),
        )
        state[row : row + 1, :] = value
    pl.semaphore_wait(barrier, 8)

    state_copies = {}
    for n, d in enumerate(DIRECTIONS):
        there = 8 - d
        state_copies[there] = pltpu.make_async_remote_copy(
            src_ref=state, dst_ref=states.at[there],
            send_sem=state_send.at[n], recv_sem=state_recv.at[there],
            device_id=neighbour(d), device_id_type=MESH,
        )
        state_copies[there].start()

    which = lax.broadcasted_iota(jnp.int32, (16, LANES), 0)
    rates = jnp.zeros((16, LANES), F32)
    for r in range(15):
        rates = jnp.where(which == r, rates_ref[r], rates)
    coef[...] = jnp.dot(
        coef_in[...], rates, precision=lax.Precision.HIGHEST, preferred_element_type=F32
    )

    get_codes.wait()
    slot_rows = lax.broadcasted_iota(jnp.int32, (48, CELLS), 0)

    def fill_onehot(step, carry):
        layer, row = step // CX, lax.rem(step, CX)
        slots = codes[layer, pl.ds(row, 1), :] >> 8
        hit = jnp.where(slots == slot_rows, 1.0, 0.0)
        onehot[:, pl.ds(pl.multiple_of(step * CELLS, CELLS), CELLS)] = hit.astype(jnp.bfloat16)
        return carry

    lax.fori_loop(0, 2 * CX, fill_onehot, 0)

    get_pops.wait()

    def fluid(chunk, carry):
        at = pl.ds(pl.multiple_of(chunk * LANES, LANES), LANES)
        p = [f[i, :, at] for i in range(19)]
        s = {a: p[a] + p[a + 1] for a in range(1, 19, 2)}
        d = {a: p[a] - p[a + 1] for a in range(1, 19, 2)}
        s_xy, a_xy = s[7] + s[9], s[7] - s[9]
        s_xz, a_xz = s[11] + s[13], s[11] - s[13]
        s_yz, a_yz = s[15] + s[17], s[15] - s[17]
        x1, x2 = d[7] + d[9], d[11] + d[13]
        y1, y2 = d[7] - d[9], d[15] + d[17]
        z1, z2 = d[11] - d[13], d[15] - d[17]
        density = (p[0] + s[1]) + (s[3] + s[5]) + (s_xy + s_xz) + s_yz
        jx, jy, jz = d[1] + x1 + x2, d[3] + y1 + y2, d[5] + z1 + z2
        inverse = 1.0 / density
        ux, uy, uz = jx * inverse, jy * inverse, jz * inverse
        for n, value in enumerate((density, jx, jy, jz, ux, uy, uz)):
            moments[n, :, at] = value
        cover = ((codes[0, :, at] & 255) + (codes[1, :, at] & 255)).astype(F32) * (1.0 / 255.0)
        keep = 1.0 - cover
        hx, hy, hz = 0.5 * jx * ux, 0.5 * jy * uy, 0.5 * jz * uz
        base = density * (1.0 / 9.0) - (hx + hy + hz) * (1.0 / 3.0)
        even = [
            s[1] - base - hx,
            s[3] - base - hy,
            s[5] - base - hz,
            s_xy - base - (hx + hy),
            s_xz - base - (hx + hz),
            s_yz - base - (hy + hz),
        ]
        even = [keep * value for value in even]

        def c(n):
            return jnp.broadcast_to(coef[n : n + 1, :], (CX, LANES))

        sums = []
        for a in range(6):
            total = c(6 * a) * even[0]
            for b in range(1, 6):
                total = total + c(6 * a + b) * even[b]
            sums.append(total)
        third = 1.0 / 3.0
        odd = []
        for axis, (first, second, flow) in enumerate(((x1, x2, jx), (y1, y2, jy), (z1, z2, jz))):
            level = flow * third
            first, second = keep * (first - level), keep * (second - level)
            k = 36 + 4 * axis
            near = c(k) * first + c(k + 1) * second
            far = c(k + 2) * first + c(k + 3) * second
            odd.append((-2.0 * (near + far), near, far))
        n_xy = keep * (a_xy - jx * uy) * c(48)
        n_xz = keep * (a_xz - jx * uz) * c(49)
        n_yz = keep * (a_yz - jy * uz) * c(50)
        post[0, :, at] = p[0] + 2.0 * (sums[0] + sums[1] + sums[2]) + 4.0 * (sums[3] + sums[4] + sums[5])
        pairs = {
            1: (sums[0], odd[0][0]),
            3: (sums[1], odd[1][0]),
            5: (sums[2], odd[2][0]),
            7: (sums[3] + n_xy, odd[0][1] + odd[1][1]),
            9: (sums[3] - n_xy, odd[0][1] - odd[1][1]),
            11: (sums[4] + n_xz, odd[0][2] + odd[2][1]),
            13: (sums[4] - n_xz, odd[0][2] - odd[2][1]),
            15: (sums[5] + n_yz, odd[1][2] + odd[2][2]),
            17: (sums[5] - n_yz, odd[1][2] - odd[2][2]),
        }
        for a, (ev, od) in pairs.items():
            od = od + cover * d[a]
            post[a, :, at] = p[a] - ev - od
            post[a + 1, :, at] = p[a + 1] - ev + od
        return carry

    lax.fori_loop(0, CHUNKS, fluid, 0)
    contrib[:, 48:64, :] = jnp.zeros((2 * CHUNKS, 16, LANES), F32)

    for there in DIRECTIONS:
        state_copies[there].wait()
    lanes16 = lax.broadcasted_iota(jnp.int32, (16, LANES), 1)
    group = lanes16 >> 2
    rows16 = lax.broadcasted_iota(jnp.int32, (16, LANES), 0)
    full = jnp.where(group == 4, state[...], 0.0)
    for d in DIRECTIONS:
        full = jnp.where(group == d, states[d], full)
    off_x = jnp.where(group >= 6, CX, jnp.where(group >= 3, 0, -CX)).astype(F32)
    third_of = group - jnp.where(group >= 6, 6, jnp.where(group >= 3, 3, 0))
    off_y = ((third_of - 1) * CY).astype(F32)
    full = full + jnp.where(rows16 == 0, off_x, jnp.where(rows16 == 1, off_y, 0.0))
    table[...] = full

    def covers(chunk, carry):
        start = pl.multiple_of(chunk * LANES, LANES)
        at = pl.ds(start, LANES)
        lanes = lax.broadcasted_iota(jnp.int32, (CX, LANES), 1)
        cell_x = lax.broadcasted_iota(jnp.int32, (CX, LANES), 0).astype(F32)
        cell_y = ((lanes >> 6) + 2 * chunk).astype(F32)
        cell_z = (lanes & 63).astype(F32)
        density, jx, jy, jz, ux, uy, uz = [moments[n, :, at] for n in range(7)]
        first = second = None
        for layer in range(2):
            packed = codes[layer, :, at]
            slot = packed >> 8
            eps = (packed & 255).astype(F32) * (1.0 / 255.0)
            got = [
                jnp.take_along_axis(
                    jnp.broadcast_to(table[n : n + 1, :], (CX, LANES)), slot,
                    axis=1, mode="promise_in_bounds",
                )
                for n in range(9)
            ]
            rx, ry, rz = cell_x - got[0], cell_y - got[1], cell_z - got[2]
            wx = got[3] + got[7] * rz - got[8] * ry
            wy = got[4] + got[8] * rx - got[6] * rz
            wz = got[5] + got[6] * ry - got[7] * rx
            weight = eps * density
            bx, by, bz = weight * wx, weight * wy, weight * wz
            fx, fy, fz = eps * jx - bx, eps * jy - by, eps * jz - bz
            rows = (fx, fy, fz, ry * fz - rz * fy, rz * fx - rx * fz, rx * fy - ry * fx)
            for n, value in enumerate(rows):
                contrib[layer * CHUNKS + chunk, CX * n : CX * (n + 1), :] = value
            quad = (bx * wx, by * wy, bz * wz, bx * wy, bx * wz, by * wz)
            if layer == 0:
                first, second, cover = (bx, by, bz), quad, eps
            else:
                first = [a + b for a, b in zip(first, (bx, by, bz))]
                second = [a + b for a, b in zip(second, quad)]
                cover = cover + eps
        ex, ey, ez = cover * jx, cover * jy, cover * jz
        hx, hy, hz = first[0] + ex, first[1] + ey, first[2] + ez
        qxx, qyy, qzz = second[0] - ex * ux, second[1] - ey * uy, second[2] - ez * uz
        qxy, qxz, qyz = second[3] - ex * uy, second[4] - ex * uz, second[5] - ey * uz
        trace = qxx + qyy + qzz
        post[0, :, at] = post[0, :, at] - 0.5 * trace
        axis_base = trace * (-1.0 / 12.0)
        half_base = trace * (-1.0 / 24.0)
        hx, hy, hz = hx * (1.0 / 12.0), hy * (1.0 / 12.0), hz * (1.0 / 12.0)
        exx, eyy, ezz = 0.125 * qxx, 0.125 * qyy, 0.125 * qzz
        exy, exz, eyz = 0.25 * qxy, 0.25 * qxz, 0.25 * qyz
        b_xy, b_xz, b_yz = half_base + exx + eyy, half_base + exx + ezz, half_base + eyy + ezz
        pairs = {
            1: (axis_base + 2.0 * exx, 2.0 * hx),
            3: (axis_base + 2.0 * eyy, 2.0 * hy),
            5: (axis_base + 2.0 * ezz, 2.0 * hz),
            7: (b_xy + exy, hx + hy),
            9: (b_xy - exy, hx - hy),
            11: (b_xz + exz, hx + hz),
            13: (b_xz - exz, hx - hz),
            15: (b_yz + eyz, hy + hz),
            17: (b_yz - eyz, hy - hz),
        }
        for a, (ev, od) in pairs.items():
            post[a, :, at] = post[a, :, at] + (ev + od)
            post[a + 1, :, at] = post[a + 1, :, at] + (ev - od)
        return carry

    lax.fori_loop(0, CHUNKS, covers, 0)

    def passed(pop):
        value = post[pop]
        shift = lane_shift(pop) % CELLS
        if shift:
            value = pltpu.roll(value, shift, 1)
        step = int(VELOCITIES[pop, 0]) % CX
        if step:
            value = pltpu.roll(value, step, 0)
        return value

    z_of = lax.broadcasted_iota(jnp.int32, (CX, CELLS), 1) & (NZ - 1)
    edge = {1: z_of == 0, -1: z_of == NZ - 1}
    lower = lax.broadcasted_iota(jnp.int32, (1, LANES), 1) < NZ
    corners = {}
    for pop in range(19):
        step_x, step_y, step_z = (int(v) for v in VELOCITIES[pop])
        value = passed(pop)
        if step_x:
            row = 0 if step_x > 0 else CX - 1
            side = 0 if step_x > 0 else 1
            n = (X_UP, X_DOWN)[side].index(pop)
            for c in range(CHUNKS):
                xsend[side, n * CHUNKS + c : n * CHUNKS + c + 1, :] = value[
                    row : row + 1, c * LANES : (c + 1) * LANES
                ]
        if step_y:
            side = 0 if step_y > 0 else 1
            n = (Y_UP, Y_DOWN)[side].index(pop)
            c = 0 if step_y > 0 else CHUNKS - 1
            ysend[side, n] = value[:, c * LANES : (c + 1) * LANES]
            if step_x:
                corners[pop] = value[row : row + 1, c * LANES : (c + 1) * LANES]
        if step_z:
            value = jnp.where(edge[step_z], post[OPPOSITE[pop]], value)
        out[pop] = value
    loads[6:7, :] = jnp.where(lower, corners[7], corners[8])
    loads[7:8, :] = jnp.where(lower, corners[10], corners[9])

    halo = []
    for n, (src, dst, d) in enumerate(
        (
            (xsend.at[0], xrecv.at[0], 7),
            (xsend.at[1], xrecv.at[1], 1),
            (ysend.at[0], yrecv.at[0], 5),
            (ysend.at[1], yrecv.at[1], 3),
        )
    ):
        halo.append(
            pltpu.make_async_remote_copy(
                src_ref=src, dst_ref=dst, send_sem=halo_send.at[n], recv_sem=halo_recv.at[n],
                device_id=neighbour(d), device_id_type=MESH,
            )
        )
        halo[-1].start()

    for layer in range(2):
        for row in range(CX):
            for c in range(CHUNKS):
                value = contrib[layer * CHUNKS + c, pl.ds(row, 8, stride=CX), :]
                high = value.astype(jnp.bfloat16).astype(F32)
                both = jnp.concatenate([high, value - high], axis=0)
                at = (layer * CX + row) * CELLS + c * LANES
                split[:, at : at + LANES] = both.astype(jnp.bfloat16)
    sums = lax.dot_general(
        split[...], onehot[...], (((1,), (1,)), ((), ())), preferred_element_type=F32
    )
    sums = sums[0:8] + sums[8:16]
    row8 = lax.broadcasted_iota(jnp.int32, (8, 48), 0)
    sums = sums * jnp.where(row8 < 3, 1.0 / RADIUS**2, 1.0 / RADIUS**3)
    loads[0:6, 0:48] = sums[0:6]

    load_copies = {}
    for n, d in enumerate(DIRECTIONS):
        there = 8 - d
        load_copies[there] = pltpu.make_async_remote_copy(
            src_ref=loads, dst_ref=loads_in.at[there],
            send_sem=load_send.at[n], recv_sem=load_recv.at[there],
            device_id=neighbour(d), device_id_type=MESH,
        )
        load_copies[there].start()

    for copy in halo:
        copy.wait()
    for side, names in enumerate((X_UP, X_DOWN)):
        row = 0 if side == 0 else CX - 1
        for n, pop in enumerate(names):
            step_z = int(VELOCITIES[pop, 2])
            for c in range(CHUNKS):
                at = slice(c * LANES, (c + 1) * LANES)
                value = xrecv[side, n * CHUNKS + c : n * CHUNKS + c + 1, :]
                if step_z:
                    value = jnp.where(edge[step_z][0:1, at], out[pop, row : row + 1, at], value)
                out[pop, row : row + 1, at] = value
    lower8 = lax.broadcasted_iota(jnp.int32, (CX, LANES), 1) < NZ
    for side, names in enumerate((Y_UP, Y_DOWN)):
        c = 0 if side == 0 else CHUNKS - 1
        at = slice(c * LANES, (c + 1) * LANES)
        for n, pop in enumerate(names):
            step_z = int(VELOCITIES[pop, 2])
            mask = lower8 if side == 0 else jnp.logical_not(lower8)
            if step_z:
                mask = jnp.logical_and(mask, jnp.logical_not(edge[step_z][:, at]))
            out[pop, :, at] = jnp.where(mask, yrecv[side, n], out[pop, :, at])

    for there in DIRECTIONS:
        load_copies[there].wait()
    for pop, source, row, c, corner_row in (
        (7, 0, 0, 0, 6),
        (8, 8, CX - 1, CHUNKS - 1, 6),
        (9, 2, 0, CHUNKS - 1, 7),
        (10, 6, CX - 1, 0, 7),
    ):
        at = slice(c * LANES, (c + 1) * LANES)
        mask = lower if c == 0 else jnp.logical_not(lower)
        out[pop, row : row + 1, at] = jnp.where(
            mask, loads_in[source, corner_row : corner_row + 1, :], out[pop, row : row + 1, at]
        )

    total = None
    for d in range(9):
        tile = loads[...] if d == 4 else loads_in[d]
        back = (4 * (8 - d)) % LANES
        tile = pltpu.roll(tile, (LANES - back) % LANES, 1) if back else tile
        total = tile if total is None else total + tile
    load_ref[...] = total.T[0:4, 0:6]


def per_device(populations, cover_codes, sphere_cell, sphere_velocity, sphere_spin, relax_rates):
    vmem, smem, anywhere = (
        pl.BlockSpec(memory_space=pltpu.VMEM),
        pl.BlockSpec(memory_space=pltpu.SMEM),
        pl.BlockSpec(memory_space=pl.ANY),
    )
    dma = pltpu.SemaphoreType.DMA
    out, load = pl.pallas_call(
        kernel,
        out_shape=(
            pltpu.VMEM((19, CX, CELLS), F32),
            jax.ShapeDtypeStruct((4, 6), F32),
        ),
        in_specs=[anywhere, anywhere, smem, smem, smem, smem, vmem],
        out_specs=(vmem, vmem),
        scratch_shapes=[
            pltpu.VMEM((19, CX, CELLS), F32),
            pltpu.VMEM((2, CX, CELLS), jnp.int32),
            pltpu.VMEM((64, LANES), F32),
            pltpu.VMEM((19, CX, CELLS), F32),
            pltpu.VMEM((7, CX, CELLS), F32),
            pltpu.VMEM((48, 2 * CX * CELLS), jnp.bfloat16),
            pltpu.VMEM((2 * CHUNKS, 64, LANES), F32),
            pltpu.VMEM((16, 2 * CX * CELLS), jnp.bfloat16),
            pltpu.VMEM((16, LANES), F32),
            pltpu.VMEM((9, 16, LANES), F32),
            pltpu.VMEM((16, LANES), F32),
            pltpu.VMEM((2, 40, LANES), F32),
            pltpu.VMEM((2, 40, LANES), F32),
            pltpu.VMEM((2, 5, CX, LANES), F32),
            pltpu.VMEM((2, 5, CX, LANES), F32),
            pltpu.VMEM((8, LANES), F32),
            pltpu.VMEM((9, 8, LANES), F32),
            dma((2,)),
            dma((1,)),
            dma((8,)),
            dma((9,)),
            dma((4,)),
            dma((4,)),
            dma((8,)),
            dma((9,)),
        ],
        compiler_params=pltpu.CompilerParams(
            collective_id=0, has_side_effects=True, vmem_limit_bytes=60 * 1024 * 1024
        ),
    )(
        populations, cover_codes, sphere_cell, sphere_velocity, sphere_spin, relax_rates,
        jnp.asarray(coefficient_rows()),
    )
    return out, load.T.reshape(6, 1, 1, 4)


def solution(mesh):
    placed = (
        P(None, "bx", "by"),
        P(None, "bx", "by"),
        P(None, "bx", "by", None),
        P(None, "bx", "by", None),
        P(None, "bx", "by", None),
        P(),
    )
    return jax.shard_map(
        per_device,
        mesh=mesh,
        in_specs=placed,
        out_specs=(P(None, "bx", "by"), P(None, "bx", "by", None)),
        check_vma=False,
    )
```

```python
import jax
import jax.numpy as jnp
import numpy as np
from jax import lax
from jax.experimental import pallas as pl
from jax.experimental.pallas import tpu as pltpu
from jax.sharding import PartitionSpec as P

NZ = 64
RADIUS = 8
CX, CY = 8, 16
CELLS = CY * NZ
LANES = 128
CHUNKS = CELLS // LANES
MESH = pl.DeviceIdType.MESH
F32 = jnp.float32

VELOCITIES = np.array(
    [
        [0, 0, 0],
        [1, 0, 0],
        [-1, 0, 0],
        [0, 1, 0],
        [0, -1, 0],
        [0, 0, 1],
        [0, 0, -1],
        [1, 1, 0],
        [-1, -1, 0],
        [1, -1, 0],
        [-1, 1, 0],
        [1, 0, 1],
        [-1, 0, -1],
        [1, 0, -1],
        [-1, 0, 1],
        [0, 1, 1],
        [0, -1, -1],
        [0, 1, -1],
        [0, -1, 1],
    ]
)
OPPOSITE = [0, 2, 1, 4, 3, 6, 5, 8, 7, 10, 9, 12, 11, 14, 13, 16, 15, 18, 17]
X_UP, X_DOWN = (1, 7, 9, 11, 13), (2, 8, 10, 12, 14)
Y_UP, Y_DOWN = (3, 7, 10, 15, 17), (4, 8, 9, 16, 18)
NEAR = [(dx, dy) for dx in range(-2, 3) for dy in range(-1, 2)]
HERE = NEAR.index((0, 0))
SENDS = [0, 2, 12, 14, 3, 5, 9, 11, 1, 13, 4, 10, 6, 8]
BESIDE = [t for t in SENDS if abs(NEAR[t][0]) < 2]
CORNERS = {7: (-1, -1), 8: (1, 1), 9: (-1, 1), 10: (1, -1)}
MOMENTS = 16
ROWS = 48


def moment_rows():
    vel_x, vel_y, vel_z = [VELOCITIES[:, component] * 1.0 for component in range(3)]
    monomials = [
        np.ones(19),
        vel_x,
        vel_y,
        vel_z,
        vel_x * vel_x,
        vel_y * vel_y,
        vel_z * vel_z,
        vel_x * vel_y,
        vel_x * vel_z,
        vel_y * vel_z,
        vel_x * vel_x * vel_y,
        vel_x * vel_x * vel_z,
        vel_y * vel_y * vel_x,
        vel_y * vel_y * vel_z,
        vel_z * vel_z * vel_x,
        vel_z * vel_z * vel_y,
        vel_x * vel_x * vel_y * vel_y,
        vel_x * vel_x * vel_z * vel_z,
        vel_y * vel_y * vel_z * vel_z,
    ]
    orthonormal = []
    for vector in monomials:
        vector = vector.copy()
        for earlier in orthonormal:
            vector = vector - np.dot(earlier, vector) * earlier
        orthonormal.append(vector / np.sqrt(np.dot(vector, vector)))
    return np.stack(orthonormal)


def coefficient_rows():
    rows = moment_rows()[4:]
    even = [1, 3, 5, 7, 11, 15]
    out = []
    for a in even:
        for b in even:
            keep = np.isin(np.arange(15), [0, 1, 2, 12, 13, 14])
            out.append(rows[:, a] * (rows[:, b] - rows[:, 0]) * keep)
    for axis, first, second, rates in ((1, 7, 11, (8, 10)), (3, 7, 15, (6, 11)), (5, 11, 15, (7, 9))):
        for a in (first, second):
            for b in (first, second):
                keep = np.isin(np.arange(15), rates)
                out.append(rows[:, a] * (rows[:, b] - rows[:, axis]) * keep)
    for rate in (3, 4, 5):
        out.append(0.25 * (np.arange(15) == rate))
    table = np.zeros((64, 16), np.float32)
    table[: len(out), :15] = np.stack(out)
    return table


def lane_shift(pop):
    return int(VELOCITIES[pop, 1]) * NZ + int(VELOCITIES[pop, 2])


def sphere_terms(density, codes, table, cell, first_slot):
    flow, square, cover = None, None, None
    for packed in codes:
        slot = (packed >> 8) + first_slot
        weight = (packed & 255).astype(F32) * (1.0 / 255.0) * density
        got = [
            jnp.take_along_axis(
                jnp.broadcast_to(table[n : n + 1, :], (CX, LANES)), slot,
                axis=1, mode="promise_in_bounds",
            )
            for n in range(9)
        ]
        rx, ry, rz = cell[0] - got[0], cell[1] - got[1], cell[2] - got[2]
        wx = got[3] + got[7] * rz - got[8] * ry
        wy = got[4] + got[8] * rx - got[6] * rz
        wz = got[5] + got[6] * ry - got[7] * rx
        bx, by, bz = weight * wx, weight * wy, weight * wz
        one = (bx, by, bz)
        two = (bx * wx, by * wy, bz * wz, bx * wy, bx * wz, by * wz)
        if flow is None:
            flow, square, cover = one, two, weight
        else:
            flow = [a + b for a, b in zip(flow, one)]
            square = [a + b for a, b in zip(square, two)]
            cover = cover + weight
    hx, hy, hz = [value * (1.0 / 12.0) for value in flow]
    qxx, qyy, qzz, qxy, qxz, qyz = square
    base = cover * (1.0 / 18.0) - (qxx + qyy + qzz) * (1.0 / 12.0)
    half = 0.5 * base
    exx, eyy, ezz = 0.125 * qxx, 0.125 * qyy, 0.125 * qzz
    exy, exz, eyz = 0.25 * qxy, 0.25 * qxz, 0.25 * qyz
    b_xy, b_xz, b_yz = half + (exx + eyy), half + (exx + ezz), half + (eyy + ezz)
    return {
        0: (6.0 * base, None),
        1: (base + 2.0 * exx, 2.0 * hx),
        3: (base + 2.0 * eyy, 2.0 * hy),
        5: (base + 2.0 * ezz, 2.0 * hz),
        7: (b_xy + exy, hx + hy),
        9: (b_xy - exy, hx - hy),
        11: (b_xz + exz, hx + hz),
        13: (b_xz - exz, hx - hz),
        15: (b_yz + eyz, hy + hz),
        17: (b_yz - eyz, hy - hz),
    }


def term_of(terms, pop):
    even, odd = terms[pop if pop % 2 else pop - 1]
    return even + odd if pop % 2 else even - odd


def kernel(
    pops_hbm, codes_hbm, cell_ref, vel_ref, spin_ref, rates_ref, coef_in,
    out, load_ref,
    f, codes, coef, post, parts, weights, split,
    state, message, arrived, table, loads, loads_in, scratch,
    in_sem, near_send, near_recv, load_send, load_recv,
):
    nx, ny = lax.axis_size("bx"), lax.axis_size("by")
    me_x, me_y = lax.axis_index("bx"), lax.axis_index("by")

    def device(t):
        dx, dy = NEAR[t]
        return (lax.rem(me_x + dx + nx, nx), lax.rem(me_y + dy + ny, ny))

    barrier = pltpu.get_barrier_semaphore()
    for t in SENDS:
        pl.semaphore_signal(barrier, inc=1, device_id=device(t), device_id_type=MESH)
    get_pops = pltpu.make_async_copy(pops_hbm, f, in_sem.at[1])
    get_pops.start()
    get_codes = pltpu.make_async_copy(codes_hbm, codes, in_sem.at[0])
    get_codes.start()

    lane = lax.broadcasted_iota(jnp.int32, (1, LANES), 1)
    sphere = lane & 3

    def along(values):
        return jnp.where(
            sphere < 2,
            jnp.where(sphere == 0, values[0], values[1]),
            jnp.where(sphere == 2, values[2], values[3]),
        )

    place = [cell_ref[0, 0, 0, k] + CX * cell_ref[1, 0, 0, k] for k in range(4)]
    rows = [along([v.astype(F32) for v in place])]
    rows.append(along([cell_ref[2, 0, 0, k].astype(F32) for k in range(4)]))
    for source in (vel_ref, spin_ref):
        for n in range(3):
            rows.append(along([source[n, 0, 0, k] for k in range(4)]))
    for n, row in enumerate(rows):
        state[n : n + 1, :] = row
    for t in SENDS:
        message[t, 0:8, :] = state[...]

    which = lax.broadcasted_iota(jnp.int32, (16, LANES), 0)
    rates = jnp.zeros((16, LANES), F32)
    for r in range(15):
        rates = jnp.where(which == r, rates_ref[r], rates)
    coef[...] = jnp.dot(
        coef_in[...], rates, precision=lax.Precision.HIGHEST, preferred_element_type=F32
    )

    lanes8 = lax.broadcasted_iota(jnp.int32, (CX, LANES), 1)
    rows8 = lax.broadcasted_iota(jnp.int32, (CX, LANES), 0)
    cell_x = rows8.astype(F32)
    cell_z = (lanes8 & (NZ - 1)).astype(F32)

    get_codes.wait()
    get_pops.wait()

    def fluid(chunk, carry):
        at = pl.ds(pl.multiple_of(chunk * LANES, LANES), LANES)
        p = [f[i, :, at] for i in range(19)]
        s = {a: p[a] + p[a + 1] for a in range(1, 19, 2)}
        d = {a: p[a] - p[a + 1] for a in range(1, 19, 2)}
        s_xy, a_xy = s[7] + s[9], s[7] - s[9]
        s_xz, a_xz = s[11] + s[13], s[11] - s[13]
        s_yz, a_yz = s[15] + s[17], s[15] - s[17]
        x1, x2 = d[7] + d[9], d[11] + d[13]
        y1, y2 = d[7] - d[9], d[15] + d[17]
        z1, z2 = d[11] - d[13], d[15] - d[17]
        density = (p[0] + s[1]) + (s[3] + s[5]) + (s_xy + s_xz) + s_yz
        jx, jy, jz = d[1] + x1 + x2, d[3] + y1 + y2, d[5] + z1 + z2
        inverse = 1.0 / density
        ux, uy, uz = jx * inverse, jy * inverse, jz * inverse
        code_of = [codes[layer, :, at] for layer in range(2)]
        cover = ((code_of[0] & 255) + (code_of[1] & 255)).astype(F32) * (1.0 / 255.0)

        my = ((lanes8 >> 6) + 2 * chunk).astype(F32)
        mz = cell_z - 32.0
        dx, dy, dz = density * cell_x, density * my, density * mz
        listed = (
            density, dx, dy, dz, dx * cell_x, dy * my, dz * mz, dx * my, dx * mz, dy * mz,
            jx, jy, jz, my * jz - mz * jy, mz * jx - cell_x * jz, cell_x * jy - my * jx,
        )
        for n, value in enumerate(listed):
            parts[chunk, CX * n : CX * (n + 1), :] = value

        keep = 1.0 - cover
        hx, hy, hz = 0.5 * jx * ux, 0.5 * jy * uy, 0.5 * jz * uz
        cxy, cxz, cyz = jx * uy, jx * uz, jy * uz
        base = density * (1.0 / 9.0) - (hx + hy + hz) * (1.0 / 3.0)
        e_x, e_y, e_z = base + hx, base + hy, base + hz
        e_xy, e_xz, e_yz = e_x + hy, e_x + hz, e_y + hz
        even = [s[1] - e_x, s[3] - e_y, s[5] - e_z, s_xy - e_xy, s_xz - e_xz, s_yz - e_yz]
        even = [keep * value for value in even]

        def c(n):
            return jnp.broadcast_to(coef[n : n + 1, :], (CX, LANES))

        sums = []
        for a in range(6):
            total = c(6 * a) * even[0]
            for b in range(1, 6):
                total = total + c(6 * a + b) * even[b]
            sums.append(total)
        third = 1.0 / 3.0
        odd = []
        for axis, (first, second, flow) in enumerate(((x1, x2, jx), (y1, y2, jy), (z1, z2, jz))):
            level = flow * third
            first, second = keep * (first - level), keep * (second - level)
            k = 36 + 4 * axis
            near = c(k) * first + c(k + 1) * second
            far = c(k + 2) * first + c(k + 3) * second
            odd.append((-2.0 * (near + far), near, far))
        n_xy = keep * (a_xy - cxy) * c(48)
        n_xz = keep * (a_xz - cxz) * c(49)
        n_yz = keep * (a_yz - cyz) * c(50)
        half, quarter = 0.5 * cover, 0.25 * cover
        gx, gy, gz = jx * (1.0 / 12.0), jy * (1.0 / 12.0), jz * (1.0 / 12.0)
        pairs = {
            1: (sums[0] + half * e_x, odd[0][0], 2.0 * gx),
            3: (sums[1] + half * e_y, odd[1][0], 2.0 * gy),
            5: (sums[2] + half * e_z, odd[2][0], 2.0 * gz),
            7: (sums[3] + n_xy + quarter * (e_xy + cxy), odd[0][1] + odd[1][1], gx + gy),
            9: (sums[3] - n_xy + quarter * (e_xy - cxy), odd[0][1] - odd[1][1], gx - gy),
            11: (sums[4] + n_xz + quarter * (e_xz + cxz), odd[0][2] + odd[2][1], gx + gz),
            13: (sums[4] - n_xz + quarter * (e_xz - cxz), odd[0][2] - odd[2][1], gx - gz),
            15: (sums[5] + n_yz + quarter * (e_yz + cyz), odd[1][2] + odd[2][2], gy + gz),
            17: (sums[5] - n_yz + quarter * (e_yz - cyz), odd[1][2] - odd[2][2], gy - gz),
        }
        rest = 2.0 * (sums[0] + sums[1] + sums[2]) + 4.0 * (sums[3] + sums[4] + sums[5])
        g = {0: p[0] + rest - 3.0 * cover * base}
        for a, (ev, od, flow) in pairs.items():
            od = od + cover * (d[a] - flow)
            g[a] = p[a] - ev - od
            g[a + 1] = p[a + 1] - ev + od
        for pop in range(19):
            post[pop, :, at] = g[pop]
        post[19, :, at] = density

        common = [density] + [value.astype(F32) for value in code_of]
        for row, names in ((CX - 1, X_UP), (0, X_DOWN)):
            t = NEAR.index((1 if row else -1, 0))
            for n, value in enumerate([g[pop] for pop in names] + common):
                message[t, pl.ds(8 + 8 * n + chunk, 1), :] = value[row : row + 1, :]
        return carry

    lax.fori_loop(0, CHUNKS, fluid, 0)

    codes_f = {c: [codes[layer, :, c * LANES : (c + 1) * LANES].astype(F32) for layer in range(2)] for c in (0, CHUNKS - 1)}
    for dy, names in ((1, Y_UP), (-1, Y_DOWN)):
        c = CHUNKS - 1 if dy > 0 else 0
        t = NEAR.index((0, dy))
        at = slice(c * LANES, (c + 1) * LANES)
        for n, value in enumerate([post[pop, :, at] for pop in (*names, 19)] + codes_f[c]):
            message[t, 8 + 8 * n : 16 + 8 * n, :] = value
    for pop, (sx, sy) in CORNERS.items():
        t = NEAR.index((-sx, -sy))
        row = CX - 1 if sx < 0 else 0
        c = CHUNKS - 1 if sy < 0 else 0
        at = slice(c * LANES, (c + 1) * LANES)
        for n, value in enumerate([post[pop, :, at], post[19, :, at]] + codes_f[c]):
            message[t, 8 + n : 9 + n, :] = value[row : row + 1, :]

    def length(t):
        dx, dy = NEAR[t]
        return 8 if abs(dx) == 2 else 16 if dx and dy else 72

    pl.semaphore_wait(barrier, 14)
    near = {}
    for n, t in enumerate(SENDS):
        there = 14 - t
        near[there] = pltpu.make_async_remote_copy(
            src_ref=message.at[t, 0 : length(t)], dst_ref=arrived.at[there, 0 : length(t)],
            send_sem=near_send.at[n], recv_sem=near_recv.at[there],
            device_id=device(t), device_id_type=MESH,
        )
        near[there].start()

    slot_rows = lax.broadcasted_iota(jnp.int32, (ROWS, CELLS), 0)

    def fill(row, carry):
        total = None
        for layer in range(2):
            packed = codes[layer, pl.ds(row, 1), :]
            level = (packed & 255).astype(F32)
            hit = jnp.where((packed >> 8) == slot_rows, level, 0.0)
            total = hit if total is None else total + hit
        weights[:, pl.ds(pl.multiple_of(row * CELLS, CELLS), CELLS)] = total.astype(jnp.bfloat16)
        return carry

    lax.fori_loop(0, CX, fill, 0)

    def halves(chunk, carry):
        for row in range(CX):
            value = parts[chunk, pl.ds(row, MOMENTS, stride=CX), :]
            high = value.astype(jnp.bfloat16).astype(F32)
            both = jnp.concatenate([high, value - high], axis=0)
            at = pl.multiple_of(row * CELLS + chunk * LANES, LANES)
            split[:, pl.ds(at, LANES)] = both.astype(jnp.bfloat16)
        return carry

    lax.fori_loop(0, CHUNKS, halves, 0)
    sums = lax.dot_general(
        split[...], weights[...], (((1,), (1,)), ((), ())), preferred_element_type=F32
    )
    loads[...] = jnp.zeros_like(loads)
    loads[:, 0:ROWS] = sums[0:MOMENTS] + sums[MOMENTS : 2 * MOMENTS]
    beside = {}
    for n, t in enumerate(BESIDE):
        there = 14 - t
        beside[there] = pltpu.make_async_remote_copy(
            src_ref=loads, dst_ref=loads_in.at[there],
            send_sem=load_send.at[n], recv_sem=load_recv.at[there],
            device_id=device(t), device_id_type=MESH,
        )
        beside[there].start()

    for t in SENDS:
        near[t].wait()
    group = (lanes8 - 4) >> 2
    full = jnp.where(group == HERE, state[...], 0.0)
    for t in SENDS:
        full = jnp.where(group == t, arrived[t, 0:8, :], full)
    place = full[0:1].astype(jnp.int32)
    group = group[0:1]
    group_x = (
        (group >= 3).astype(jnp.int32) + (group >= 6).astype(jnp.int32)
        + (group >= 9).astype(jnp.int32) + (group >= 12).astype(jnp.int32)
    )
    table[0:1, :] = ((place & (CX - 1)) + (group_x - 2) * CX).astype(F32)
    table[1:2, :] = ((place >> 3) + (group - 3 * group_x - 1) * CY).astype(F32)
    table[2:9, :] = full[1:8]

    def covers(chunk, carry):
        at = pl.ds(pl.multiple_of(chunk * LANES, LANES), LANES)
        cell_y = ((lanes8 >> 6) + 2 * chunk).astype(F32)
        terms = sphere_terms(
            post[19, :, at], [codes[layer, :, at] for layer in range(2)], table,
            (cell_x, cell_y, cell_z), 4 + 4 * 3,
        )
        post[0, :, at] = post[0, :, at] + terms[0][0]
        for pop in range(1, 19):
            post[pop, :, at] = post[pop, :, at] + term_of(terms, pop)
        return carry

    lax.fori_loop(0, CHUNKS, covers, 0)

    lower = lanes8 < NZ
    halo_x = {}
    for side, names in ((0, X_UP), (1, X_DOWN)):
        t = NEAR.index((-1 if side == 0 else 1, 0))
        got = [arrived[t, 8 + 8 * n : 16 + 8 * n, :] for n in range(8)]
        cells = (
            jnp.full((CX, LANES), -1.0 if side == 0 else float(CX), F32),
            (2 * rows8 + (lanes8 >> 6)).astype(F32),
            cell_z,
        )
        terms = sphere_terms(
            got[5], [v.astype(jnp.int32) for v in got[6:8]], table, cells, 16 + (-12 if side == 0 else 12)
        )
        for n, pop in enumerate(names):
            value = got[n] + term_of(terms, pop)
            shift = lane_shift(pop) % LANES
            if shift:
                value = pltpu.roll(value, shift, 1)
            step_y = int(VELOCITIES[pop, 1])
            if step_y:
                crossed = lower if step_y > 0 else jnp.logical_not(lower)
                value = jnp.where(crossed, pltpu.roll(value, step_y % CX, 0), value)
            halo_x[pop] = value
    from_low, from_high = NEAR.index((0, -1)), NEAR.index((0, 1))
    got_low = [arrived[from_low, 8 + 8 * n : 16 + 8 * n, :] for n in range(8)]
    got_high = [arrived[from_high, 8 + 8 * n : 16 + 8 * n, :] for n in range(8)]
    mixed = [jnp.where(lower, got_high[n], got_low[n]) for n in range(5, 8)]
    cells = (cell_x, jnp.where(lower, float(CY), -1.0), cell_z)
    terms = sphere_terms(
        mixed[0], [v.astype(jnp.int32) for v in mixed[1:]], table, cells, jnp.where(lower, 20, 12)
    )
    halo_y = {}
    for names, got in ((Y_UP, got_low), (Y_DOWN, got_high)):
        for n, pop in enumerate(names):
            value = got[n] + term_of(terms, pop)
            value = pltpu.roll(value, lane_shift(pop) % LANES, 1)
            step_x = int(VELOCITIES[pop, 0])
            if step_x:
                value = pltpu.roll(value, step_x % CX, 0)
            halo_y[pop] = value
    corner = [jnp.zeros((CX, LANES), F32) for _ in range(4)]
    corner_x = corner_y = jnp.zeros((CX, LANES), F32)
    corner_slot = jnp.zeros((CX, LANES), jnp.int32)
    for row, (pop, (sx, sy)) in enumerate(CORNERS.items()):
        t = NEAR.index((sx, sy))
        here = rows8 == row
        for n in range(4):
            piece = jnp.broadcast_to(arrived[t, 8 + n : 9 + n, :], (CX, LANES))
            corner[n] = jnp.where(here, piece, corner[n])
        corner_x = jnp.where(here, -1.0 if sx < 0 else float(CX), corner_x)
        corner_y = jnp.where(here, -1.0 if sy < 0 else float(CY), corner_y)
        corner_slot = jnp.where(here, 16 + 12 * sx + 4 * sy, corner_slot)
    terms = sphere_terms(
        corner[1], [v.astype(jnp.int32) for v in corner[2:4]], table, (corner_x, corner_y, cell_z), corner_slot
    )
    corner_term = jnp.zeros((CX, LANES), F32)
    for row, pop in enumerate(CORNERS):
        corner_term = jnp.where(rows8 == row, term_of(terms, pop), corner_term)
    corner_of = pltpu.roll(corner[0] + corner_term, NZ, 1)

    z_of = lax.broadcasted_iota(jnp.int32, (CX, CELLS), 1) & (NZ - 1)
    edge = {1: z_of == 0, -1: z_of == NZ - 1}
    row_of = lax.broadcasted_iota(jnp.int32, (CX, CELLS), 0)
    for n, pop in enumerate((*X_UP, *X_DOWN)):
        scratch[n] = halo_x[pop]
    for pop in range(19):
        step_x, step_y, step_z = (int(v) for v in VELOCITIES[pop])
        value = post[pop]
        shift = lane_shift(pop) % CELLS
        if shift:
            value = pltpu.roll(value, shift, 1)
        if step_x:
            value = pltpu.roll(value, step_x % CX, 0)
            row = 0 if step_x > 0 else CX - 1
            n = (*X_UP, *X_DOWN).index(pop)
            beside_x = jnp.concatenate(
                [jnp.broadcast_to(scratch[n, c : c + 1, :], (CX, LANES)) for c in range(CHUNKS)], axis=1
            )
            value = jnp.where(row_of == row, beside_x, value)
        if step_y:
            tile = halo_y[pop]
            if step_x:
                k = list(CORNERS).index(pop)
                tile = jnp.where(rows8 == row, jnp.broadcast_to(corner_of[k : k + 1], (CX, LANES)), tile)
            if step_y > 0:
                value = jnp.concatenate([jnp.where(lower, tile, value[:, :LANES]), value[:, LANES:]], axis=1)
            else:
                value = jnp.concatenate([value[:, :-LANES], jnp.where(lower, value[:, -LANES:], tile)], axis=1)
        if step_z:
            value = jnp.where(edge[step_z], post[OPPOSITE[pop]], value)
        out[pop] = value

    for t in BESIDE:
        beside[t].wait()
    lanes16 = lax.broadcasted_iota(jnp.int32, (MOMENTS, LANES), 1) >> 2
    moment = jnp.where(lanes16 == 4, loads[...], 0.0)
    for t in BESIDE:
        dx, dy = NEAR[t]
        moment = jnp.where(lanes16 == (1 - dx) * 3 + 1 - dy, loads_in[t], moment)
    m = [moment[n : n + 1, :] for n in range(MOMENTS)]
    group = lane >> 2
    group_x = (group >= 3).astype(jnp.int32) + (group >= 6).astype(jnp.int32)
    place = state[0:1, :].astype(jnp.int32)
    cx = ((place & (CX - 1)) + (group_x - 1) * CX).astype(F32)
    cy = ((place >> 3) + (group - 3 * group_x - 1) * CY).astype(F32)
    cz = state[1:2, :] - 32.0
    vx, vy, vz, sx, sy, sz = [state[n : n + 1, :] for n in range(2, 8)]
    ex, ey, ez = m[1] - cx * m[0], m[2] - cy * m[0], m[3] - cz * m[0]
    qxx = m[4] - cx * (m[1] + ex)
    qyy = m[5] - cy * (m[2] + ey)
    qzz = m[6] - cz * (m[3] + ez)
    qxy = m[7] - cx * m[2] - cy * ex
    qxz = m[8] - cx * m[3] - cz * ex
    qyz = m[9] - cy * m[3] - cz * ey
    fx = m[10] - vx * m[0] - (sy * ez - sz * ey)
    fy = m[11] - vy * m[0] - (sz * ex - sx * ez)
    fz = m[12] - vz * m[0] - (sx * ey - sy * ex)
    tx = m[13] - (cy * m[12] - cz * m[11]) - (ey * vz - ez * vy) - (sx * (qyy + qzz) - sy * qxy - sz * qxz)
    ty = m[14] - (cz * m[10] - cx * m[12]) - (ez * vx - ex * vz) - (sy * (qxx + qzz) - sx * qxy - sz * qyz)
    tz = m[15] - (cx * m[11] - cy * m[10]) - (ex * vy - ey * vx) - (sz * (qxx + qyy) - sx * qxz - sy * qyz)
    force, torque = 1.0 / (255.0 * RADIUS**2), 1.0 / (255.0 * RADIUS**3)
    listed = (fx * force, fy * force, fz * force, tx * torque, ty * torque, tz * torque)
    tile = jnp.zeros((CX, LANES), F32)
    for n, value in enumerate(listed):
        tile = jnp.where(rows8 == n, jnp.broadcast_to(value, (CX, LANES)), tile)
    tile = jnp.where(lanes8 < 36, tile, 0.0)
    total = tile
    for g in range(1, 9):
        total = total + pltpu.roll(tile, LANES - 4 * g, 1)
    load_ref[...] = total.T[0:4, 0:6]


def per_device(populations, cover_codes, sphere_cell, sphere_velocity, sphere_spin, relax_rates):
    vmem, smem, anywhere = (
        pl.BlockSpec(memory_space=pltpu.VMEM),
        pl.BlockSpec(memory_space=pltpu.SMEM),
        pl.BlockSpec(memory_space=pl.ANY),
    )
    dma = pltpu.SemaphoreType.DMA
    out, load = pl.pallas_call(
        kernel,
        out_shape=(
            pltpu.VMEM((19, CX, CELLS), F32),
            jax.ShapeDtypeStruct((4, 6), F32),
        ),
        in_specs=[anywhere, anywhere, smem, smem, smem, smem, vmem],
        out_specs=(vmem, vmem),
        scratch_shapes=[
            pltpu.VMEM((19, CX, CELLS), F32),
            pltpu.VMEM((2, CX, CELLS), jnp.int32),
            pltpu.VMEM((64, LANES), F32),
            pltpu.VMEM((20, CX, CELLS), F32),
            pltpu.VMEM((CHUNKS, MOMENTS * CX, LANES), F32),
            pltpu.VMEM((ROWS, CX * CELLS), jnp.bfloat16),
            pltpu.VMEM((2 * MOMENTS, CX * CELLS), jnp.bfloat16),
            pltpu.VMEM((8, LANES), F32),
            pltpu.VMEM((15, 72, LANES), F32),
            pltpu.VMEM((15, 72, LANES), F32),
            pltpu.VMEM((16, LANES), F32),
            pltpu.VMEM((MOMENTS, LANES), F32),
            pltpu.VMEM((15, MOMENTS, LANES), F32),
            pltpu.VMEM((10, CX, LANES), F32),
            dma((2,)),
            dma((14,)),
            dma((15,)),
            dma((8,)),
            dma((15,)),
        ],
        compiler_params=pltpu.CompilerParams(
            collective_id=0, has_side_effects=True, vmem_limit_bytes=60 * 1024 * 1024
        ),
    )(
        populations, cover_codes, sphere_cell, sphere_velocity, sphere_spin, relax_rates,
        jnp.asarray(coefficient_rows()),
    )
    return out, load.T.reshape(6, 1, 1, 4)


def solution(mesh):
    placed = (
        P(None, "bx", "by"),
        P(None, "bx", "by"),
        P(None, "bx", "by", None),
        P(None, "bx", "by", None),
        P(None, "bx", "by", None),
        P(),
    )
    return jax.shard_map(
        per_device,
        mesh=mesh,
        in_specs=placed,
        out_specs=(P(None, "bx", "by"), P(None, "bx", "by", None)),
        check_vma=False,
    )
```

```python
import jax
import jax.numpy as jnp
import numpy as np
from jax import lax
from jax.experimental import pallas as pl
from jax.experimental.pallas import tpu as pltpu
from jax.sharding import PartitionSpec as P

NZ = 64
RADIUS = 8
CX, CY = 8, 16
CELLS = CY * NZ
LANES = 128
CHUNKS = CELLS // LANES
MESH = pl.DeviceIdType.MESH
F32 = jnp.float32

VELOCITIES = np.array(
    [
        [0, 0, 0],
        [1, 0, 0],
        [-1, 0, 0],
        [0, 1, 0],
        [0, -1, 0],
        [0, 0, 1],
        [0, 0, -1],
        [1, 1, 0],
        [-1, -1, 0],
        [1, -1, 0],
        [-1, 1, 0],
        [1, 0, 1],
        [-1, 0, -1],
        [1, 0, -1],
        [-1, 0, 1],
        [0, 1, 1],
        [0, -1, -1],
        [0, 1, -1],
        [0, -1, 1],
    ]
)
OPPOSITE = [0, 2, 1, 4, 3, 6, 5, 8, 7, 10, 9, 12, 11, 14, 13, 16, 15, 18, 17]
X_UP, X_DOWN = (1, 7, 9, 11, 13), (2, 8, 10, 12, 14)
Y_UP, Y_DOWN = (3, 7, 10, 15, 17), (4, 8, 9, 16, 18)
NEAR = [(dx, dy) for dx in range(-2, 3) for dy in range(-1, 2)]
HERE = NEAR.index((0, 0))
SENDS = [0, 2, 12, 14, 3, 5, 9, 11, 1, 13, 4, 10, 6, 8]
BESIDE = [t for t in SENDS if abs(NEAR[t][0]) < 2]
CORNERS = {7: (-1, -1), 8: (1, 1), 9: (-1, 1), 10: (1, -1)}
MOMENTS = 16
ROWS = 48


def moment_rows():
    vel_x, vel_y, vel_z = [VELOCITIES[:, component] * 1.0 for component in range(3)]
    monomials = [
        np.ones(19),
        vel_x,
        vel_y,
        vel_z,
        vel_x * vel_x,
        vel_y * vel_y,
        vel_z * vel_z,
        vel_x * vel_y,
        vel_x * vel_z,
        vel_y * vel_z,
        vel_x * vel_x * vel_y,
        vel_x * vel_x * vel_z,
        vel_y * vel_y * vel_x,
        vel_y * vel_y * vel_z,
        vel_z * vel_z * vel_x,
        vel_z * vel_z * vel_y,
        vel_x * vel_x * vel_y * vel_y,
        vel_x * vel_x * vel_z * vel_z,
        vel_y * vel_y * vel_z * vel_z,
    ]
    orthonormal = []
    for vector in monomials:
        vector = vector.copy()
        for earlier in orthonormal:
            vector = vector - np.dot(earlier, vector) * earlier
        orthonormal.append(vector / np.sqrt(np.dot(vector, vector)))
    return np.stack(orthonormal)


def coefficient_rows():
    rows = moment_rows()[4:]
    even = [1, 3, 5, 7, 11, 15]
    out = []
    for a in even:
        for b in even:
            keep = np.isin(np.arange(15), [0, 1, 2, 12, 13, 14])
            out.append(rows[:, a] * (rows[:, b] - rows[:, 0]) * keep)
    for axis, first, second, rates in ((1, 7, 11, (8, 10)), (3, 7, 15, (6, 11)), (5, 11, 15, (7, 9))):
        for a in (first, second):
            for b in (first, second):
                keep = np.isin(np.arange(15), rates)
                out.append(rows[:, a] * (rows[:, b] - rows[:, axis]) * keep)
    for rate in (3, 4, 5):
        out.append(0.25 * (np.arange(15) == rate))
    table = np.zeros((64, 16), np.float32)
    table[: len(out), :15] = np.stack(out)
    return table


def lane_shift(pop):
    return int(VELOCITIES[pop, 1]) * NZ + int(VELOCITIES[pop, 2])


def sphere_terms(density, codes, table, cell, first_slot):
    flow, square, cover = None, None, None
    for packed in codes:
        slot = (packed >> 8) + first_slot
        weight = (packed & 255).astype(F32) * (1.0 / 255.0) * density
        got = [
            jnp.take_along_axis(
                jnp.broadcast_to(table[n : n + 1, :], (CX, LANES)), slot,
                axis=1, mode="promise_in_bounds",
            )
            for n in range(9)
        ]
        rx, ry, rz = cell[0] - got[0], cell[1] - got[1], cell[2] - got[2]
        wx = got[3] + got[7] * rz - got[8] * ry
        wy = got[4] + got[8] * rx - got[6] * rz
        wz = got[5] + got[6] * ry - got[7] * rx
        bx, by, bz = weight * wx, weight * wy, weight * wz
        one = (bx, by, bz)
        two = (bx * wx, by * wy, bz * wz, bx * wy, bx * wz, by * wz)
        if flow is None:
            flow, square, cover = one, two, weight
        else:
            flow = [a + b for a, b in zip(flow, one)]
            square = [a + b for a, b in zip(square, two)]
            cover = cover + weight
    hx, hy, hz = [value * (1.0 / 12.0) for value in flow]
    qxx, qyy, qzz, qxy, qxz, qyz = square
    base = cover * (1.0 / 18.0) - (qxx + qyy + qzz) * (1.0 / 12.0)
    half = 0.5 * base
    exx, eyy, ezz = 0.125 * qxx, 0.125 * qyy, 0.125 * qzz
    exy, exz, eyz = 0.25 * qxy, 0.25 * qxz, 0.25 * qyz
    b_xy, b_xz, b_yz = half + (exx + eyy), half + (exx + ezz), half + (eyy + ezz)
    return {
        0: (6.0 * base, None),
        1: (base + 2.0 * exx, 2.0 * hx),
        3: (base + 2.0 * eyy, 2.0 * hy),
        5: (base + 2.0 * ezz, 2.0 * hz),
        7: (b_xy + exy, hx + hy),
        9: (b_xy - exy, hx - hy),
        11: (b_xz + exz, hx + hz),
        13: (b_xz - exz, hx - hz),
        15: (b_yz + eyz, hy + hz),
        17: (b_yz - eyz, hy - hz),
    }


def term_of(terms, pop):
    even, odd = terms[pop if pop % 2 else pop - 1]
    return even + odd if pop % 2 else even - odd


def kernel(
    pops_hbm, codes_hbm, cell_hbm, vel_hbm, spin_hbm, rates_hbm, coef_hbm,
    post, halo, corner_out, load_ref,
    cell_ref, vel_ref, spin_ref, rates_ref, coef_in, f, codes, coef, parts, weights, split,
    state, message, arrived, table, loads, loads_in,
    in_sem, near_send, near_recv, load_send, load_recv,
):
    nx, ny = lax.axis_size("bx"), lax.axis_size("by")
    me_x, me_y = lax.axis_index("bx"), lax.axis_index("by")

    def device(t):
        dx, dy = NEAR[t]
        return (lax.rem(me_x + dx + nx, nx), lax.rem(me_y + dy + ny, ny))

    barrier = pltpu.get_barrier_semaphore()
    for t in SENDS:
        pl.semaphore_signal(barrier, inc=1, device_id=device(t), device_id_type=MESH)
    fetched = []
    for n, (src, dst) in enumerate(
        (
            (cell_hbm, cell_ref), (vel_hbm, vel_ref), (spin_hbm, spin_ref), (rates_hbm, rates_ref),
            (coef_hbm, coef_in), (codes_hbm, codes), (pops_hbm, f),
        )
    ):
        fetched.append(pltpu.make_async_copy(src, dst, in_sem.at[n]))
        fetched[-1].start()

    lane = lax.broadcasted_iota(jnp.int32, (1, LANES), 1)
    sphere = lane & 3

    def along(values):
        return jnp.where(
            sphere < 2,
            jnp.where(sphere == 0, values[0], values[1]),
            jnp.where(sphere == 2, values[2], values[3]),
        )

    for copy in fetched[:5]:
        copy.wait()
    place = [cell_ref[0, 0, 0, k] + CX * cell_ref[1, 0, 0, k] for k in range(4)]
    rows = [along([v.astype(F32) for v in place])]
    rows.append(along([cell_ref[2, 0, 0, k].astype(F32) for k in range(4)]))
    for source in (vel_ref, spin_ref):
        for n in range(3):
            rows.append(along([source[n, 0, 0, k] for k in range(4)]))
    for n, row in enumerate(rows):
        state[n : n + 1, :] = row
    for t in SENDS:
        message[t, 0:8, :] = state[...]

    which = lax.broadcasted_iota(jnp.int32, (16, LANES), 0)
    rates = jnp.zeros((16, LANES), F32)
    for r in range(15):
        rates = jnp.where(which == r, rates_ref[r], rates)
    coef[...] = jnp.dot(
        coef_in[...], rates, precision=lax.Precision.HIGHEST, preferred_element_type=F32
    )

    lanes8 = lax.broadcasted_iota(jnp.int32, (CX, LANES), 1)
    rows8 = lax.broadcasted_iota(jnp.int32, (CX, LANES), 0)
    cell_x = rows8.astype(F32)
    cell_z = (lanes8 & (NZ - 1)).astype(F32)

    fetched[5].wait()
    slot_rows = lax.broadcasted_iota(jnp.int32, (ROWS, CELLS), 0)

    def fill(row, carry):
        total = None
        for layer in range(2):
            packed = codes[layer, pl.ds(row, 1), :]
            level = (packed & 255).astype(F32)
            hit = jnp.where((packed >> 8) == slot_rows, level, 0.0)
            total = hit if total is None else total + hit
        weights[:, pl.ds(pl.multiple_of(row * CELLS, CELLS), CELLS)] = total.astype(jnp.bfloat16)
        return carry

    lax.fori_loop(0, CX, fill, 0, unroll=8)
    fetched[6].wait()

    def fluid(chunk, carry):
        at = pl.ds(pl.multiple_of(chunk * LANES, LANES), LANES)
        p = [f[i, :, at] for i in range(19)]
        s = {a: p[a] + p[a + 1] for a in range(1, 19, 2)}
        d = {a: p[a] - p[a + 1] for a in range(1, 19, 2)}
        s_xy, a_xy = s[7] + s[9], s[7] - s[9]
        s_xz, a_xz = s[11] + s[13], s[11] - s[13]
        s_yz, a_yz = s[15] + s[17], s[15] - s[17]
        x1, x2 = d[7] + d[9], d[11] + d[13]
        y1, y2 = d[7] - d[9], d[15] + d[17]
        z1, z2 = d[11] - d[13], d[15] - d[17]
        density = (p[0] + s[1]) + (s[3] + s[5]) + (s_xy + s_xz) + s_yz
        jx, jy, jz = d[1] + x1 + x2, d[3] + y1 + y2, d[5] + z1 + z2
        inverse = 1.0 / density
        ux, uy, uz = jx * inverse, jy * inverse, jz * inverse
        code_of = [codes[layer, :, at] for layer in range(2)]
        cover = ((code_of[0] & 255) + (code_of[1] & 255)).astype(F32) * (1.0 / 255.0)

        my = ((lanes8 >> 6) + 2 * chunk).astype(F32)
        mz = cell_z - 32.0
        dx, dy, dz = density * cell_x, density * my, density * mz
        listed = (
            density, dx, dy, dz, dx * cell_x, dy * my, dz * mz, dx * my, dx * mz, dy * mz,
            jx, jy, jz, my * jz - mz * jy, mz * jx - cell_x * jz, cell_x * jy - my * jx,
        )
        for n, value in enumerate(listed):
            parts[chunk, CX * n : CX * (n + 1), :] = value

        keep = 1.0 - cover
        hx, hy, hz = 0.5 * jx * ux, 0.5 * jy * uy, 0.5 * jz * uz
        cxy, cxz, cyz = jx * uy, jx * uz, jy * uz
        base = density * (1.0 / 9.0) - (hx + hy + hz) * (1.0 / 3.0)
        e_x, e_y, e_z = base + hx, base + hy, base + hz
        e_xy, e_xz, e_yz = e_x + hy, e_x + hz, e_y + hz
        even = [s[1] - e_x, s[3] - e_y, s[5] - e_z, s_xy - e_xy, s_xz - e_xz, s_yz - e_yz]
        even = [keep * value for value in even]

        def c(n):
            return jnp.broadcast_to(coef[n : n + 1, :], (CX, LANES))

        sums = []
        for a in range(6):
            total = c(6 * a) * even[0]
            for b in range(1, 6):
                total = total + c(6 * a + b) * even[b]
            sums.append(total)
        third = 1.0 / 3.0
        odd = []
        for axis, (first, second, flow) in enumerate(((x1, x2, jx), (y1, y2, jy), (z1, z2, jz))):
            level = flow * third
            first, second = keep * (first - level), keep * (second - level)
            k = 36 + 4 * axis
            near = c(k) * first + c(k + 1) * second
            far = c(k + 2) * first + c(k + 3) * second
            odd.append((-2.0 * (near + far), near, far))
        n_xy = keep * (a_xy - cxy) * c(48)
        n_xz = keep * (a_xz - cxz) * c(49)
        n_yz = keep * (a_yz - cyz) * c(50)
        half, quarter = 0.5 * cover, 0.25 * cover
        gx, gy, gz = jx * (1.0 / 12.0), jy * (1.0 / 12.0), jz * (1.0 / 12.0)
        pairs = {
            1: (sums[0] + half * e_x, odd[0][0], 2.0 * gx),
            3: (sums[1] + half * e_y, odd[1][0], 2.0 * gy),
            5: (sums[2] + half * e_z, odd[2][0], 2.0 * gz),
            7: (sums[3] + n_xy + quarter * (e_xy + cxy), odd[0][1] + odd[1][1], gx + gy),
            9: (sums[3] - n_xy + quarter * (e_xy - cxy), odd[0][1] - odd[1][1], gx - gy),
            11: (sums[4] + n_xz + quarter * (e_xz + cxz), odd[0][2] + odd[2][1], gx + gz),
            13: (sums[4] - n_xz + quarter * (e_xz - cxz), odd[0][2] - odd[2][1], gx - gz),
            15: (sums[5] + n_yz + quarter * (e_yz + cyz), odd[1][2] + odd[2][2], gy + gz),
            17: (sums[5] - n_yz + quarter * (e_yz - cyz), odd[1][2] - odd[2][2], gy - gz),
        }
        rest = 2.0 * (sums[0] + sums[1] + sums[2]) + 4.0 * (sums[3] + sums[4] + sums[5])
        g = {0: p[0] + rest - 3.0 * cover * base}
        for a, (ev, od, flow) in pairs.items():
            od = od + cover * (d[a] - flow)
            g[a] = p[a] - ev - od
            g[a + 1] = p[a + 1] - ev + od
        for pop in range(19):
            post[pop, :, at] = g[pop]
        post[19, :, at] = density

        common = [density] + [value.astype(F32) for value in code_of]
        for row, names in ((CX - 1, X_UP), (0, X_DOWN)):
            t = NEAR.index((1 if row else -1, 0))
            for n, value in enumerate([g[pop] for pop in names] + common):
                message[t, pl.ds(8 + 8 * n + chunk, 1), :] = value[row : row + 1, :]
        return carry

    lax.fori_loop(0, CHUNKS, fluid, 0, unroll=8)

    codes_f = {c: [codes[layer, :, c * LANES : (c + 1) * LANES].astype(F32) for layer in range(2)] for c in (0, CHUNKS - 1)}
    for dy, names in ((1, Y_UP), (-1, Y_DOWN)):
        c = CHUNKS - 1 if dy > 0 else 0
        t = NEAR.index((0, dy))
        at = slice(c * LANES, (c + 1) * LANES)
        for n, value in enumerate([post[pop, :, at] for pop in (*names, 19)] + codes_f[c]):
            message[t, 8 + 8 * n : 16 + 8 * n, :] = value
    for pop, (sx, sy) in CORNERS.items():
        t = NEAR.index((-sx, -sy))
        row = CX - 1 if sx < 0 else 0
        c = CHUNKS - 1 if sy < 0 else 0
        at = slice(c * LANES, (c + 1) * LANES)
        for n, value in enumerate([post[pop, :, at], post[19, :, at]] + codes_f[c]):
            message[t, 8 + n : 9 + n, :] = value[row : row + 1, :]

    def length(t):
        dx, dy = NEAR[t]
        return 8 if abs(dx) == 2 else 16 if dx and dy else 72

    pl.semaphore_wait(barrier, 14)
    near = {}
    for n, t in enumerate(SENDS):
        there = 14 - t
        near[there] = pltpu.make_async_remote_copy(
            src_ref=message.at[t, 0 : length(t)], dst_ref=arrived.at[there, 0 : length(t)],
            send_sem=near_send.at[n], recv_sem=near_recv.at[there],
            device_id=device(t), device_id_type=MESH,
        )
        near[there].start()

    def halves(chunk, carry):
        for row in range(CX):
            value = parts[chunk, pl.ds(row, MOMENTS, stride=CX), :]
            high = value.astype(jnp.bfloat16).astype(F32)
            both = jnp.concatenate([high, value - high], axis=0)
            at = pl.multiple_of(row * CELLS + chunk * LANES, LANES)
            split[:, pl.ds(at, LANES)] = both.astype(jnp.bfloat16)
        return carry

    lax.fori_loop(0, CHUNKS, halves, 0, unroll=8)
    sums = lax.dot_general(
        split[...], weights[...], (((1,), (1,)), ((), ())), preferred_element_type=F32
    )
    loads[...] = jnp.zeros_like(loads)
    loads[:, 0:ROWS] = sums[0:MOMENTS] + sums[MOMENTS : 2 * MOMENTS]
    beside = {}
    for n, t in enumerate(BESIDE):
        there = 14 - t
        beside[there] = pltpu.make_async_remote_copy(
            src_ref=loads, dst_ref=loads_in.at[there],
            send_sem=load_send.at[n], recv_sem=load_recv.at[there],
            device_id=device(t), device_id_type=MESH,
        )
        beside[there].start()

    for t in SENDS:
        near[t].wait()
    group = (lanes8 - 4) >> 2
    full = jnp.where(group == HERE, state[...], 0.0)
    for t in SENDS:
        full = jnp.where(group == t, arrived[t, 0:8, :], full)
    place = full[0:1].astype(jnp.int32)
    group = group[0:1]
    group_x = (
        (group >= 3).astype(jnp.int32) + (group >= 6).astype(jnp.int32)
        + (group >= 9).astype(jnp.int32) + (group >= 12).astype(jnp.int32)
    )
    table[0:1, :] = ((place & (CX - 1)) + (group_x - 2) * CX).astype(F32)
    table[1:2, :] = ((place >> 3) + (group - 3 * group_x - 1) * CY).astype(F32)
    table[2:9, :] = full[1:8]

    def covers(chunk, carry):
        at = pl.ds(pl.multiple_of(chunk * LANES, LANES), LANES)
        cell_y = ((lanes8 >> 6) + 2 * chunk).astype(F32)
        terms = sphere_terms(
            post[19, :, at], [codes[layer, :, at] for layer in range(2)], table,
            (cell_x, cell_y, cell_z), 4 + 4 * 3,
        )
        post[0, :, at] = post[0, :, at] + terms[0][0]
        for pop in range(1, 19):
            post[pop, :, at] = post[pop, :, at] + term_of(terms, pop)
        return carry

    lax.fori_loop(0, CHUNKS, covers, 0, unroll=8)

    lower = lanes8 < NZ
    halo_x = {}
    for side, names in ((0, X_UP), (1, X_DOWN)):
        t = NEAR.index((-1 if side == 0 else 1, 0))
        got = [arrived[t, 8 + 8 * n : 16 + 8 * n, :] for n in range(8)]
        cells = (
            jnp.full((CX, LANES), -1.0 if side == 0 else float(CX), F32),
            (2 * rows8 + (lanes8 >> 6)).astype(F32),
            cell_z,
        )
        terms = sphere_terms(
            got[5], [v.astype(jnp.int32) for v in got[6:8]], table, cells, 16 + (-12 if side == 0 else 12)
        )
        for n, pop in enumerate(names):
            value = got[n] + term_of(terms, pop)
            shift = lane_shift(pop) % LANES
            if shift:
                value = pltpu.roll(value, shift, 1)
            step_y = int(VELOCITIES[pop, 1])
            if step_y:
                crossed = lower if step_y > 0 else jnp.logical_not(lower)
                value = jnp.where(crossed, pltpu.roll(value, step_y % CX, 0), value)
            halo_x[pop] = value
    from_low, from_high = NEAR.index((0, -1)), NEAR.index((0, 1))
    got_low = [arrived[from_low, 8 + 8 * n : 16 + 8 * n, :] for n in range(8)]
    got_high = [arrived[from_high, 8 + 8 * n : 16 + 8 * n, :] for n in range(8)]
    mixed = [jnp.where(lower, got_high[n], got_low[n]) for n in range(5, 8)]
    cells = (cell_x, jnp.where(lower, float(CY), -1.0), cell_z)
    terms = sphere_terms(
        mixed[0], [v.astype(jnp.int32) for v in mixed[1:]], table, cells, jnp.where(lower, 20, 12)
    )
    halo_y = {}
    for names, got in ((Y_UP, got_low), (Y_DOWN, got_high)):
        for n, pop in enumerate(names):
            value = got[n] + term_of(terms, pop)
            value = pltpu.roll(value, lane_shift(pop) % LANES, 1)
            step_x = int(VELOCITIES[pop, 0])
            if step_x:
                value = pltpu.roll(value, step_x % CX, 0)
            halo_y[pop] = value
    corner = [jnp.zeros((CX, LANES), F32) for _ in range(4)]
    corner_x = corner_y = jnp.zeros((CX, LANES), F32)
    corner_slot = jnp.zeros((CX, LANES), jnp.int32)
    for row, (pop, (sx, sy)) in enumerate(CORNERS.items()):
        t = NEAR.index((sx, sy))
        here = rows8 == row
        for n in range(4):
            piece = jnp.broadcast_to(arrived[t, 8 + n : 9 + n, :], (CX, LANES))
            corner[n] = jnp.where(here, piece, corner[n])
        corner_x = jnp.where(here, -1.0 if sx < 0 else float(CX), corner_x)
        corner_y = jnp.where(here, -1.0 if sy < 0 else float(CY), corner_y)
        corner_slot = jnp.where(here, 16 + 12 * sx + 4 * sy, corner_slot)
    terms = sphere_terms(
        corner[1], [v.astype(jnp.int32) for v in corner[2:4]], table, (corner_x, corner_y, cell_z), corner_slot
    )
    corner_term = jnp.zeros((CX, LANES), F32)
    for row, pop in enumerate(CORNERS):
        corner_term = jnp.where(rows8 == row, term_of(terms, pop), corner_term)
    corner_of = pltpu.roll(corner[0] + corner_term, NZ, 1)

    for n, pop in enumerate((*X_UP, *X_DOWN)):
        halo[0, n] = halo_x[pop]
    for n, pop in enumerate((*Y_UP, *Y_DOWN)):
        halo[1, n] = halo_y[pop]
    corner_out[...] = corner_of

    for t in BESIDE:
        beside[t].wait()
    lanes16 = lax.broadcasted_iota(jnp.int32, (MOMENTS, LANES), 1) >> 2
    moment = jnp.where(lanes16 == 4, loads[...], 0.0)
    for t in BESIDE:
        dx, dy = NEAR[t]
        moment = jnp.where(lanes16 == (1 - dx) * 3 + 1 - dy, loads_in[t], moment)
    m = [moment[n : n + 1, :] for n in range(MOMENTS)]
    group = lane >> 2
    group_x = (group >= 3).astype(jnp.int32) + (group >= 6).astype(jnp.int32)
    place = state[0:1, :].astype(jnp.int32)
    cx = ((place & (CX - 1)) + (group_x - 1) * CX).astype(F32)
    cy = ((place >> 3) + (group - 3 * group_x - 1) * CY).astype(F32)
    cz = state[1:2, :] - 32.0
    vx, vy, vz, sx, sy, sz = [state[n : n + 1, :] for n in range(2, 8)]
    ex, ey, ez = m[1] - cx * m[0], m[2] - cy * m[0], m[3] - cz * m[0]
    qxx = m[4] - cx * (m[1] + ex)
    qyy = m[5] - cy * (m[2] + ey)
    qzz = m[6] - cz * (m[3] + ez)
    qxy = m[7] - cx * m[2] - cy * ex
    qxz = m[8] - cx * m[3] - cz * ex
    qyz = m[9] - cy * m[3] - cz * ey
    fx = m[10] - vx * m[0] - (sy * ez - sz * ey)
    fy = m[11] - vy * m[0] - (sz * ex - sx * ez)
    fz = m[12] - vz * m[0] - (sx * ey - sy * ex)
    tx = m[13] - (cy * m[12] - cz * m[11]) - (ey * vz - ez * vy) - (sx * (qyy + qzz) - sy * qxy - sz * qxz)
    ty = m[14] - (cz * m[10] - cx * m[12]) - (ez * vx - ex * vz) - (sy * (qxx + qzz) - sx * qxy - sz * qyz)
    tz = m[15] - (cx * m[11] - cy * m[10]) - (ex * vy - ey * vx) - (sz * (qxx + qyy) - sx * qxz - sy * qyz)
    force, torque = 1.0 / (255.0 * RADIUS**2), 1.0 / (255.0 * RADIUS**3)
    listed = (fx * force, fy * force, fz * force, tx * torque, ty * torque, tz * torque)
    tile = jnp.zeros((CX, LANES), F32)
    for n, value in enumerate(listed):
        tile = jnp.where(rows8 == n, jnp.broadcast_to(value, (CX, LANES)), tile)
    tile = jnp.where(lanes8 < 36, tile, 0.0)
    total = tile
    for g in range(1, 9):
        total = total + pltpu.roll(tile, LANES - 4 * g, 1)
    load_ref[...] = total.T[0:4, 0:6]


def finish(post, halo, corner_of, load, out_hbm, load_hbm, out, out_sem):
    put_load = pltpu.make_async_copy(load, load_hbm, out_sem.at[19])
    put_load.start()
    puts = []
    lanes8 = lax.broadcasted_iota(jnp.int32, (CX, LANES), 1)
    rows8 = lax.broadcasted_iota(jnp.int32, (CX, LANES), 0)
    lower = lanes8 < NZ
    z_of = lax.broadcasted_iota(jnp.int32, (CX, CELLS), 1) & (NZ - 1)
    edge = {1: z_of == 0, -1: z_of == NZ - 1}
    row_of = lax.broadcasted_iota(jnp.int32, (CX, CELLS), 0)
    for pop in range(19):
        step_x, step_y, step_z = (int(v) for v in VELOCITIES[pop])
        value = post[pop]
        shift = lane_shift(pop) % CELLS
        if shift:
            value = pltpu.roll(value, shift, 1)
        if step_x:
            value = pltpu.roll(value, step_x % CX, 0)
            row = 0 if step_x > 0 else CX - 1
            n = (*X_UP, *X_DOWN).index(pop)
            beside_x = jnp.concatenate(
                [jnp.broadcast_to(halo[0, n, c : c + 1, :], (CX, LANES)) for c in range(CHUNKS)], axis=1
            )
            value = jnp.where(row_of == row, beside_x, value)
        if step_y:
            tile = halo[1, (*Y_UP, *Y_DOWN).index(pop)]
            if step_x:
                k = list(CORNERS).index(pop)
                tile = jnp.where(rows8 == row, jnp.broadcast_to(corner_of[k : k + 1, :], (CX, LANES)), tile)
            if step_y > 0:
                value = jnp.concatenate([jnp.where(lower, tile, value[:, :LANES]), value[:, LANES:]], axis=1)
            else:
                value = jnp.concatenate([value[:, :-LANES], jnp.where(lower, value[:, -LANES:], tile)], axis=1)
        if step_z:
            value = jnp.where(edge[step_z], post[OPPOSITE[pop]], value)
        out[pop] = value
        puts.append(pltpu.make_async_copy(out.at[pop], out_hbm.at[pop], out_sem.at[pop]))
        puts[-1].start()
    put_load.wait()
    for put in puts:
        put.wait()


def per_device(populations, cover_codes, sphere_cell, sphere_velocity, sphere_spin, relax_rates):
    vmem, anywhere = pl.BlockSpec(memory_space=pltpu.VMEM), pl.BlockSpec(memory_space=pl.ANY)
    dma = pltpu.SemaphoreType.DMA
    post, halo, corner, load = pl.pallas_call(
        kernel,
        out_shape=(
            pltpu.VMEM((20, CX, CELLS), F32),
            pltpu.VMEM((2, 10, CX, LANES), F32),
            pltpu.VMEM((CX, LANES), F32),
            pltpu.VMEM((4, 6), F32),
        ),
        in_specs=[anywhere] * 7,
        out_specs=(vmem,) * 4,
        scratch_shapes=[
            pltpu.SMEM((3, 1, 1, 4), jnp.int32),
            pltpu.SMEM((3, 1, 1, 4), F32),
            pltpu.SMEM((3, 1, 1, 4), F32),
            pltpu.SMEM((15,), F32),
            pltpu.VMEM((64, 16), F32),
            pltpu.VMEM((19, CX, CELLS), F32),
            pltpu.VMEM((2, CX, CELLS), jnp.int32),
            pltpu.VMEM((64, LANES), F32),
            pltpu.VMEM((CHUNKS, MOMENTS * CX, LANES), F32),
            pltpu.VMEM((ROWS, CX * CELLS), jnp.bfloat16),
            pltpu.VMEM((2 * MOMENTS, CX * CELLS), jnp.bfloat16),
            pltpu.VMEM((8, LANES), F32),
            pltpu.VMEM((15, 72, LANES), F32),
            pltpu.VMEM((15, 72, LANES), F32),
            pltpu.VMEM((16, LANES), F32),
            pltpu.VMEM((MOMENTS, LANES), F32),
            pltpu.VMEM((15, MOMENTS, LANES), F32),
            dma((7,)),
            dma((14,)),
            dma((15,)),
            dma((8,)),
            dma((15,)),
        ],
        compiler_params=pltpu.CompilerParams(
            collective_id=0, has_side_effects=True, vmem_limit_bytes=60 * 1024 * 1024
        ),
    )(
        populations, cover_codes, sphere_cell, sphere_velocity, sphere_spin, relax_rates,
        jnp.asarray(coefficient_rows()),
    )
    out, load = pl.pallas_call(
        finish,
        out_shape=(jax.ShapeDtypeStruct((19, CX, CELLS), F32), jax.ShapeDtypeStruct((4, 6), F32)),
        in_specs=[vmem] * 4,
        out_specs=(anywhere, anywhere),
        scratch_shapes=[pltpu.VMEM((19, CX, CELLS), F32), dma((20,))],
        compiler_params=pltpu.CompilerParams(vmem_limit_bytes=8 * 1024 * 1024),
    )(*[pltpu.with_memory_space_constraint(v, pltpu.VMEM) for v in (post, halo, corner, load)])
    return out, load.T.reshape(6, 1, 1, 4)


def solution(mesh):
    placed = (
        P(None, "bx", "by"),
        P(None, "bx", "by"),
        P(None, "bx", "by", None),
        P(None, "bx", "by", None),
        P(None, "bx", "by", None),
        P(),
    )
    return jax.shard_map(
        per_device,
        mesh=mesh,
        in_specs=placed,
        out_specs=(P(None, "bx", "by"), P(None, "bx", "by", None)),
        check_vma=False,
    )
```

```python
import jax
import jax.numpy as jnp
import numpy as np
from jax import lax
from jax.experimental import pallas as pl
from jax.experimental.pallas import tpu as pltpu
from jax.sharding import PartitionSpec as P

NZ = 64
RADIUS = 8
CX, CY = 8, 16
CELLS = CY * NZ
LANES = 128
CHUNKS = CELLS // LANES
MESH = pl.DeviceIdType.MESH
F32 = jnp.float32

VELOCITIES = np.array(
    [
        [0, 0, 0],
        [1, 0, 0],
        [-1, 0, 0],
        [0, 1, 0],
        [0, -1, 0],
        [0, 0, 1],
        [0, 0, -1],
        [1, 1, 0],
        [-1, -1, 0],
        [1, -1, 0],
        [-1, 1, 0],
        [1, 0, 1],
        [-1, 0, -1],
        [1, 0, -1],
        [-1, 0, 1],
        [0, 1, 1],
        [0, -1, -1],
        [0, 1, -1],
        [0, -1, 1],
    ]
)
OPPOSITE = [0, 2, 1, 4, 3, 6, 5, 8, 7, 10, 9, 12, 11, 14, 13, 16, 15, 18, 17]
X_UP, X_DOWN = (1, 7, 9, 11, 13), (2, 8, 10, 12, 14)
Y_UP, Y_DOWN = (3, 7, 10, 15, 17), (4, 8, 9, 16, 18)
NEAR = [(dx, dy) for dx in range(-2, 3) for dy in range(-1, 2)]
HERE = NEAR.index((0, 0))
SENDS = [0, 2, 12, 14, 3, 5, 9, 11, 1, 13, 4, 10, 6, 8]
BESIDE = [t for t in SENDS if abs(NEAR[t][0]) < 2]
CORNERS = {7: (-1, -1), 8: (1, 1), 9: (-1, 1), 10: (1, -1)}
MOMENTS = 16
ROWS = 48


def moment_rows():
    vel_x, vel_y, vel_z = [VELOCITIES[:, component] * 1.0 for component in range(3)]
    monomials = [
        np.ones(19),
        vel_x,
        vel_y,
        vel_z,
        vel_x * vel_x,
        vel_y * vel_y,
        vel_z * vel_z,
        vel_x * vel_y,
        vel_x * vel_z,
        vel_y * vel_z,
        vel_x * vel_x * vel_y,
        vel_x * vel_x * vel_z,
        vel_y * vel_y * vel_x,
        vel_y * vel_y * vel_z,
        vel_z * vel_z * vel_x,
        vel_z * vel_z * vel_y,
        vel_x * vel_x * vel_y * vel_y,
        vel_x * vel_x * vel_z * vel_z,
        vel_y * vel_y * vel_z * vel_z,
    ]
    orthonormal = []
    for vector in monomials:
        vector = vector.copy()
        for earlier in orthonormal:
            vector = vector - np.dot(earlier, vector) * earlier
        orthonormal.append(vector / np.sqrt(np.dot(vector, vector)))
    return np.stack(orthonormal)


def coefficient_rows():
    rows = moment_rows()[4:]
    even = [1, 3, 5, 7, 11, 15]
    out = []
    for a in even:
        for b in even:
            keep = np.isin(np.arange(15), [0, 1, 2, 12, 13, 14])
            out.append(rows[:, a] * (rows[:, b] - rows[:, 0]) * keep)
    for axis, first, second, rates in ((1, 7, 11, (8, 10)), (3, 7, 15, (6, 11)), (5, 11, 15, (7, 9))):
        for a in (first, second):
            for b in (first, second):
                keep = np.isin(np.arange(15), rates)
                out.append(rows[:, a] * (rows[:, b] - rows[:, axis]) * keep)
    for rate in (3, 4, 5):
        out.append(0.25 * (np.arange(15) == rate))
    table = np.zeros((64, 16), np.float32)
    table[: len(out), :15] = np.stack(out)
    return table


def lane_shift(pop):
    return int(VELOCITIES[pop, 1]) * NZ + int(VELOCITIES[pop, 2])


def sphere_terms(density, codes, table, cell, first_slot):
    flow, square, cover = None, None, None
    for packed in codes:
        slot = ((packed >> 8) + first_slot) & 63
        weight = (packed & 255).astype(F32) * (1.0 / 255.0) * density
        got = [
            jnp.take_along_axis(
                jnp.broadcast_to(table[n : n + 1, :], (CX, LANES)), at,
                axis=1, mode="promise_in_bounds",
            )
            for n, at in ((0, slot), (0, slot + 64), *((n, slot) for n in range(1, 8)))
        ]
        rx, ry, rz = cell[0] - got[0], cell[1] - got[1], cell[2] - got[2]
        wx = got[3] + got[7] * rz - got[8] * ry
        wy = got[4] + got[8] * rx - got[6] * rz
        wz = got[5] + got[6] * ry - got[7] * rx
        bx, by, bz = weight * wx, weight * wy, weight * wz
        one = (bx, by, bz)
        two = (bx * wx, by * wy, bz * wz, bx * wy, bx * wz, by * wz)
        if flow is None:
            flow, square, cover = one, two, weight
        else:
            flow = [a + b for a, b in zip(flow, one)]
            square = [a + b for a, b in zip(square, two)]
            cover = cover + weight
    hx, hy, hz = [value * (1.0 / 12.0) for value in flow]
    qxx, qyy, qzz, qxy, qxz, qyz = square
    base = cover * (1.0 / 18.0) - (qxx + qyy + qzz) * (1.0 / 12.0)
    half = 0.5 * base
    exx, eyy, ezz = 0.125 * qxx, 0.125 * qyy, 0.125 * qzz
    exy, exz, eyz = 0.25 * qxy, 0.25 * qxz, 0.25 * qyz
    b_xy, b_xz, b_yz = half + (exx + eyy), half + (exx + ezz), half + (eyy + ezz)
    return {
        0: (6.0 * base, None),
        1: (base + 2.0 * exx, 2.0 * hx),
        3: (base + 2.0 * eyy, 2.0 * hy),
        5: (base + 2.0 * ezz, 2.0 * hz),
        7: (b_xy + exy, hx + hy),
        9: (b_xy - exy, hx - hy),
        11: (b_xz + exz, hx + hz),
        13: (b_xz - exz, hx - hz),
        15: (b_yz + eyz, hy + hz),
        17: (b_yz - eyz, hy - hz),
    }


def term_of(terms, pop):
    even, odd = terms[pop if pop % 2 else pop - 1]
    return even + odd if pop % 2 else even - odd


def kernel(
    pops_hbm, codes_hbm, cell_hbm, vel_hbm, spin_hbm, rates_hbm, coef_hbm,
    post, halo, corner_out, load_ref,
    cell_ref, vel_ref, spin_ref, rates_ref, coef_in, f, codes, coef, parts, weights, split,
    state, message, arrived, table, loads,
    in_sem, near_send, near_recv,
):
    nx, ny = lax.axis_size("bx"), lax.axis_size("by")
    me_x, me_y = lax.axis_index("bx"), lax.axis_index("by")

    def device(t):
        dx, dy = NEAR[t]
        return (lax.rem(me_x + dx + nx, nx), lax.rem(me_y + dy + ny, ny))

    barrier = pltpu.get_barrier_semaphore()
    for t in SENDS:
        pl.semaphore_signal(barrier, inc=1, device_id=device(t), device_id_type=MESH)
    fetched = []
    for n, (src, dst) in enumerate(
        (
            (cell_hbm, cell_ref), (vel_hbm, vel_ref), (spin_hbm, spin_ref), (rates_hbm, rates_ref),
            (coef_hbm, coef_in), (codes_hbm, codes), (pops_hbm, f),
        )
    ):
        fetched.append(pltpu.make_async_copy(src, dst, in_sem.at[n]))
        fetched[-1].start()

    lane = lax.broadcasted_iota(jnp.int32, (1, LANES), 1)
    sphere = lane & 3

    def along(values):
        return jnp.where(
            sphere < 2,
            jnp.where(sphere == 0, values[0], values[1]),
            jnp.where(sphere == 2, values[2], values[3]),
        )

    for copy in fetched[:5]:
        copy.wait()
    place = [along([cell_ref[n, 0, 0, k].astype(F32) for k in range(4)]) for n in range(3)]
    rows = [jnp.where(lane < NZ, place[0], place[1]), place[2]]
    for source in (vel_ref, spin_ref):
        for n in range(3):
            rows.append(along([source[n, 0, 0, k] for k in range(4)]))
    for n, row in enumerate(rows):
        state[n : n + 1, :] = row
    for t in SENDS:
        message[t, 0:8, :] = state[...]

    which = lax.broadcasted_iota(jnp.int32, (16, LANES), 0)
    rates = jnp.zeros((16, LANES), F32)
    for r in range(15):
        rates = jnp.where(which == r, rates_ref[r], rates)
    coef[...] = jnp.dot(
        coef_in[...], rates, precision=lax.Precision.HIGHEST, preferred_element_type=F32
    )

    lanes8 = lax.broadcasted_iota(jnp.int32, (CX, LANES), 1)
    rows8 = lax.broadcasted_iota(jnp.int32, (CX, LANES), 0)
    cell_x = rows8.astype(F32)
    cell_z = (lanes8 & (NZ - 1)).astype(F32)

    fetched[5].wait()
    slot_rows = lax.broadcasted_iota(jnp.int32, (ROWS, CELLS), 0)

    def fill(row, carry):
        total = None
        for layer in range(2):
            packed = codes[layer, pl.ds(row, 1), :]
            level = (packed & 255).astype(F32)
            hit = jnp.where((packed >> 8) == slot_rows, level, 0.0)
            total = hit if total is None else total + hit
        weights[:, pl.ds(pl.multiple_of(row * CELLS, CELLS), CELLS)] = total.astype(jnp.bfloat16)
        return carry

    lax.fori_loop(0, CX, fill, 0, unroll=8)
    fetched[6].wait()

    def fluid(chunk, carry):
        at = pl.ds(pl.multiple_of(chunk * LANES, LANES), LANES)
        p = [f[i, :, at] for i in range(19)]
        s = {a: p[a] + p[a + 1] for a in range(1, 19, 2)}
        d = {a: p[a] - p[a + 1] for a in range(1, 19, 2)}
        s_xy, a_xy = s[7] + s[9], s[7] - s[9]
        s_xz, a_xz = s[11] + s[13], s[11] - s[13]
        s_yz, a_yz = s[15] + s[17], s[15] - s[17]
        x1, x2 = d[7] + d[9], d[11] + d[13]
        y1, y2 = d[7] - d[9], d[15] + d[17]
        z1, z2 = d[11] - d[13], d[15] - d[17]
        density = (p[0] + s[1]) + (s[3] + s[5]) + (s_xy + s_xz) + s_yz
        jx, jy, jz = d[1] + x1 + x2, d[3] + y1 + y2, d[5] + z1 + z2
        inverse = 1.0 / density
        ux, uy, uz = jx * inverse, jy * inverse, jz * inverse
        code_of = [codes[layer, :, at] for layer in range(2)]
        cover = ((code_of[0] & 255) + (code_of[1] & 255)).astype(F32) * (1.0 / 255.0)

        my = ((lanes8 >> 6) + 2 * chunk).astype(F32)
        mz = cell_z - 32.0
        dx, dy, dz = density * cell_x, density * my, density * mz
        listed = (
            density, dx, dy, dz, dx * cell_x, dy * my, dz * mz, dx * my, dx * mz, dy * mz,
            jx, jy, jz, my * jz - mz * jy, mz * jx - cell_x * jz, cell_x * jy - my * jx,
        )
        for n, value in enumerate(listed):
            parts[chunk, CX * n : CX * (n + 1), :] = value

        keep = 1.0 - cover
        hx, hy, hz = 0.5 * jx * ux, 0.5 * jy * uy, 0.5 * jz * uz
        cxy, cxz, cyz = jx * uy, jx * uz, jy * uz
        base = density * (1.0 / 9.0) - (hx + hy + hz) * (1.0 / 3.0)
        e_x, e_y, e_z = base + hx, base + hy, base + hz
        e_xy, e_xz, e_yz = e_x + hy, e_x + hz, e_y + hz
        even = [s[1] - e_x, s[3] - e_y, s[5] - e_z, s_xy - e_xy, s_xz - e_xz, s_yz - e_yz]
        even = [keep * value for value in even]

        def c(n):
            return jnp.broadcast_to(coef[n : n + 1, :], (CX, LANES))

        sums = []
        for a in range(6):
            total = c(6 * a) * even[0]
            for b in range(1, 6):
                total = total + c(6 * a + b) * even[b]
            sums.append(total)
        third = 1.0 / 3.0
        odd = []
        for axis, (first, second, flow) in enumerate(((x1, x2, jx), (y1, y2, jy), (z1, z2, jz))):
            level = flow * third
            first, second = keep * (first - level), keep * (second - level)
            k = 36 + 4 * axis
            near = c(k) * first + c(k + 1) * second
            far = c(k + 2) * first + c(k + 3) * second
            odd.append((-2.0 * (near + far), near, far))
        n_xy = keep * (a_xy - cxy) * c(48)
        n_xz = keep * (a_xz - cxz) * c(49)
        n_yz = keep * (a_yz - cyz) * c(50)
        half, quarter = 0.5 * cover, 0.25 * cover
        gx, gy, gz = jx * (1.0 / 12.0), jy * (1.0 / 12.0), jz * (1.0 / 12.0)
        pairs = {
            1: (sums[0] + half * e_x, odd[0][0], 2.0 * gx),
            3: (sums[1] + half * e_y, odd[1][0], 2.0 * gy),
            5: (sums[2] + half * e_z, odd[2][0], 2.0 * gz),
            7: (sums[3] + n_xy + quarter * (e_xy + cxy), odd[0][1] + odd[1][1], gx + gy),
            9: (sums[3] - n_xy + quarter * (e_xy - cxy), odd[0][1] - odd[1][1], gx - gy),
            11: (sums[4] + n_xz + quarter * (e_xz + cxz), odd[0][2] + odd[2][1], gx + gz),
            13: (sums[4] - n_xz + quarter * (e_xz - cxz), odd[0][2] - odd[2][1], gx - gz),
            15: (sums[5] + n_yz + quarter * (e_yz + cyz), odd[1][2] + odd[2][2], gy + gz),
            17: (sums[5] - n_yz + quarter * (e_yz - cyz), odd[1][2] - odd[2][2], gy - gz),
        }
        rest = 2.0 * (sums[0] + sums[1] + sums[2]) + 4.0 * (sums[3] + sums[4] + sums[5])
        g = {0: p[0] + rest - 3.0 * cover * base}
        for a, (ev, od, flow) in pairs.items():
            od = od + cover * (d[a] - flow)
            g[a] = p[a] - ev - od
            g[a + 1] = p[a + 1] - ev + od
        for pop in range(19):
            post[pop, :, at] = g[pop]
        post[19, :, at] = density

        common = [density] + [value.astype(F32) for value in code_of]
        for row, names in ((CX - 1, X_UP), (0, X_DOWN)):
            t = NEAR.index((1 if row else -1, 0))
            for n, value in enumerate([g[pop] for pop in names] + common):
                message[t, pl.ds(16 + 8 * n + chunk, 1), :] = value[row : row + 1, :]
        return carry

    lax.fori_loop(0, CHUNKS, fluid, 0, unroll=8)

    codes_f = {c: [codes[layer, :, c * LANES : (c + 1) * LANES].astype(F32) for layer in range(2)] for c in (0, CHUNKS - 1)}
    for dy, names in ((1, Y_UP), (-1, Y_DOWN)):
        c = CHUNKS - 1 if dy > 0 else 0
        t = NEAR.index((0, dy))
        at = slice(c * LANES, (c + 1) * LANES)
        for n, value in enumerate([post[pop, :, at] for pop in (*names, 19)] + codes_f[c]):
            message[t, 16 + 8 * n : 24 + 8 * n, :] = value
    for pop, (sx, sy) in CORNERS.items():
        t = NEAR.index((-sx, -sy))
        row = CX - 1 if sx < 0 else 0
        c = CHUNKS - 1 if sy < 0 else 0
        at = slice(c * LANES, (c + 1) * LANES)
        for n, value in enumerate([post[pop, :, at], post[19, :, at]] + codes_f[c]):
            message[t, 16 + n : 17 + n, :] = value[row : row + 1, :]

    def halves(chunk, carry):
        for row in range(CX):
            value = parts[chunk, pl.ds(row, MOMENTS, stride=CX), :]
            high = value.astype(jnp.bfloat16).astype(F32)
            both = jnp.concatenate([high, value - high], axis=0)
            at = pl.multiple_of(row * CELLS + chunk * LANES, LANES)
            split[:, pl.ds(at, LANES)] = both.astype(jnp.bfloat16)
        return carry

    lax.fori_loop(0, CHUNKS, halves, 0, unroll=8)
    sums = lax.dot_general(
        split[...], weights[...], (((1,), (1,)), ((), ())), preferred_element_type=F32
    )
    sums = sums[0:MOMENTS] + sums[MOMENTS : 2 * MOMENTS]
    loads[...] = jnp.zeros_like(loads)
    loads[:, 0:ROWS] = sums[0:8]
    loads[:, NZ : NZ + ROWS] = sums[8:16]
    for t in BESIDE:
        message[t, 8:16, :] = loads[...]

    def length(t):
        dx, dy = NEAR[t]
        return 8 if abs(dx) == 2 else 24 if dx and dy else 80

    pl.semaphore_wait(barrier, 14)
    near = {}
    for n, t in enumerate(SENDS):
        there = 14 - t
        near[there] = pltpu.make_async_remote_copy(
            src_ref=message.at[t, 0 : length(t)], dst_ref=arrived.at[there, 0 : length(t)],
            send_sem=near_send.at[n], recv_sem=near_recv.at[there],
            device_id=device(t), device_id_type=MESH,
        )
        near[there].start()

    for t in SENDS:
        near[t].wait()
    group = (lanes8 & 63) >> 2
    full = state[...]
    for t in SENDS:
        full = jnp.where(group == t, arrived[t, 0:8, :], full)
    group = group[0:1]
    group_x = (
        (group >= 3).astype(jnp.int32) + (group >= 6).astype(jnp.int32)
        + (group >= 9).astype(jnp.int32) + (group >= 12).astype(jnp.int32)
    )
    moved = jnp.where(lane < NZ, (group_x - 2) * CX, (group - 3 * group_x - 1) * CY)
    table[0:1, :] = full[0:1] + moved.astype(F32)
    table[1:8, :] = full[1:8]

    def covers(chunk, carry):
        at = pl.ds(pl.multiple_of(chunk * LANES, LANES), LANES)
        cell_y = ((lanes8 >> 6) + 2 * chunk).astype(F32)
        terms = sphere_terms(
            post[19, :, at], [codes[layer, :, at] for layer in range(2)], table,
            (cell_x, cell_y, cell_z), 12,
        )
        post[0, :, at] = post[0, :, at] + terms[0][0]
        for pop in range(1, 19):
            post[pop, :, at] = post[pop, :, at] + term_of(terms, pop)
        return carry

    lax.fori_loop(0, CHUNKS, covers, 0, unroll=8)

    lower = lanes8 < NZ
    halo_x = {}
    for side, names in ((0, X_UP), (1, X_DOWN)):
        t = NEAR.index((-1 if side == 0 else 1, 0))
        got = [arrived[t, 16 + 8 * n : 24 + 8 * n, :] for n in range(8)]
        cells = (
            jnp.full((CX, LANES), -1.0 if side == 0 else float(CX), F32),
            (2 * rows8 + (lanes8 >> 6)).astype(F32),
            cell_z,
        )
        terms = sphere_terms(
            got[5], [v.astype(jnp.int32) for v in got[6:8]], table, cells, 12 + (-12 if side == 0 else 12)
        )
        for n, pop in enumerate(names):
            value = got[n] + term_of(terms, pop)
            shift = lane_shift(pop) % LANES
            if shift:
                value = pltpu.roll(value, shift, 1)
            step_y = int(VELOCITIES[pop, 1])
            if step_y:
                crossed = lower if step_y > 0 else jnp.logical_not(lower)
                value = jnp.where(crossed, pltpu.roll(value, step_y % CX, 0), value)
            halo_x[pop] = value
    from_low, from_high = NEAR.index((0, -1)), NEAR.index((0, 1))
    got_low = [arrived[from_low, 16 + 8 * n : 24 + 8 * n, :] for n in range(8)]
    got_high = [arrived[from_high, 16 + 8 * n : 24 + 8 * n, :] for n in range(8)]
    mixed = [jnp.where(lower, got_high[n], got_low[n]) for n in range(5, 8)]
    cells = (cell_x, jnp.where(lower, float(CY), -1.0), cell_z)
    terms = sphere_terms(
        mixed[0], [v.astype(jnp.int32) for v in mixed[1:]], table, cells, jnp.where(lower, 16, 8)
    )
    halo_y = {}
    for names, got in ((Y_UP, got_low), (Y_DOWN, got_high)):
        for n, pop in enumerate(names):
            value = got[n] + term_of(terms, pop)
            value = pltpu.roll(value, lane_shift(pop) % LANES, 1)
            step_x = int(VELOCITIES[pop, 0])
            if step_x:
                value = pltpu.roll(value, step_x % CX, 0)
            halo_y[pop] = value
    corner = [jnp.zeros((CX, LANES), F32) for _ in range(4)]
    corner_x = corner_y = jnp.zeros((CX, LANES), F32)
    corner_slot = jnp.zeros((CX, LANES), jnp.int32)
    for row, (pop, (sx, sy)) in enumerate(CORNERS.items()):
        t = NEAR.index((sx, sy))
        here = rows8 == row
        for n in range(4):
            piece = jnp.broadcast_to(arrived[t, 16 + n : 17 + n, :], (CX, LANES))
            corner[n] = jnp.where(here, piece, corner[n])
        corner_x = jnp.where(here, -1.0 if sx < 0 else float(CX), corner_x)
        corner_y = jnp.where(here, -1.0 if sy < 0 else float(CY), corner_y)
        corner_slot = jnp.where(here, 12 + 12 * sx + 4 * sy, corner_slot)
    terms = sphere_terms(
        corner[1], [v.astype(jnp.int32) for v in corner[2:4]], table, (corner_x, corner_y, cell_z), corner_slot
    )
    corner_term = jnp.zeros((CX, LANES), F32)
    for row, pop in enumerate(CORNERS):
        corner_term = jnp.where(rows8 == row, term_of(terms, pop), corner_term)
    corner_of = pltpu.roll(corner[0] + corner_term, NZ, 1)

    for n, pop in enumerate((*X_UP, *X_DOWN)):
        halo[0, n] = halo_x[pop]
    for n, pop in enumerate((*Y_UP, *Y_DOWN)):
        halo[1, n] = halo_y[pop]
    corner_out[...] = corner_of

    named = (lanes8 & 63) >> 2
    moment = jnp.where(named == 4, loads[...], 0.0)
    for t in BESIDE:
        dx, dy = NEAR[t]
        moment = jnp.where(named == (1 - dx) * 3 + 1 - dy, arrived[t, 8:16, :], moment)
    upper = pltpu.roll(moment, NZ, 1)
    m = [half[n : n + 1, :] for half in (moment, upper) for n in range(8)]
    group = lane >> 2
    group_x = (group >= 3).astype(jnp.int32) + (group >= 6).astype(jnp.int32)
    cx = state[0:1, :] + ((group_x - 1) * CX).astype(F32)
    cy = pltpu.roll(state[0:1, :], NZ, 1) + ((group - 3 * group_x - 1) * CY).astype(F32)
    cz = state[1:2, :] - 32.0
    vx, vy, vz, sx, sy, sz = [state[n : n + 1, :] for n in range(2, 8)]
    ex, ey, ez = m[1] - cx * m[0], m[2] - cy * m[0], m[3] - cz * m[0]
    qxx = m[4] - cx * (m[1] + ex)
    qyy = m[5] - cy * (m[2] + ey)
    qzz = m[6] - cz * (m[3] + ez)
    qxy = m[7] - cx * m[2] - cy * ex
    qxz = m[8] - cx * m[3] - cz * ex
    qyz = m[9] - cy * m[3] - cz * ey
    fx = m[10] - vx * m[0] - (sy * ez - sz * ey)
    fy = m[11] - vy * m[0] - (sz * ex - sx * ez)
    fz = m[12] - vz * m[0] - (sx * ey - sy * ex)
    tx = m[13] - (cy * m[12] - cz * m[11]) - (ey * vz - ez * vy) - (sx * (qyy + qzz) - sy * qxy - sz * qxz)
    ty = m[14] - (cz * m[10] - cx * m[12]) - (ez * vx - ex * vz) - (sy * (qxx + qzz) - sx * qxy - sz * qyz)
    tz = m[15] - (cx * m[11] - cy * m[10]) - (ex * vy - ey * vx) - (sz * (qxx + qyy) - sx * qxz - sy * qyz)
    force, torque = 1.0 / (255.0 * RADIUS**2), 1.0 / (255.0 * RADIUS**3)
    listed = (fx * force, fy * force, fz * force, tx * torque, ty * torque, tz * torque)
    tile = jnp.zeros((CX, LANES), F32)
    for n, value in enumerate(listed):
        tile = jnp.where(rows8 == n, jnp.broadcast_to(value, (CX, LANES)), tile)
    tile = jnp.where(lanes8 < 36, tile, 0.0)
    total = tile
    for g in range(1, 9):
        total = total + pltpu.roll(tile, LANES - 4 * g, 1)
    load_ref[...] = total.T[0:4, 0:6]


def finish(post, halo, corner_of, load, out_hbm, load_hbm, out, out_sem):
    put_load = pltpu.make_async_copy(load, load_hbm, out_sem.at[19])
    put_load.start()
    puts = []
    lanes8 = lax.broadcasted_iota(jnp.int32, (CX, LANES), 1)
    rows8 = lax.broadcasted_iota(jnp.int32, (CX, LANES), 0)
    lower = lanes8 < NZ
    z_of = lax.broadcasted_iota(jnp.int32, (CX, CELLS), 1) & (NZ - 1)
    edge = {1: z_of == 0, -1: z_of == NZ - 1}
    row_of = lax.broadcasted_iota(jnp.int32, (CX, CELLS), 0)
    for pop in range(19):
        step_x, step_y, step_z = (int(v) for v in VELOCITIES[pop])
        value = post[pop]
        shift = lane_shift(pop) % CELLS
        if shift:
            value = pltpu.roll(value, shift, 1)
        if step_x:
            value = pltpu.roll(value, step_x % CX, 0)
            row = 0 if step_x > 0 else CX - 1
            n = (*X_UP, *X_DOWN).index(pop)
            beside_x = jnp.concatenate(
                [jnp.broadcast_to(halo[0, n, c : c + 1, :], (CX, LANES)) for c in range(CHUNKS)], axis=1
            )
            value = jnp.where(row_of == row, beside_x, value)
        if step_y:
            tile = halo[1, (*Y_UP, *Y_DOWN).index(pop)]
            if step_x:
                k = list(CORNERS).index(pop)
                tile = jnp.where(rows8 == row, jnp.broadcast_to(corner_of[k : k + 1, :], (CX, LANES)), tile)
            if step_y > 0:
                value = jnp.concatenate([jnp.where(lower, tile, value[:, :LANES]), value[:, LANES:]], axis=1)
            else:
                value = jnp.concatenate([value[:, :-LANES], jnp.where(lower, value[:, -LANES:], tile)], axis=1)
        if step_z:
            value = jnp.where(edge[step_z], post[OPPOSITE[pop]], value)
        out[pop] = value
        puts.append(pltpu.make_async_copy(out.at[pop], out_hbm.at[pop], out_sem.at[pop]))
        puts[-1].start()
    put_load.wait()
    for put in puts:
        put.wait()


def per_device(populations, cover_codes, sphere_cell, sphere_velocity, sphere_spin, relax_rates):
    vmem, anywhere = pl.BlockSpec(memory_space=pltpu.VMEM), pl.BlockSpec(memory_space=pl.ANY)
    dma = pltpu.SemaphoreType.DMA
    post, halo, corner, load = pl.pallas_call(
        kernel,
        out_shape=(
            pltpu.VMEM((20, CX, CELLS), F32),
            pltpu.VMEM((2, 10, CX, LANES), F32),
            pltpu.VMEM((CX, LANES), F32),
            pltpu.VMEM((4, 6), F32),
        ),
        in_specs=[anywhere] * 7,
        out_specs=(vmem,) * 4,
        scratch_shapes=[
            pltpu.SMEM((3, 1, 1, 4), jnp.int32),
            pltpu.SMEM((3, 1, 1, 4), F32),
            pltpu.SMEM((3, 1, 1, 4), F32),
            pltpu.SMEM((15,), F32),
            pltpu.VMEM((64, 16), F32),
            pltpu.VMEM((19, CX, CELLS), F32),
            pltpu.VMEM((2, CX, CELLS), jnp.int32),
            pltpu.VMEM((64, LANES), F32),
            pltpu.VMEM((CHUNKS, MOMENTS * CX, LANES), F32),
            pltpu.VMEM((ROWS, CX * CELLS), jnp.bfloat16),
            pltpu.VMEM((2 * MOMENTS, CX * CELLS), jnp.bfloat16),
            pltpu.VMEM((8, LANES), F32),
            pltpu.VMEM((15, 80, LANES), F32),
            pltpu.VMEM((15, 80, LANES), F32),
            pltpu.VMEM((8, LANES), F32),
            pltpu.VMEM((8, LANES), F32),
            dma((7,)),
            dma((14,)),
            dma((15,)),
        ],
        compiler_params=pltpu.CompilerParams(
            collective_id=0, has_side_effects=True, vmem_limit_bytes=60 * 1024 * 1024
        ),
    )(
        populations, cover_codes, sphere_cell, sphere_velocity, sphere_spin, relax_rates,
        jnp.asarray(coefficient_rows()),
    )
    out, load = pl.pallas_call(
        finish,
        out_shape=(jax.ShapeDtypeStruct((19, CX, CELLS), F32), jax.ShapeDtypeStruct((4, 6), F32)),
        in_specs=[vmem] * 4,
        out_specs=(anywhere, anywhere),
        scratch_shapes=[pltpu.VMEM((19, CX, CELLS), F32), dma((20,))],
        compiler_params=pltpu.CompilerParams(vmem_limit_bytes=8 * 1024 * 1024),
    )(*[pltpu.with_memory_space_constraint(v, pltpu.VMEM) for v in (post, halo, corner, load)])
    return out, load.T.reshape(6, 1, 1, 4)


def solution(mesh):
    placed = (
        P(None, "bx", "by"),
        P(None, "bx", "by"),
        P(None, "bx", "by", None),
        P(None, "bx", "by", None),
        P(None, "bx", "by", None),
        P(),
    )
    return jax.shard_map(
        per_device,
        mesh=mesh,
        in_specs=placed,
        out_specs=(P(None, "bx", "by"), P(None, "bx", "by", None)),
        check_vma=False,
    )
```

```python
import jax
import jax.numpy as jnp
import numpy as np
from jax import lax
from jax.experimental import pallas as pl
from jax.experimental.pallas import tpu as pltpu
from jax.sharding import PartitionSpec as P

NZ = 64
RADIUS = 8
CX, CY = 8, 16
CELLS = CY * NZ
LANES = 128
CHUNKS = CELLS // LANES
MESH = pl.DeviceIdType.MESH
F32 = jnp.float32

VELOCITIES = np.array(
    [
        [0, 0, 0],
        [1, 0, 0],
        [-1, 0, 0],
        [0, 1, 0],
        [0, -1, 0],
        [0, 0, 1],
        [0, 0, -1],
        [1, 1, 0],
        [-1, -1, 0],
        [1, -1, 0],
        [-1, 1, 0],
        [1, 0, 1],
        [-1, 0, -1],
        [1, 0, -1],
        [-1, 0, 1],
        [0, 1, 1],
        [0, -1, -1],
        [0, 1, -1],
        [0, -1, 1],
    ]
)
OPPOSITE = [0, 2, 1, 4, 3, 6, 5, 8, 7, 10, 9, 12, 11, 14, 13, 16, 15, 18, 17]
X_UP, X_DOWN = (1, 7, 9, 11, 13), (2, 8, 10, 12, 14)
Y_UP, Y_DOWN = (3, 7, 10, 15, 17), (4, 8, 9, 16, 18)
NEAR = [(dx, dy) for dx in range(-2, 3) for dy in range(-1, 2)]
HERE = NEAR.index((0, 0))
SENDS = [0, 2, 12, 14, 3, 5, 9, 11, 1, 13, 4, 10, 6, 8]
BESIDE = [t for t in SENDS if abs(NEAR[t][0]) < 2]
STRAIGHT = 3
CORNERS = {7: (-1, -1), 8: (1, 1), 9: (-1, 1), 10: (1, -1)}
MOMENTS = 16
ROWS = 48


def moment_rows():
    vel_x, vel_y, vel_z = [VELOCITIES[:, component] * 1.0 for component in range(3)]
    monomials = [
        np.ones(19),
        vel_x,
        vel_y,
        vel_z,
        vel_x * vel_x,
        vel_y * vel_y,
        vel_z * vel_z,
        vel_x * vel_y,
        vel_x * vel_z,
        vel_y * vel_z,
        vel_x * vel_x * vel_y,
        vel_x * vel_x * vel_z,
        vel_y * vel_y * vel_x,
        vel_y * vel_y * vel_z,
        vel_z * vel_z * vel_x,
        vel_z * vel_z * vel_y,
        vel_x * vel_x * vel_y * vel_y,
        vel_x * vel_x * vel_z * vel_z,
        vel_y * vel_y * vel_z * vel_z,
    ]
    orthonormal = []
    for vector in monomials:
        vector = vector.copy()
        for earlier in orthonormal:
            vector = vector - np.dot(earlier, vector) * earlier
        orthonormal.append(vector / np.sqrt(np.dot(vector, vector)))
    return np.stack(orthonormal)


def coefficient_rows():
    rows = moment_rows()[4:]
    even = [1, 3, 5, 7, 11, 15]
    out = []
    for a in even:
        for b in even:
            keep = np.isin(np.arange(15), [0, 1, 2, 12, 13, 14])
            out.append(rows[:, a] * (rows[:, b] - rows[:, 0]) * keep)
    for axis, first, second, rates in ((1, 7, 11, (8, 10)), (3, 7, 15, (6, 11)), (5, 11, 15, (7, 9))):
        for a in (first, second):
            for b in (first, second):
                keep = np.isin(np.arange(15), rates)
                out.append(rows[:, a] * (rows[:, b] - rows[:, axis]) * keep)
    for rate in (3, 4, 5):
        out.append(0.25 * (np.arange(15) == rate))
    table = np.zeros((64, 16), np.float32)
    table[: len(out), :15] = np.stack(out)
    return table


def length(t):
    dx, dy = NEAR[t]
    return 0 if t == HERE else 1 if abs(dx) == 2 else 12 if dx and dy else 72 if dx else 40


FIRST = [0] + [sum(-(-length(t) // 8) * 8 for t in range(n + 1)) for n in range(15)]
TOTAL = FIRST[15]
SENT = sum(length(t) for t in range(15))


def rows_of(t, start, stop):
    return slice(FIRST[t] + start, FIRST[t] + stop)


def lane_shift(pop):
    return int(VELOCITIES[pop, 1]) * NZ + int(VELOCITIES[pop, 2])


def sphere_terms(density, codes, table, cell, first_slot):
    flow, square, cover = None, None, None
    for packed in codes:
        slot = ((packed >> 8) + first_slot) & 63
        weight = (packed & 255).astype(F32) * (1.0 / 255.0) * density
        ax, ay, az, sx, sy, sz = [
            jnp.take_along_axis(
                jnp.broadcast_to(table[n : n + 1, :], (CX, LANES)), slot,
                axis=1, mode="promise_in_bounds",
            )
            for n in range(6)
        ]
        wx = ax + (sy * cell[2] - sz * cell[1])
        wy = ay + (sz * cell[0] - sx * cell[2])
        wz = az + (sx * cell[1] - sy * cell[0])
        bx, by, bz = weight * wx, weight * wy, weight * wz
        one = (bx, by, bz)
        two = (bx * wx, by * wy, bz * wz, bx * wy, bx * wz, by * wz)
        if flow is None:
            flow, square, cover = one, two, weight
        else:
            flow = [a + b for a, b in zip(flow, one)]
            square = [a + b for a, b in zip(square, two)]
            cover = cover + weight
    hx, hy, hz = [value * (1.0 / 12.0) for value in flow]
    qxx, qyy, qzz, qxy, qxz, qyz = square
    base = cover * (1.0 / 18.0) - (qxx + qyy + qzz) * (1.0 / 12.0)
    half = 0.5 * base
    exx, eyy, ezz = 0.125 * qxx, 0.125 * qyy, 0.125 * qzz
    exy, exz, eyz = 0.25 * qxy, 0.25 * qxz, 0.25 * qyz
    b_xy, b_xz, b_yz = half + (exx + eyy), half + (exx + ezz), half + (eyy + ezz)
    return {
        0: (6.0 * base, None),
        1: (base + 2.0 * exx, 2.0 * hx),
        3: (base + 2.0 * eyy, 2.0 * hy),
        5: (base + 2.0 * ezz, 2.0 * hz),
        7: (b_xy + exy, hx + hy),
        9: (b_xy - exy, hx - hy),
        11: (b_xz + exz, hx + hz),
        13: (b_xz - exz, hx - hz),
        15: (b_yz + eyz, hy + hz),
        17: (b_yz - eyz, hy - hz),
    }


def term_of(terms, pop):
    even, odd = terms[pop if pop % 2 else pop - 1]
    return even + odd if pop % 2 else even - odd


def kernel(
    pops_hbm, codes_hbm, cell_hbm, vel_hbm, spin_hbm, rates_hbm, coef_hbm,
    post, halo, corner_out, load_ref,
    cell_ref, vel_ref, spin_ref, rates_ref, coef_in, f, codes, coef, parts, weights, split,
    state, message, arrived, table, loads,
    in_sem, near_send, near_recv,
):
    nx, ny = lax.axis_size("bx"), lax.axis_size("by")
    me_x, me_y = lax.axis_index("bx"), lax.axis_index("by")

    def wrapped(at, size):
        return jnp.where(at < 0, at + size, jnp.where(at >= size, at - size, at))

    x_of = {d: wrapped(me_x + d, nx) for d in range(-2, 3)}
    y_of = {d: wrapped(me_y + d, ny) for d in range(-1, 2)}

    def device(t):
        dx, dy = NEAR[t]
        return (x_of[dx], y_of[dy])

    barrier = pltpu.get_barrier_semaphore()
    for t in SENDS:
        pl.semaphore_signal(barrier, inc=1, device_id=device(t), device_id_type=MESH)
    fetched = []
    for n, (src, dst) in enumerate(
        (
            (cell_hbm, cell_ref), (vel_hbm, vel_ref), (spin_hbm, spin_ref), (rates_hbm, rates_ref),
            (coef_hbm, coef_in), (codes_hbm, codes), (pops_hbm, f),
        )
    ):
        fetched.append(pltpu.make_async_copy(src, dst, in_sem.at[n]))
        fetched[-1].start()

    lane = lax.broadcasted_iota(jnp.int32, (1, LANES), 1)
    sphere = lane & 3

    def along(values):
        return jnp.where(
            sphere < 2,
            jnp.where(sphere == 0, values[0], values[1]),
            jnp.where(sphere == 2, values[2], values[3]),
        )

    for copy in fetched[:5]:
        copy.wait()
    place = [along([cell_ref[n, 0, 0, k].astype(F32) for k in range(4)]) for n in range(3)]
    rows = [jnp.where(lane < NZ, place[0], place[1]), place[2]]
    for source in (vel_ref, spin_ref):
        for n in range(3):
            rows.append(along([source[n, 0, 0, k] for k in range(4)]))
    for n, row in enumerate(rows):
        state[n : n + 1, :] = row

    which = lax.broadcasted_iota(jnp.int32, (16, LANES), 0)
    rates = jnp.zeros((16, LANES), F32)
    for r in range(15):
        rates = jnp.where(which == r, rates_ref[r], rates)
    coef[...] = jnp.dot(
        coef_in[...], rates, precision=lax.Precision.HIGHEST, preferred_element_type=F32
    )

    lanes8 = lax.broadcasted_iota(jnp.int32, (CX, LANES), 1)
    rows8 = lax.broadcasted_iota(jnp.int32, (CX, LANES), 0)
    cell_x = rows8.astype(F32)
    cell_z = (lanes8 & (NZ - 1)).astype(F32)

    fetched[5].wait()
    slot_rows = lax.broadcasted_iota(jnp.int32, (ROWS, CELLS), 0)

    def fill(row, carry):
        total = None
        for layer in range(2):
            packed = codes[layer, pl.ds(row, 1), :]
            level = (packed & 255).astype(F32)
            hit = jnp.where((packed >> 8) == slot_rows, level, 0.0)
            total = hit if total is None else total + hit
        weights[:, pl.ds(pl.multiple_of(row * CELLS, CELLS), CELLS)] = total.astype(jnp.bfloat16)
        return carry

    lax.fori_loop(0, CX, fill, 0, unroll=8)
    fetched[6].wait()

    def fluid(chunk, carry):
        at = pl.ds(pl.multiple_of(chunk * LANES, LANES), LANES)
        p = [f[i, :, at] for i in range(19)]
        s = {a: p[a] + p[a + 1] for a in range(1, 19, 2)}
        d = {a: p[a] - p[a + 1] for a in range(1, 19, 2)}
        s_xy, a_xy = s[7] + s[9], s[7] - s[9]
        s_xz, a_xz = s[11] + s[13], s[11] - s[13]
        s_yz, a_yz = s[15] + s[17], s[15] - s[17]
        x1, x2 = d[7] + d[9], d[11] + d[13]
        y1, y2 = d[7] - d[9], d[15] + d[17]
        z1, z2 = d[11] - d[13], d[15] - d[17]
        density = (p[0] + s[1]) + (s[3] + s[5]) + (s_xy + s_xz) + s_yz
        jx, jy, jz = d[1] + x1 + x2, d[3] + y1 + y2, d[5] + z1 + z2
        inverse = 1.0 / density
        ux, uy, uz = jx * inverse, jy * inverse, jz * inverse
        code_of = [codes[layer, :, at] for layer in range(2)]
        cover = ((code_of[0] & 255) + (code_of[1] & 255)).astype(F32) * (1.0 / 255.0)

        my = ((lanes8 >> 6) + 2 * chunk).astype(F32)
        mz = cell_z - 32.0
        dx, dy, dz = density * cell_x, density * my, density * mz
        listed = (
            density, dx, dy, dz, dx * cell_x, dy * my, dz * mz, dx * my, dx * mz, dy * mz,
            jx, jy, jz, my * jz - mz * jy, mz * jx - cell_x * jz, cell_x * jy - my * jx,
        )
        for n, value in enumerate(listed):
            parts[chunk, CX * n : CX * (n + 1), :] = value

        keep = 1.0 - cover
        hx, hy, hz = 0.5 * jx * ux, 0.5 * jy * uy, 0.5 * jz * uz
        cxy, cxz, cyz = jx * uy, jx * uz, jy * uz
        base = density * (1.0 / 9.0) - (hx + hy + hz) * (1.0 / 3.0)
        e_x, e_y, e_z = base + hx, base + hy, base + hz
        e_xy, e_xz, e_yz = e_x + hy, e_x + hz, e_y + hz
        even = [s[1] - e_x, s[3] - e_y, s[5] - e_z, s_xy - e_xy, s_xz - e_xz, s_yz - e_yz]
        even = [keep * value for value in even]

        def c(n):
            return jnp.broadcast_to(coef[n : n + 1, :], (CX, LANES))

        sums = []
        for a in range(6):
            total = c(6 * a) * even[0]
            for b in range(1, 6):
                total = total + c(6 * a + b) * even[b]
            sums.append(total)
        third = 1.0 / 3.0
        odd = []
        for axis, (first, second, flow) in enumerate(((x1, x2, jx), (y1, y2, jy), (z1, z2, jz))):
            level = flow * third
            first, second = keep * (first - level), keep * (second - level)
            k = 36 + 4 * axis
            near = c(k) * first + c(k + 1) * second
            far = c(k + 2) * first + c(k + 3) * second
            odd.append((-2.0 * (near + far), near, far))
        n_xy = keep * (a_xy - cxy) * c(48)
        n_xz = keep * (a_xz - cxz) * c(49)
        n_yz = keep * (a_yz - cyz) * c(50)
        half, quarter = 0.5 * cover, 0.25 * cover
        gx, gy, gz = jx * (1.0 / 12.0), jy * (1.0 / 12.0), jz * (1.0 / 12.0)
        pairs = {
            1: (sums[0] + half * e_x, odd[0][0], 2.0 * gx),
            3: (sums[1] + half * e_y, odd[1][0], 2.0 * gy),
            5: (sums[2] + half * e_z, odd[2][0], 2.0 * gz),
            7: (sums[3] + n_xy + quarter * (e_xy + cxy), odd[0][1] + odd[1][1], gx + gy),
            9: (sums[3] - n_xy + quarter * (e_xy - cxy), odd[0][1] - odd[1][1], gx - gy),
            11: (sums[4] + n_xz + quarter * (e_xz + cxz), odd[0][2] + odd[2][1], gx + gz),
            13: (sums[4] - n_xz + quarter * (e_xz - cxz), odd[0][2] - odd[2][1], gx - gz),
            15: (sums[5] + n_yz + quarter * (e_yz + cyz), odd[1][2] + odd[2][2], gy + gz),
            17: (sums[5] - n_yz + quarter * (e_yz - cyz), odd[1][2] - odd[2][2], gy - gz),
        }
        rest = 2.0 * (sums[0] + sums[1] + sums[2]) + 4.0 * (sums[3] + sums[4] + sums[5])
        g = {0: p[0] + rest - 3.0 * cover * base}
        for a, (ev, od, flow) in pairs.items():
            od = od + cover * (d[a] - flow)
            g[a] = p[a] - ev - od
            g[a + 1] = p[a + 1] - ev + od
        for pop in range(19):
            post[pop, :, at] = g[pop]
        post[19, :, at] = density

        common = [density] + [value.astype(F32) for value in code_of]
        for row, names in ((CX - 1, X_UP), (0, X_DOWN)):
            t = NEAR.index((1 if row else -1, 0))
            for n, value in enumerate([g[pop] for pop in names] + common):
                message[pl.ds(FIRST[t] + 8 + 8 * n + chunk, 1), :] = value[row : row + 1, :]
        return carry

    lax.fori_loop(0, CHUNKS, fluid, 0, unroll=8)

    codes_f = {c: [codes[layer, :, c * LANES : (c + 1) * LANES].astype(F32) for layer in range(2)] for c in (0, CHUNKS - 1)}
    for dy, names in ((1, Y_UP), (-1, Y_DOWN)):
        c = CHUNKS - 1 if dy > 0 else 0
        t = NEAR.index((0, dy))
        at = slice(c * LANES, (c + 1) * LANES)
        straight = [post[19, :, at], *codes_f[c], post[names[STRAIGHT], :, at]]
        turned = [pltpu.roll(post[pop, :, at], NZ, 1) for n, pop in enumerate(names) if n != STRAIGHT]
        for n, (one, two) in enumerate(zip(straight, turned)):
            message[rows_of(t, 8 + 8 * n, 16 + 8 * n), :] = jnp.where(
                lanes8 < NZ, *((two, one) if dy > 0 else (one, two))
            )
    for pop, (sx, sy) in CORNERS.items():
        t = NEAR.index((-sx, -sy))
        row = CX - 1 if sx < 0 else 0
        c = CHUNKS - 1 if sy < 0 else 0
        at = slice(c * LANES, (c + 1) * LANES)
        for n, value in enumerate([post[pop, :, at], post[19, :, at]] + codes_f[c]):
            message[rows_of(t, 8 + n, 9 + n), :] = value[row : row + 1, :]

    def halves(chunk, carry):
        for row in range(CX):
            value = parts[chunk, pl.ds(row, MOMENTS, stride=CX), :]
            high = value.astype(jnp.bfloat16).astype(F32)
            both = jnp.concatenate([high, value - high], axis=0)
            at = pl.multiple_of(row * CELLS + chunk * LANES, LANES)
            split[:, pl.ds(at, LANES)] = both.astype(jnp.bfloat16)
        return carry

    lax.fori_loop(0, CHUNKS, halves, 0, unroll=8)
    sums = lax.dot_general(
        split[...], weights[...], (((1,), (1,)), ((), ())), preferred_element_type=F32
    )
    sums = sums[0:MOMENTS] + sums[MOMENTS : 2 * MOMENTS]
    loads[...] = state[...]
    loads[:, 0:ROWS] = sums[0:8]
    loads[:, NZ : NZ + ROWS] = sums[8:16]
    for t in BESIDE:
        message[rows_of(t, 0, 8), :] = loads[...]
    packed = jnp.zeros((1, LANES), F32)
    for n, row in enumerate((place[0], *rows[1:], place[1])):
        packed = jnp.where(lane >> 2 == n, row, packed)
    for t in SENDS:
        if t not in BESIDE:
            message[rows_of(t, 0, 1), :] = packed

    pl.semaphore_wait(barrier, 14)
    for t in SENDS:
        there = 14 - t
        pltpu.make_async_remote_copy(
            src_ref=message.at[rows_of(t, 0, length(t))],
            dst_ref=arrived.at[rows_of(there, 0, length(t))],
            send_sem=near_send.at[0], recv_sem=near_recv.at[0],
            device_id=device(t), device_id_type=MESH,
        ).start()

    pltpu.make_async_copy(arrived.at[0:SENT], arrived.at[0:SENT], near_recv.at[0]).wait()
    group = (lanes8 & 63) >> 2
    full = state[...]
    where = jnp.where(lanes8 < NZ, ROWS, NZ + ROWS) + (lanes8 & 3)
    afar = 4 * jnp.where(jnp.logical_and(lanes8 >= NZ, rows8 == 0), 8, rows8) + (lanes8 & 3)
    for t in SENDS:
        if t in BESIDE:
            tile, at = arrived[rows_of(t, 0, 8), :], where
        else:
            tile, at = jnp.broadcast_to(arrived[rows_of(t, 0, 1), :], (CX, LANES)), afar
        spread = jnp.take_along_axis(tile, at, axis=1, mode="promise_in_bounds")
        full = jnp.where(group == t, spread, full)
    group = group[0:1]
    group_x = (
        (group >= 3).astype(jnp.int32) + (group >= 6).astype(jnp.int32)
        + (group >= 9).astype(jnp.int32) + (group >= 12).astype(jnp.int32)
    )
    moved = jnp.where(lane < NZ, (group_x - 2) * CX, (group - 3 * group_x - 1) * CY)
    centre_x = full[0:1] + moved.astype(F32)
    centre_y = pltpu.roll(centre_x, NZ, 1)
    centre_z = full[1:2]
    spin_x, spin_y, spin_z = full[5:6], full[6:7], full[7:8]
    table[0:1, :] = full[2:3] - (spin_y * centre_z - spin_z * centre_y)
    table[1:2, :] = full[3:4] - (spin_z * centre_x - spin_x * centre_z)
    table[2:3, :] = full[4:5] - (spin_x * centre_y - spin_y * centre_x)
    table[3:6, :] = full[5:8]

    def covers(chunk, carry):
        at = pl.ds(pl.multiple_of(chunk * LANES, LANES), LANES)
        cell_y = ((lanes8 >> 6) + 2 * chunk).astype(F32)
        terms = sphere_terms(
            post[19, :, at], [codes[layer, :, at] for layer in range(2)], table,
            (cell_x, cell_y, cell_z), 12,
        )
        post[0, :, at] = post[0, :, at] + terms[0][0]
        for pop in range(1, 19):
            post[pop, :, at] = post[pop, :, at] + term_of(terms, pop)
        return carry

    lax.fori_loop(0, CHUNKS, covers, 0, unroll=8)

    lower = lanes8 < NZ
    halo_x = {}
    for side, names in ((0, X_UP), (1, X_DOWN)):
        t = NEAR.index((-1 if side == 0 else 1, 0))
        got = [arrived[rows_of(t, 8 + 8 * n, 16 + 8 * n), :] for n in range(8)]
        cells = (
            jnp.full((CX, LANES), -1.0 if side == 0 else float(CX), F32),
            (2 * rows8 + (lanes8 >> 6)).astype(F32),
            cell_z,
        )
        terms = sphere_terms(
            got[5], [v.astype(jnp.int32) for v in got[6:8]], table, cells, 12 + (-12 if side == 0 else 12)
        )
        for n, pop in enumerate(names):
            value = got[n] + term_of(terms, pop)
            shift = lane_shift(pop) % LANES
            if shift:
                value = pltpu.roll(value, shift, 1)
            step_y = int(VELOCITIES[pop, 1])
            if step_y:
                crossed = lower if step_y > 0 else jnp.logical_not(lower)
                value = jnp.where(crossed, pltpu.roll(value, step_y % CX, 0), value)
            halo_x[pop] = value
    from_low, from_high = NEAR.index((0, -1)), NEAR.index((0, 1))
    got_low = [arrived[rows_of(from_low, 8 + 8 * n, 16 + 8 * n), :] for n in range(4)]
    got_high = [arrived[rows_of(from_high, 8 + 8 * n, 16 + 8 * n), :] for n in range(4)]
    mixed = [jnp.where(lower, got_high[n], got_low[n]) for n in range(3)]
    cells = (cell_x, jnp.where(lower, float(CY), -1.0), cell_z)
    terms = sphere_terms(
        mixed[0], [v.astype(jnp.int32) for v in mixed[1:]], table, cells, jnp.where(lower, 16, 8)
    )
    halo_y = {}
    for names, got in ((Y_UP, got_low), (Y_DOWN, got_high)):
        for n, pop in enumerate(names):
            if n == STRAIGHT:
                value = pltpu.roll(got[3] + term_of(terms, pop), lane_shift(pop) % LANES, 1)
            else:
                value = got[n - (n > STRAIGHT)] + pltpu.roll(term_of(terms, pop), NZ, 1)
                if VELOCITIES[pop, 2]:
                    value = pltpu.roll(value, int(VELOCITIES[pop, 2]) % LANES, 1)
            step_x = int(VELOCITIES[pop, 0])
            if step_x:
                value = pltpu.roll(value, step_x % CX, 0)
            halo_y[pop] = value
    corner = [jnp.zeros((CX, LANES), F32) for _ in range(4)]
    corner_x = corner_y = jnp.zeros((CX, LANES), F32)
    corner_slot = jnp.zeros((CX, LANES), jnp.int32)
    for row, (pop, (sx, sy)) in enumerate(CORNERS.items()):
        t = NEAR.index((sx, sy))
        here = rows8 == row
        for n in range(4):
            piece = jnp.broadcast_to(arrived[rows_of(t, 8 + n, 9 + n), :], (CX, LANES))
            corner[n] = jnp.where(here, piece, corner[n])
        corner_x = jnp.where(here, -1.0 if sx < 0 else float(CX), corner_x)
        corner_y = jnp.where(here, -1.0 if sy < 0 else float(CY), corner_y)
        corner_slot = jnp.where(here, 12 + 12 * sx + 4 * sy, corner_slot)
    terms = sphere_terms(
        corner[1], [v.astype(jnp.int32) for v in corner[2:4]], table, (corner_x, corner_y, cell_z), corner_slot
    )
    corner_term = jnp.zeros((CX, LANES), F32)
    for row, pop in enumerate(CORNERS):
        corner_term = jnp.where(rows8 == row, term_of(terms, pop), corner_term)
    corner_of = pltpu.roll(corner[0] + corner_term, NZ, 1)

    for n, pop in enumerate((*X_UP, *X_DOWN)):
        halo[0, n] = halo_x[pop]
    for n, pop in enumerate((*Y_UP, *Y_DOWN)):
        halo[1, n] = halo_y[pop]
    corner_out[...] = corner_of

    named = (lanes8 & 63) >> 2
    moment = jnp.where(named == 4, loads[...], 0.0)
    for t in BESIDE:
        dx, dy = NEAR[t]
        moment = jnp.where(named == (1 - dx) * 3 + 1 - dy, arrived[rows_of(t, 0, 8), :], moment)
    upper = pltpu.roll(moment, NZ, 1)
    m = [half[n : n + 1, :] for half in (moment, upper) for n in range(8)]
    group = lane >> 2
    group_x = (group >= 3).astype(jnp.int32) + (group >= 6).astype(jnp.int32)
    cx = state[0:1, :] + ((group_x - 1) * CX).astype(F32)
    cy = pltpu.roll(state[0:1, :], NZ, 1) + ((group - 3 * group_x - 1) * CY).astype(F32)
    cz = state[1:2, :] - 32.0
    vx, vy, vz, sx, sy, sz = [state[n : n + 1, :] for n in range(2, 8)]
    ex, ey, ez = m[1] - cx * m[0], m[2] - cy * m[0], m[3] - cz * m[0]
    qxx = m[4] - cx * (m[1] + ex)
    qyy = m[5] - cy * (m[2] + ey)
    qzz = m[6] - cz * (m[3] + ez)
    qxy = m[7] - cx * m[2] - cy * ex
    qxz = m[8] - cx * m[3] - cz * ex
    qyz = m[9] - cy * m[3] - cz * ey
    fx = m[10] - vx * m[0] - (sy * ez - sz * ey)
    fy = m[11] - vy * m[0] - (sz * ex - sx * ez)
    fz = m[12] - vz * m[0] - (sx * ey - sy * ex)
    tx = m[13] - (cy * m[12] - cz * m[11]) - (ey * vz - ez * vy) - (sx * (qyy + qzz) - sy * qxy - sz * qxz)
    ty = m[14] - (cz * m[10] - cx * m[12]) - (ez * vx - ex * vz) - (sy * (qxx + qzz) - sx * qxy - sz * qyz)
    tz = m[15] - (cx * m[11] - cy * m[10]) - (ex * vy - ey * vx) - (sz * (qxx + qyy) - sx * qxz - sy * qyz)
    force, torque = 1.0 / (255.0 * RADIUS**2), 1.0 / (255.0 * RADIUS**3)
    listed = (fx * force, fy * force, fz * force, tx * torque, ty * torque, tz * torque)
    tile = jnp.zeros((CX, LANES), F32)
    for n, value in enumerate(listed):
        tile = jnp.where(rows8 == n, jnp.broadcast_to(value, (CX, LANES)), tile)
    tile = jnp.where(lanes8 < 36, tile, 0.0)
    total = tile
    for g in range(1, 9):
        total = total + pltpu.roll(tile, LANES - 4 * g, 1)
    load_ref[...] = total.T[0:4, 0:6]
    pltpu.make_async_copy(message.at[0:SENT], message.at[0:SENT], near_send.at[0]).wait()


def finish(post, halo, corner_of, load, out_hbm, load_hbm, out, out_sem):
    put_load = pltpu.make_async_copy(load, load_hbm, out_sem.at[19])
    put_load.start()
    puts = []
    lanes8 = lax.broadcasted_iota(jnp.int32, (CX, LANES), 1)
    rows8 = lax.broadcasted_iota(jnp.int32, (CX, LANES), 0)
    lower = lanes8 < NZ
    z_of = lax.broadcasted_iota(jnp.int32, (CX, CELLS), 1) & (NZ - 1)
    edge = {1: z_of == 0, -1: z_of == NZ - 1}
    row_of = lax.broadcasted_iota(jnp.int32, (CX, CELLS), 0)
    for pop in range(19):
        step_x, step_y, step_z = (int(v) for v in VELOCITIES[pop])
        value = post[pop]
        shift = lane_shift(pop) % CELLS
        if shift:
            value = pltpu.roll(value, shift, 1)
        if step_x:
            value = pltpu.roll(value, step_x % CX, 0)
            row = 0 if step_x > 0 else CX - 1
            n = (*X_UP, *X_DOWN).index(pop)
            beside_x = jnp.concatenate(
                [jnp.broadcast_to(halo[0, n, c : c + 1, :], (CX, LANES)) for c in range(CHUNKS)], axis=1
            )
            value = jnp.where(row_of == row, beside_x, value)
        if step_y:
            tile = halo[1, (*Y_UP, *Y_DOWN).index(pop)]
            if step_x:
                k = list(CORNERS).index(pop)
                tile = jnp.where(rows8 == row, jnp.broadcast_to(corner_of[k : k + 1, :], (CX, LANES)), tile)
            if step_y > 0:
                value = jnp.concatenate([jnp.where(lower, tile, value[:, :LANES]), value[:, LANES:]], axis=1)
            else:
                value = jnp.concatenate([value[:, :-LANES], jnp.where(lower, value[:, -LANES:], tile)], axis=1)
        if step_z:
            value = jnp.where(edge[step_z], post[OPPOSITE[pop]], value)
        out[pop] = value
        puts.append(pltpu.make_async_copy(out.at[pop], out_hbm.at[pop], out_sem.at[pop]))
        puts[-1].start()
    put_load.wait()
    for put in puts:
        put.wait()


def per_device(populations, cover_codes, sphere_cell, sphere_velocity, sphere_spin, relax_rates):
    vmem, anywhere = pl.BlockSpec(memory_space=pltpu.VMEM), pl.BlockSpec(memory_space=pl.ANY)
    dma = pltpu.SemaphoreType.DMA
    post, halo, corner, load = pl.pallas_call(
        kernel,
        out_shape=(
            pltpu.VMEM((20, CX, CELLS), F32),
            pltpu.VMEM((2, 10, CX, LANES), F32),
            pltpu.VMEM((CX, LANES), F32),
            pltpu.VMEM((4, 6), F32),
        ),
        in_specs=[anywhere] * 7,
        out_specs=(vmem,) * 4,
        scratch_shapes=[
            pltpu.SMEM((3, 1, 1, 4), jnp.int32),
            pltpu.SMEM((3, 1, 1, 4), F32),
            pltpu.SMEM((3, 1, 1, 4), F32),
            pltpu.SMEM((15,), F32),
            pltpu.VMEM((64, 16), F32),
            pltpu.VMEM((19, CX, CELLS), F32),
            pltpu.VMEM((2, CX, CELLS), jnp.int32),
            pltpu.VMEM((64, LANES), F32),
            pltpu.VMEM((CHUNKS, MOMENTS * CX, LANES), F32),
            pltpu.VMEM((ROWS, CX * CELLS), jnp.bfloat16),
            pltpu.VMEM((2 * MOMENTS, CX * CELLS), jnp.bfloat16),
            pltpu.VMEM((8, LANES), F32),
            pltpu.VMEM((TOTAL, LANES), F32),
            pltpu.VMEM((TOTAL, LANES), F32),
            pltpu.VMEM((8, LANES), F32),
            pltpu.VMEM((8, LANES), F32),
            dma((7,)),
            dma((1,)),
            dma((1,)),
        ],
        compiler_params=pltpu.CompilerParams(
            collective_id=0, has_side_effects=True, vmem_limit_bytes=60 * 1024 * 1024
        ),
    )(
        populations, cover_codes, sphere_cell, sphere_velocity, sphere_spin, relax_rates,
        jnp.asarray(coefficient_rows()),
    )
    out, load = pl.pallas_call(
        finish,
        out_shape=(jax.ShapeDtypeStruct((19, CX, CELLS), F32), jax.ShapeDtypeStruct((4, 6), F32)),
        in_specs=[vmem] * 4,
        out_specs=(anywhere, anywhere),
        scratch_shapes=[pltpu.VMEM((19, CX, CELLS), F32), dma((20,))],
        compiler_params=pltpu.CompilerParams(vmem_limit_bytes=8 * 1024 * 1024),
    )(*[pltpu.with_memory_space_constraint(v, pltpu.VMEM) for v in (post, halo, corner, load)])
    return out, load.T.reshape(6, 1, 1, 4)


def solution(mesh):
    placed = (
        P(None, "bx", "by"),
        P(None, "bx", "by"),
        P(None, "bx", "by", None),
        P(None, "bx", "by", None),
        P(None, "bx", "by", None),
        P(),
    )
    return jax.shard_map(
        per_device,
        mesh=mesh,
        in_specs=placed,
        out_specs=(P(None, "bx", "by"), P(None, "bx", "by", None)),
        check_vma=False,
    )
```

```python
import jax
import jax.numpy as jnp
import numpy as np
from jax import lax
from jax.experimental import pallas as pl
from jax.experimental.pallas import tpu as pltpu
from jax.sharding import PartitionSpec as P

NZ = 64
RADIUS = 8
CX, CY = 8, 16
CELLS = CY * NZ
LANES = 128
CHUNKS = CELLS // LANES
MESH = pl.DeviceIdType.MESH
F32 = jnp.float32

VELOCITIES = np.array(
    [
        [0, 0, 0],
        [1, 0, 0],
        [-1, 0, 0],
        [0, 1, 0],
        [0, -1, 0],
        [0, 0, 1],
        [0, 0, -1],
        [1, 1, 0],
        [-1, -1, 0],
        [1, -1, 0],
        [-1, 1, 0],
        [1, 0, 1],
        [-1, 0, -1],
        [1, 0, -1],
        [-1, 0, 1],
        [0, 1, 1],
        [0, -1, -1],
        [0, 1, -1],
        [0, -1, 1],
    ]
)
OPPOSITE = [0, 2, 1, 4, 3, 6, 5, 8, 7, 10, 9, 12, 11, 14, 13, 16, 15, 18, 17]
X_UP, X_DOWN = (1, 7, 9, 11, 13), (2, 8, 10, 12, 14)
Y_UP, Y_DOWN = (3, 7, 10, 15, 17), (4, 8, 9, 16, 18)
NEAR = [(dx, dy) for dx in range(-2, 3) for dy in range(-1, 2)]
HERE = NEAR.index((0, 0))
SENDS = [2, 14, 5, 11, 8, 0, 12, 3, 9, 6, 1, 13, 4, 10]
BESIDE = [t for t in SENDS if abs(NEAR[t][0]) < 2]
STRAIGHT = 3
CORNERS = {7: (-1, -1), 8: (1, 1), 9: (-1, 1), 10: (1, -1)}
MOMENTS = 16
ROWS = 48


def moment_rows():
    vel_x, vel_y, vel_z = [VELOCITIES[:, component] * 1.0 for component in range(3)]
    monomials = [
        np.ones(19),
        vel_x,
        vel_y,
        vel_z,
        vel_x * vel_x,
        vel_y * vel_y,
        vel_z * vel_z,
        vel_x * vel_y,
        vel_x * vel_z,
        vel_y * vel_z,
        vel_x * vel_x * vel_y,
        vel_x * vel_x * vel_z,
        vel_y * vel_y * vel_x,
        vel_y * vel_y * vel_z,
        vel_z * vel_z * vel_x,
        vel_z * vel_z * vel_y,
        vel_x * vel_x * vel_y * vel_y,
        vel_x * vel_x * vel_z * vel_z,
        vel_y * vel_y * vel_z * vel_z,
    ]
    orthonormal = []
    for vector in monomials:
        vector = vector.copy()
        for earlier in orthonormal:
            vector = vector - np.dot(earlier, vector) * earlier
        orthonormal.append(vector / np.sqrt(np.dot(vector, vector)))
    return np.stack(orthonormal)


def coefficient_rows():
    rows = moment_rows()[4:]
    even = [1, 3, 5, 7, 11, 15]
    out = []
    for a in even:
        for b in even:
            keep = np.isin(np.arange(15), [0, 1, 2, 12, 13, 14])
            out.append(rows[:, a] * (rows[:, b] - rows[:, 0]) * keep)
    for axis, first, second, rates in ((1, 7, 11, (8, 10)), (3, 7, 15, (6, 11)), (5, 11, 15, (7, 9))):
        for a in (first, second):
            for b in (first, second):
                keep = np.isin(np.arange(15), rates)
                out.append(rows[:, a] * (rows[:, b] - rows[:, axis]) * keep)
    for rate in (3, 4, 5):
        out.append(0.25 * (np.arange(15) == rate))
    table = np.zeros((64, 16), np.float32)
    table[: len(out), :15] = np.stack(out)
    return table


def length(t):
    dx, dy = NEAR[t]
    return 0 if t == HERE else 1 if abs(dx) == 2 else 12 if dx and dy else 72 if dx else 40


FIRST = [0] + [sum(-(-length(t) // 8) * 8 for t in range(n + 1)) for n in range(15)]
TOTAL = FIRST[15]
SENT = sum(length(t) for t in range(15))


def rows_of(t, start, stop):
    return slice(FIRST[t] + start, FIRST[t] + stop)


def lane_shift(pop):
    return int(VELOCITIES[pop, 1]) * NZ + int(VELOCITIES[pop, 2])


def sphere_terms(density, codes, table, cell, first_slot):
    flow, square, cover = None, None, None
    for packed in codes:
        slot = ((packed >> 8) + first_slot) & 63
        weight = (packed & 255).astype(F32) * (1.0 / 255.0) * density
        ax, ay, az, sx, sy, sz = [
            jnp.take_along_axis(
                jnp.broadcast_to(table[n : n + 1, :], (CX, LANES)), slot,
                axis=1, mode="promise_in_bounds",
            )
            for n in range(6)
        ]
        wx = ax + (sy * cell[2] - sz * cell[1])
        wy = ay + (sz * cell[0] - sx * cell[2])
        wz = az + (sx * cell[1] - sy * cell[0])
        bx, by, bz = weight * wx, weight * wy, weight * wz
        one = (bx, by, bz)
        two = (bx * wx, by * wy, bz * wz, bx * wy, bx * wz, by * wz)
        if flow is None:
            flow, square, cover = one, two, weight
        else:
            flow = [a + b for a, b in zip(flow, one)]
            square = [a + b for a, b in zip(square, two)]
            cover = cover + weight
    hx, hy, hz = [value * (1.0 / 12.0) for value in flow]
    qxx, qyy, qzz, qxy, qxz, qyz = square
    base = cover * (1.0 / 18.0) - (qxx + qyy + qzz) * (1.0 / 12.0)
    half = 0.5 * base
    exx, eyy, ezz = 0.125 * qxx, 0.125 * qyy, 0.125 * qzz
    exy, exz, eyz = 0.25 * qxy, 0.25 * qxz, 0.25 * qyz
    b_xy, b_xz, b_yz = half + (exx + eyy), half + (exx + ezz), half + (eyy + ezz)
    return {
        0: (6.0 * base, None),
        1: (base + 2.0 * exx, 2.0 * hx),
        3: (base + 2.0 * eyy, 2.0 * hy),
        5: (base + 2.0 * ezz, 2.0 * hz),
        7: (b_xy + exy, hx + hy),
        9: (b_xy - exy, hx - hy),
        11: (b_xz + exz, hx + hz),
        13: (b_xz - exz, hx - hz),
        15: (b_yz + eyz, hy + hz),
        17: (b_yz - eyz, hy - hz),
    }


def term_of(terms, pop):
    even, odd = terms[pop if pop % 2 else pop - 1]
    return even + odd if pop % 2 else even - odd


def kernel(
    pops_hbm, codes_hbm, cell_hbm, vel_hbm, spin_hbm, rates_hbm, coef_hbm,
    post, halo, corner_out, load_ref,
    cell_ref, vel_ref, spin_ref, rates_ref, coef_in, f, codes, coef, parts, weights, split,
    state, message, arrived, table, loads,
    in_sem, near_send, near_recv,
):
    nx, ny = lax.axis_size("bx"), lax.axis_size("by")
    me_x, me_y = lax.axis_index("bx"), lax.axis_index("by")

    def wrapped(at, size):
        return jnp.where(at < 0, at + size, jnp.where(at >= size, at - size, at))

    x_of = {d: wrapped(me_x + d, nx) for d in range(-2, 3)}
    y_of = {d: wrapped(me_y + d, ny) for d in range(-1, 2)}

    def device(t):
        dx, dy = NEAR[t]
        return (x_of[dx], y_of[dy])

    barrier = pltpu.get_barrier_semaphore()
    for t in SENDS:
        pl.semaphore_signal(barrier, inc=1, device_id=device(t), device_id_type=MESH)
    fetched = []
    for n, (src, dst) in enumerate(
        (
            (cell_hbm, cell_ref), (vel_hbm, vel_ref), (spin_hbm, spin_ref), (rates_hbm, rates_ref),
            (coef_hbm, coef_in), (codes_hbm, codes), (pops_hbm, f),
        )
    ):
        fetched.append(pltpu.make_async_copy(src, dst, in_sem.at[n]))
        fetched[-1].start()

    lane = lax.broadcasted_iota(jnp.int32, (1, LANES), 1)
    sphere = lane & 3

    def along(values):
        return jnp.where(
            sphere < 2,
            jnp.where(sphere == 0, values[0], values[1]),
            jnp.where(sphere == 2, values[2], values[3]),
        )

    for copy in fetched[:5]:
        copy.wait()
    place = [along([cell_ref[n, 0, 0, k].astype(F32) for k in range(4)]) for n in range(3)]
    rows = [jnp.where(lane < NZ, place[0], place[1]), place[2]]
    for source in (vel_ref, spin_ref):
        for n in range(3):
            rows.append(along([source[n, 0, 0, k] for k in range(4)]))
    for n, row in enumerate(rows):
        state[n : n + 1, :] = row

    which = lax.broadcasted_iota(jnp.int32, (16, LANES), 0)
    rates = jnp.zeros((16, LANES), F32)
    for r in range(15):
        rates = jnp.where(which == r, rates_ref[r], rates)
    coef[...] = jnp.dot(
        coef_in[...], rates, precision=lax.Precision.HIGHEST, preferred_element_type=F32
    )

    lanes8 = lax.broadcasted_iota(jnp.int32, (CX, LANES), 1)
    rows8 = lax.broadcasted_iota(jnp.int32, (CX, LANES), 0)
    cell_x = rows8.astype(F32)
    cell_z = (lanes8 & (NZ - 1)).astype(F32)

    fetched[5].wait()
    slot_rows = lax.broadcasted_iota(jnp.int32, (ROWS, CELLS), 0)

    def fill(row, carry):
        total = None
        for layer in range(2):
            packed = codes[layer, pl.ds(row, 1), :]
            level = (packed & 255).astype(F32)
            hit = jnp.where((packed >> 8) == slot_rows, level, 0.0)
            total = hit if total is None else total + hit
        weights[:, pl.ds(pl.multiple_of(row * CELLS, CELLS), CELLS)] = total.astype(jnp.bfloat16)
        return carry

    lax.fori_loop(0, CX, fill, 0, unroll=8)
    fetched[6].wait()

    def fluid(chunk, carry):
        at = pl.ds(pl.multiple_of(chunk * LANES, LANES), LANES)
        p = [f[i, :, at] for i in range(19)]
        s = {a: p[a] + p[a + 1] for a in range(1, 19, 2)}
        d = {a: p[a] - p[a + 1] for a in range(1, 19, 2)}
        s_xy, a_xy = s[7] + s[9], s[7] - s[9]
        s_xz, a_xz = s[11] + s[13], s[11] - s[13]
        s_yz, a_yz = s[15] + s[17], s[15] - s[17]
        x1, x2 = d[7] + d[9], d[11] + d[13]
        y1, y2 = d[7] - d[9], d[15] + d[17]
        z1, z2 = d[11] - d[13], d[15] - d[17]
        density = (p[0] + s[1]) + (s[3] + s[5]) + (s_xy + s_xz) + s_yz
        jx, jy, jz = d[1] + x1 + x2, d[3] + y1 + y2, d[5] + z1 + z2
        inverse = 1.0 / density
        ux, uy, uz = jx * inverse, jy * inverse, jz * inverse
        code_of = [codes[layer, :, at] for layer in range(2)]
        cover = ((code_of[0] & 255) + (code_of[1] & 255)).astype(F32) * (1.0 / 255.0)

        my = ((lanes8 >> 6) + 2 * chunk).astype(F32)
        mz = cell_z - 32.0
        dx, dy, dz = density * cell_x, density * my, density * mz
        listed = (
            density, dx, dy, dz, dx * cell_x, dy * my, dz * mz, dx * my, dx * mz, dy * mz,
            jx, jy, jz, my * jz - mz * jy, mz * jx - cell_x * jz, cell_x * jy - my * jx,
        )
        for n, value in enumerate(listed):
            parts[chunk, CX * n : CX * (n + 1), :] = value

        keep = 1.0 - cover
        hx, hy, hz = 0.5 * jx * ux, 0.5 * jy * uy, 0.5 * jz * uz
        cxy, cxz, cyz = jx * uy, jx * uz, jy * uz
        base = density * (1.0 / 9.0) - (hx + hy + hz) * (1.0 / 3.0)
        e_x, e_y, e_z = base + hx, base + hy, base + hz
        e_xy, e_xz, e_yz = e_x + hy, e_x + hz, e_y + hz
        even = [s[1] - e_x, s[3] - e_y, s[5] - e_z, s_xy - e_xy, s_xz - e_xz, s_yz - e_yz]
        even = [keep * value for value in even]

        def c(n):
            return jnp.broadcast_to(coef[n : n + 1, :], (CX, LANES))

        sums = []
        for a in range(6):
            total = c(6 * a) * even[0]
            for b in range(1, 6):
                total = total + c(6 * a + b) * even[b]
            sums.append(total)
        third = 1.0 / 3.0
        odd = []
        for axis, (first, second, flow) in enumerate(((x1, x2, jx), (y1, y2, jy), (z1, z2, jz))):
            level = flow * third
            first, second = keep * (first - level), keep * (second - level)
            k = 36 + 4 * axis
            near = c(k) * first + c(k + 1) * second
            far = c(k + 2) * first + c(k + 3) * second
            odd.append((-2.0 * (near + far), near, far))
        n_xy = keep * (a_xy - cxy) * c(48)
        n_xz = keep * (a_xz - cxz) * c(49)
        n_yz = keep * (a_yz - cyz) * c(50)
        half, quarter = 0.5 * cover, 0.25 * cover
        gx, gy, gz = jx * (1.0 / 12.0), jy * (1.0 / 12.0), jz * (1.0 / 12.0)
        pairs = {
            1: (sums[0] + half * e_x, odd[0][0], 2.0 * gx),
            3: (sums[1] + half * e_y, odd[1][0], 2.0 * gy),
            5: (sums[2] + half * e_z, odd[2][0], 2.0 * gz),
            7: (sums[3] + n_xy + quarter * (e_xy + cxy), odd[0][1] + odd[1][1], gx + gy),
            9: (sums[3] - n_xy + quarter * (e_xy - cxy), odd[0][1] - odd[1][1], gx - gy),
            11: (sums[4] + n_xz + quarter * (e_xz + cxz), odd[0][2] + odd[2][1], gx + gz),
            13: (sums[4] - n_xz + quarter * (e_xz - cxz), odd[0][2] - odd[2][1], gx - gz),
            15: (sums[5] + n_yz + quarter * (e_yz + cyz), odd[1][2] + odd[2][2], gy + gz),
            17: (sums[5] - n_yz + quarter * (e_yz - cyz), odd[1][2] - odd[2][2], gy - gz),
        }
        rest = 2.0 * (sums[0] + sums[1] + sums[2]) + 4.0 * (sums[3] + sums[4] + sums[5])
        g = {0: p[0] + rest - 3.0 * cover * base}
        for a, (ev, od, flow) in pairs.items():
            od = od + cover * (d[a] - flow)
            g[a] = p[a] - ev - od
            g[a + 1] = p[a + 1] - ev + od
        for pop in range(19):
            post[pop, :, at] = g[pop]
        post[19, :, at] = density

        common = [density] + [value.astype(F32) for value in code_of]
        for row, names in ((CX - 1, X_UP), (0, X_DOWN)):
            t = NEAR.index((1 if row else -1, 0))
            for n, value in enumerate([g[pop] for pop in names] + common):
                message[pl.ds(FIRST[t] + 8 + 8 * n + chunk, 1), :] = value[row : row + 1, :]
        return carry

    lax.fori_loop(0, CHUNKS, fluid, 0, unroll=8)

    codes_f = {c: [codes[layer, :, c * LANES : (c + 1) * LANES].astype(F32) for layer in range(2)] for c in (0, CHUNKS - 1)}
    for dy, names in ((1, Y_UP), (-1, Y_DOWN)):
        c = CHUNKS - 1 if dy > 0 else 0
        t = NEAR.index((0, dy))
        at = slice(c * LANES, (c + 1) * LANES)
        straight = [post[19, :, at], *codes_f[c], post[names[STRAIGHT], :, at]]
        turned = [pltpu.roll(post[pop, :, at], NZ, 1) for n, pop in enumerate(names) if n != STRAIGHT]
        for n, (one, two) in enumerate(zip(straight, turned)):
            message[rows_of(t, 8 + 8 * n, 16 + 8 * n), :] = jnp.where(
                lanes8 < NZ, *((two, one) if dy > 0 else (one, two))
            )
    for pop, (sx, sy) in CORNERS.items():
        t = NEAR.index((-sx, -sy))
        row = CX - 1 if sx < 0 else 0
        c = CHUNKS - 1 if sy < 0 else 0
        at = slice(c * LANES, (c + 1) * LANES)
        for n, value in enumerate([post[pop, :, at], post[19, :, at]] + codes_f[c]):
            message[rows_of(t, 8 + n, 9 + n), :] = value[row : row + 1, :]

    def halves(chunk, carry):
        for row in range(CX):
            value = parts[chunk, pl.ds(row, MOMENTS, stride=CX), :]
            high = value.astype(jnp.bfloat16).astype(F32)
            both = jnp.concatenate([high, value - high], axis=0)
            at = pl.multiple_of(row * CELLS + chunk * LANES, LANES)
            split[:, pl.ds(at, LANES)] = both.astype(jnp.bfloat16)
        return carry

    lax.fori_loop(0, CHUNKS, halves, 0, unroll=8)
    sums = lax.dot_general(
        split[...], weights[...], (((1,), (1,)), ((), ())), preferred_element_type=F32
    )
    sums = sums[0:MOMENTS] + sums[MOMENTS : 2 * MOMENTS]
    loads[...] = state[...]
    loads[:, 0:ROWS] = sums[0:8]
    loads[:, NZ : NZ + ROWS] = sums[8:16]
    for t in BESIDE:
        message[rows_of(t, 0, 8), :] = loads[...]
    packed = jnp.zeros((1, LANES), F32)
    for n, row in enumerate((place[0], *rows[1:], place[1])):
        packed = jnp.where(lane >> 2 == n, row, packed)
    for t in SENDS:
        if t not in BESIDE:
            message[rows_of(t, 0, 1), :] = packed

    pl.semaphore_wait(barrier, 14)
    for t in SENDS:
        there = 14 - t
        pltpu.make_async_remote_copy(
            src_ref=message.at[rows_of(t, 0, length(t))],
            dst_ref=arrived.at[rows_of(there, 0, length(t))],
            send_sem=near_send.at[0], recv_sem=near_recv.at[0],
            device_id=device(t), device_id_type=MESH,
        ).start()

    pltpu.make_async_copy(arrived.at[0:SENT], arrived.at[0:SENT], near_recv.at[0]).wait()
    group = (lanes8 & 63) >> 2
    full = state[...]
    where = jnp.where(lanes8 < NZ, ROWS, NZ + ROWS) + (lanes8 & 3)
    afar = 4 * jnp.where(jnp.logical_and(lanes8 >= NZ, rows8 == 0), 8, rows8) + (lanes8 & 3)
    for t in SENDS:
        if t in BESIDE:
            tile, at = arrived[rows_of(t, 0, 8), :], where
        else:
            tile, at = jnp.broadcast_to(arrived[rows_of(t, 0, 1), :], (CX, LANES)), afar
        spread = jnp.take_along_axis(tile, at, axis=1, mode="promise_in_bounds")
        full = jnp.where(group == t, spread, full)
    group = group[0:1]
    group_x = (
        (group >= 3).astype(jnp.int32) + (group >= 6).astype(jnp.int32)
        + (group >= 9).astype(jnp.int32) + (group >= 12).astype(jnp.int32)
    )
    moved = jnp.where(lane < NZ, (group_x - 2) * CX, (group - 3 * group_x - 1) * CY)
    centre_x = full[0:1] + moved.astype(F32)
    centre_y = pltpu.roll(centre_x, NZ, 1)
    centre_z = full[1:2]
    spin_x, spin_y, spin_z = full[5:6], full[6:7], full[7:8]
    table[0:1, :] = full[2:3] - (spin_y * centre_z - spin_z * centre_y)
    table[1:2, :] = full[3:4] - (spin_z * centre_x - spin_x * centre_z)
    table[2:3, :] = full[4:5] - (spin_x * centre_y - spin_y * centre_x)
    table[3:6, :] = full[5:8]

    named = (lanes8 & 63) >> 2
    moment = jnp.where(named == 4, loads[...], 0.0)
    for t in BESIDE:
        dx, dy = NEAR[t]
        moment = jnp.where(named == (1 - dx) * 3 + 1 - dy, arrived[rows_of(t, 0, 8), :], moment)
    upper = pltpu.roll(moment, NZ, 1)
    m = [half[n : n + 1, :] for half in (moment, upper) for n in range(8)]
    group = lane >> 2
    group_x = (group >= 3).astype(jnp.int32) + (group >= 6).astype(jnp.int32)
    cx = state[0:1, :] + ((group_x - 1) * CX).astype(F32)
    cy = pltpu.roll(state[0:1, :], NZ, 1) + ((group - 3 * group_x - 1) * CY).astype(F32)
    cz = state[1:2, :] - 32.0
    vx, vy, vz, sx, sy, sz = [state[n : n + 1, :] for n in range(2, 8)]
    ex, ey, ez = m[1] - cx * m[0], m[2] - cy * m[0], m[3] - cz * m[0]
    qxx = m[4] - cx * (m[1] + ex)
    qyy = m[5] - cy * (m[2] + ey)
    qzz = m[6] - cz * (m[3] + ez)
    qxy = m[7] - cx * m[2] - cy * ex
    qxz = m[8] - cx * m[3] - cz * ex
    qyz = m[9] - cy * m[3] - cz * ey
    fx = m[10] - vx * m[0] - (sy * ez - sz * ey)
    fy = m[11] - vy * m[0] - (sz * ex - sx * ez)
    fz = m[12] - vz * m[0] - (sx * ey - sy * ex)
    tx = m[13] - (cy * m[12] - cz * m[11]) - (ey * vz - ez * vy) - (sx * (qyy + qzz) - sy * qxy - sz * qxz)
    ty = m[14] - (cz * m[10] - cx * m[12]) - (ez * vx - ex * vz) - (sy * (qxx + qzz) - sx * qxy - sz * qyz)
    tz = m[15] - (cx * m[11] - cy * m[10]) - (ex * vy - ey * vx) - (sz * (qxx + qyy) - sx * qxz - sy * qyz)
    force, torque = 1.0 / (255.0 * RADIUS**2), 1.0 / (255.0 * RADIUS**3)
    listed = (fx * force, fy * force, fz * force, tx * torque, ty * torque, tz * torque)
    tile = jnp.zeros((CX, LANES), F32)
    for n, value in enumerate(listed):
        tile = jnp.where(rows8 == n, jnp.broadcast_to(value, (CX, LANES)), tile)
    tile = jnp.where(lanes8 < 36, tile, 0.0)
    total = tile
    for g in range(1, 9):
        total = total + pltpu.roll(tile, LANES - 4 * g, 1)
    load_ref[...] = total.T[0:4, 0:6]
    lower = lanes8 < NZ
    halo_x = {}
    for side, names in ((0, X_UP), (1, X_DOWN)):
        t = NEAR.index((-1 if side == 0 else 1, 0))
        got = [arrived[rows_of(t, 8 + 8 * n, 16 + 8 * n), :] for n in range(8)]
        cells = (
            jnp.full((CX, LANES), -1.0 if side == 0 else float(CX), F32),
            (2 * rows8 + (lanes8 >> 6)).astype(F32),
            cell_z,
        )
        terms = sphere_terms(
            got[5], [v.astype(jnp.int32) for v in got[6:8]], table, cells, 12 + (-12 if side == 0 else 12)
        )
        for n, pop in enumerate(names):
            value = got[n] + term_of(terms, pop)
            shift = lane_shift(pop) % LANES
            if shift:
                value = pltpu.roll(value, shift, 1)
            step_y = int(VELOCITIES[pop, 1])
            if step_y:
                crossed = lower if step_y > 0 else jnp.logical_not(lower)
                value = jnp.where(crossed, pltpu.roll(value, step_y % CX, 0), value)
            halo_x[pop] = value
    from_low, from_high = NEAR.index((0, -1)), NEAR.index((0, 1))
    got_low = [arrived[rows_of(from_low, 8 + 8 * n, 16 + 8 * n), :] for n in range(4)]
    got_high = [arrived[rows_of(from_high, 8 + 8 * n, 16 + 8 * n), :] for n in range(4)]
    mixed = [jnp.where(lower, got_high[n], got_low[n]) for n in range(3)]
    cells = (cell_x, jnp.where(lower, float(CY), -1.0), cell_z)
    terms = sphere_terms(
        mixed[0], [v.astype(jnp.int32) for v in mixed[1:]], table, cells, jnp.where(lower, 16, 8)
    )
    halo_y = {}
    for names, got in ((Y_UP, got_low), (Y_DOWN, got_high)):
        for n, pop in enumerate(names):
            if n == STRAIGHT:
                value = pltpu.roll(got[3] + term_of(terms, pop), lane_shift(pop) % LANES, 1)
            else:
                value = got[n - (n > STRAIGHT)] + pltpu.roll(term_of(terms, pop), NZ, 1)
                if VELOCITIES[pop, 2]:
                    value = pltpu.roll(value, int(VELOCITIES[pop, 2]) % LANES, 1)
            step_x = int(VELOCITIES[pop, 0])
            if step_x:
                value = pltpu.roll(value, step_x % CX, 0)
            halo_y[pop] = value
    corner = [jnp.zeros((CX, LANES), F32) for _ in range(4)]
    corner_x = corner_y = jnp.zeros((CX, LANES), F32)
    corner_slot = jnp.zeros((CX, LANES), jnp.int32)
    for row, (pop, (sx, sy)) in enumerate(CORNERS.items()):
        t = NEAR.index((sx, sy))
        here = rows8 == row
        for n in range(4):
            piece = jnp.broadcast_to(arrived[rows_of(t, 8 + n, 9 + n), :], (CX, LANES))
            corner[n] = jnp.where(here, piece, corner[n])
        corner_x = jnp.where(here, -1.0 if sx < 0 else float(CX), corner_x)
        corner_y = jnp.where(here, -1.0 if sy < 0 else float(CY), corner_y)
        corner_slot = jnp.where(here, 12 + 12 * sx + 4 * sy, corner_slot)
    terms = sphere_terms(
        corner[1], [v.astype(jnp.int32) for v in corner[2:4]], table, (corner_x, corner_y, cell_z), corner_slot
    )
    corner_term = jnp.zeros((CX, LANES), F32)
    for row, pop in enumerate(CORNERS):
        corner_term = jnp.where(rows8 == row, term_of(terms, pop), corner_term)
    corner_of = pltpu.roll(corner[0] + corner_term, NZ, 1)

    for n, pop in enumerate((*X_UP, *X_DOWN)):
        halo[0, n] = halo_x[pop]
    for n, pop in enumerate((*Y_UP, *Y_DOWN)):
        halo[1, n] = halo_y[pop]
    corner_out[...] = corner_of

    def covers(chunk, carry):
        at = pl.ds(pl.multiple_of(chunk * LANES, LANES), LANES)
        cell_y = ((lanes8 >> 6) + 2 * chunk).astype(F32)
        terms = sphere_terms(
            post[19, :, at], [codes[layer, :, at] for layer in range(2)], table,
            (cell_x, cell_y, cell_z), 12,
        )
        post[0, :, at] = post[0, :, at] + terms[0][0]
        for pop in range(1, 19):
            post[pop, :, at] = post[pop, :, at] + term_of(terms, pop)
        return carry

    lax.fori_loop(0, CHUNKS, covers, 0, unroll=8)

    pltpu.make_async_copy(message.at[0:SENT], message.at[0:SENT], near_send.at[0]).wait()


def finish(post, halo, corner_of, load, out_hbm, load_hbm, out, out_sem):
    put_load = pltpu.make_async_copy(load, load_hbm, out_sem.at[19])
    put_load.start()
    puts = []
    lanes8 = lax.broadcasted_iota(jnp.int32, (CX, LANES), 1)
    rows8 = lax.broadcasted_iota(jnp.int32, (CX, LANES), 0)
    lower = lanes8 < NZ
    z_of = lax.broadcasted_iota(jnp.int32, (CX, CELLS), 1) & (NZ - 1)
    edge = {1: z_of == 0, -1: z_of == NZ - 1}
    row_of = lax.broadcasted_iota(jnp.int32, (CX, CELLS), 0)
    for pop in range(19):
        step_x, step_y, step_z = (int(v) for v in VELOCITIES[pop])
        value = post[pop]
        shift = lane_shift(pop) % CELLS
        if shift:
            value = pltpu.roll(value, shift, 1)
        if step_x:
            value = pltpu.roll(value, step_x % CX, 0)
            row = 0 if step_x > 0 else CX - 1
            n = (*X_UP, *X_DOWN).index(pop)
            beside_x = jnp.concatenate(
                [jnp.broadcast_to(halo[0, n, c : c + 1, :], (CX, LANES)) for c in range(CHUNKS)], axis=1
            )
            value = jnp.where(row_of == row, beside_x, value)
        if step_y:
            tile = halo[1, (*Y_UP, *Y_DOWN).index(pop)]
            if step_x:
                k = list(CORNERS).index(pop)
                tile = jnp.where(rows8 == row, jnp.broadcast_to(corner_of[k : k + 1, :], (CX, LANES)), tile)
            if step_y > 0:
                value = jnp.concatenate([jnp.where(lower, tile, value[:, :LANES]), value[:, LANES:]], axis=1)
            else:
                value = jnp.concatenate([value[:, :-LANES], jnp.where(lower, value[:, -LANES:], tile)], axis=1)
        if step_z:
            value = jnp.where(edge[step_z], post[OPPOSITE[pop]], value)
        out[pop] = value
        puts.append(pltpu.make_async_copy(out.at[pop], out_hbm.at[pop], out_sem.at[pop]))
        puts[-1].start()
    put_load.wait()
    for put in puts:
        put.wait()


def per_device(populations, cover_codes, sphere_cell, sphere_velocity, sphere_spin, relax_rates):
    vmem, anywhere = pl.BlockSpec(memory_space=pltpu.VMEM), pl.BlockSpec(memory_space=pl.ANY)
    dma = pltpu.SemaphoreType.DMA
    post, halo, corner, load = pl.pallas_call(
        kernel,
        out_shape=(
            pltpu.VMEM((20, CX, CELLS), F32),
            pltpu.VMEM((2, 10, CX, LANES), F32),
            pltpu.VMEM((CX, LANES), F32),
            pltpu.VMEM((4, 6), F32),
        ),
        in_specs=[anywhere] * 7,
        out_specs=(vmem,) * 4,
        scratch_shapes=[
            pltpu.SMEM((3, 1, 1, 4), jnp.int32),
            pltpu.SMEM((3, 1, 1, 4), F32),
            pltpu.SMEM((3, 1, 1, 4), F32),
            pltpu.SMEM((15,), F32),
            pltpu.VMEM((64, 16), F32),
            pltpu.VMEM((19, CX, CELLS), F32),
            pltpu.VMEM((2, CX, CELLS), jnp.int32),
            pltpu.VMEM((64, LANES), F32),
            pltpu.VMEM((CHUNKS, MOMENTS * CX, LANES), F32),
            pltpu.VMEM((ROWS, CX * CELLS), jnp.bfloat16),
            pltpu.VMEM((2 * MOMENTS, CX * CELLS), jnp.bfloat16),
            pltpu.VMEM((8, LANES), F32),
            pltpu.VMEM((TOTAL, LANES), F32),
            pltpu.VMEM((TOTAL, LANES), F32),
            pltpu.VMEM((8, LANES), F32),
            pltpu.VMEM((8, LANES), F32),
            dma((7,)),
            dma((1,)),
            dma((1,)),
        ],
        compiler_params=pltpu.CompilerParams(
            collective_id=0, has_side_effects=True, vmem_limit_bytes=60 * 1024 * 1024
        ),
    )(
        populations, cover_codes, sphere_cell, sphere_velocity, sphere_spin, relax_rates,
        jnp.asarray(coefficient_rows()),
    )
    out, load = pl.pallas_call(
        finish,
        out_shape=(jax.ShapeDtypeStruct((19, CX, CELLS), F32), jax.ShapeDtypeStruct((4, 6), F32)),
        in_specs=[vmem] * 4,
        out_specs=(anywhere, anywhere),
        scratch_shapes=[pltpu.VMEM((19, CX, CELLS), F32), dma((20,))],
        compiler_params=pltpu.CompilerParams(vmem_limit_bytes=8 * 1024 * 1024),
    )(*[pltpu.with_memory_space_constraint(v, pltpu.VMEM) for v in (post, halo, corner, load)])
    return out, load.T.reshape(6, 1, 1, 4)


def solution(mesh):
    placed = (
        P(None, "bx", "by"),
        P(None, "bx", "by"),
        P(None, "bx", "by", None),
        P(None, "bx", "by", None),
        P(None, "bx", "by", None),
        P(),
    )
    return jax.shard_map(
        per_device,
        mesh=mesh,
        in_specs=placed,
        out_specs=(P(None, "bx", "by"), P(None, "bx", "by", None)),
        check_vma=False,
    )
```

```python
import jax
import jax.numpy as jnp
import numpy as np
from jax import lax
from jax.experimental import pallas as pl
from jax.experimental.pallas import tpu as pltpu
from jax.sharding import PartitionSpec as P

NZ = 64
RADIUS = 8
CX, CY = 8, 16
CELLS = CY * NZ
LANES = 128
CHUNKS = CELLS // LANES
MESH = pl.DeviceIdType.MESH
F32 = jnp.float32

VELOCITIES = np.array(
    [
        [0, 0, 0],
        [1, 0, 0],
        [-1, 0, 0],
        [0, 1, 0],
        [0, -1, 0],
        [0, 0, 1],
        [0, 0, -1],
        [1, 1, 0],
        [-1, -1, 0],
        [1, -1, 0],
        [-1, 1, 0],
        [1, 0, 1],
        [-1, 0, -1],
        [1, 0, -1],
        [-1, 0, 1],
        [0, 1, 1],
        [0, -1, -1],
        [0, 1, -1],
        [0, -1, 1],
    ]
)
OPPOSITE = [0, 2, 1, 4, 3, 6, 5, 8, 7, 10, 9, 12, 11, 14, 13, 16, 15, 18, 17]
X_UP, X_DOWN = (1, 7, 9, 11, 13), (2, 8, 10, 12, 14)
Y_UP, Y_DOWN = (3, 7, 10, 15, 17), (4, 8, 9, 16, 18)
NEAR = [(dx, dy) for dx in range(-2, 3) for dy in range(-1, 2)]
HERE = NEAR.index((0, 0))
SENDS = [0, 2, 12, 14, 3, 5, 9, 11, 1, 13, 4, 10, 6, 8]
BESIDE = [t for t in SENDS if abs(NEAR[t][0]) < 2]
STRAIGHT = 3
CORNERS = {7: (-1, -1), 8: (1, 1), 9: (-1, 1), 10: (1, -1)}
MOMENTS = 16
ROWS = 48


def moment_rows():
    vel_x, vel_y, vel_z = [VELOCITIES[:, component] * 1.0 for component in range(3)]
    monomials = [
        np.ones(19),
        vel_x,
        vel_y,
        vel_z,
        vel_x * vel_x,
        vel_y * vel_y,
        vel_z * vel_z,
        vel_x * vel_y,
        vel_x * vel_z,
        vel_y * vel_z,
        vel_x * vel_x * vel_y,
        vel_x * vel_x * vel_z,
        vel_y * vel_y * vel_x,
        vel_y * vel_y * vel_z,
        vel_z * vel_z * vel_x,
        vel_z * vel_z * vel_y,
        vel_x * vel_x * vel_y * vel_y,
        vel_x * vel_x * vel_z * vel_z,
        vel_y * vel_y * vel_z * vel_z,
    ]
    orthonormal = []
    for vector in monomials:
        vector = vector.copy()
        for earlier in orthonormal:
            vector = vector - np.dot(earlier, vector) * earlier
        orthonormal.append(vector / np.sqrt(np.dot(vector, vector)))
    return np.stack(orthonormal)


def coefficient_rows():
    rows = moment_rows()[4:]
    even = [1, 3, 5, 7, 11, 15]
    out = []
    for a in even:
        for b in even:
            keep = np.isin(np.arange(15), [0, 1, 2, 12, 13, 14])
            out.append(rows[:, a] * (rows[:, b] - rows[:, 0]) * keep)
    for axis, first, second, rates in ((1, 7, 11, (8, 10)), (3, 7, 15, (6, 11)), (5, 11, 15, (7, 9))):
        for a in (first, second):
            for b in (first, second):
                keep = np.isin(np.arange(15), rates)
                out.append(rows[:, a] * (rows[:, b] - rows[:, axis]) * keep)
    for rate in (3, 4, 5):
        out.append(0.25 * (np.arange(15) == rate))
    table = np.zeros((64, 16), np.float32)
    table[: len(out), :15] = np.stack(out)
    return table


def length(t):
    dx, dy = NEAR[t]
    return 0 if t == HERE else 1 if abs(dx) == 2 else 12 if dx and dy else 72 if dx else 40


FIRST = [0] + [sum(-(-length(t) // 8) * 8 for t in range(n + 1)) for n in range(15)]
TOTAL = FIRST[15]
SENT = sum(length(t) for t in range(15))


def rows_of(t, start, stop):
    return slice(FIRST[t] + start, FIRST[t] + stop)


def lane_shift(pop):
    return int(VELOCITIES[pop, 1]) * NZ + int(VELOCITIES[pop, 2])


def sphere_terms(density, codes, table, cell, first_slot):
    flow, square, cover = None, None, None
    for packed in codes:
        slot = ((packed >> 8) + first_slot) & 63
        weight = (packed & 255).astype(F32) * (1.0 / 255.0) * density
        ax, ay, az, sx, sy, sz = [
            jnp.take_along_axis(
                jnp.broadcast_to(table[n : n + 1, :], (CX, LANES)), slot,
                axis=1, mode="promise_in_bounds",
            )
            for n in range(6)
        ]
        wx = ax + (sy * cell[2] - sz * cell[1])
        wy = ay + (sz * cell[0] - sx * cell[2])
        wz = az + (sx * cell[1] - sy * cell[0])
        bx, by, bz = weight * wx, weight * wy, weight * wz
        one = (bx, by, bz)
        two = (bx * wx, by * wy, bz * wz, bx * wy, bx * wz, by * wz)
        if flow is None:
            flow, square, cover = one, two, weight
        else:
            flow = [a + b for a, b in zip(flow, one)]
            square = [a + b for a, b in zip(square, two)]
            cover = cover + weight
    hx, hy, hz = [value * (1.0 / 12.0) for value in flow]
    qxx, qyy, qzz, qxy, qxz, qyz = square
    base = cover * (1.0 / 18.0) - (qxx + qyy + qzz) * (1.0 / 12.0)
    half = 0.5 * base
    exx, eyy, ezz = 0.125 * qxx, 0.125 * qyy, 0.125 * qzz
    exy, exz, eyz = 0.25 * qxy, 0.25 * qxz, 0.25 * qyz
    b_xy, b_xz, b_yz = half + (exx + eyy), half + (exx + ezz), half + (eyy + ezz)
    return {
        0: (6.0 * base, None),
        1: (base + 2.0 * exx, 2.0 * hx),
        3: (base + 2.0 * eyy, 2.0 * hy),
        5: (base + 2.0 * ezz, 2.0 * hz),
        7: (b_xy + exy, hx + hy),
        9: (b_xy - exy, hx - hy),
        11: (b_xz + exz, hx + hz),
        13: (b_xz - exz, hx - hz),
        15: (b_yz + eyz, hy + hz),
        17: (b_yz - eyz, hy - hz),
    }


def term_of(terms, pop):
    even, odd = terms[pop if pop % 2 else pop - 1]
    return even + odd if pop % 2 else even - odd


def kernel(
    pops_hbm, codes_hbm, cell_hbm, vel_hbm, spin_hbm, rates_hbm, coef_hbm,
    post, halo, corner_out, load_ref,
    cell_ref, vel_ref, spin_ref, rates_ref, coef_in, f, codes, coef, parts, weights, split,
    state, message, arrived, table, loads,
    in_sem, near_send, near_recv,
):
    nx, ny = lax.axis_size("bx"), lax.axis_size("by")
    me_x, me_y = lax.axis_index("bx"), lax.axis_index("by")

    def wrapped(at, size):
        return jnp.where(at < 0, at + size, jnp.where(at >= size, at - size, at))

    x_of = {d: wrapped(me_x + d, nx) for d in range(-2, 3)}
    y_of = {d: wrapped(me_y + d, ny) for d in range(-1, 2)}

    def device(t):
        dx, dy = NEAR[t]
        return (x_of[dx], y_of[dy])

    barrier = pltpu.get_barrier_semaphore()
    for t in SENDS:
        pl.semaphore_signal(barrier, inc=1, device_id=device(t), device_id_type=MESH)
    fetched = []
    for n, (src, dst) in enumerate(
        (
            (cell_hbm, cell_ref), (vel_hbm, vel_ref), (spin_hbm, spin_ref), (rates_hbm, rates_ref),
            (coef_hbm, coef_in), (codes_hbm, codes), (pops_hbm, f),
        )
    ):
        fetched.append(pltpu.make_async_copy(src, dst, in_sem.at[n]))
        fetched[-1].start()

    lane = lax.broadcasted_iota(jnp.int32, (1, LANES), 1)
    sphere = lane & 3

    def along(values):
        return jnp.where(
            sphere < 2,
            jnp.where(sphere == 0, values[0], values[1]),
            jnp.where(sphere == 2, values[2], values[3]),
        )

    for copy in fetched[:5]:
        copy.wait()
    place = [along([cell_ref[n, 0, 0, k].astype(F32) for k in range(4)]) for n in range(3)]
    rows = [jnp.where(lane < NZ, place[0], place[1]), place[2]]
    for source in (vel_ref, spin_ref):
        for n in range(3):
            rows.append(along([source[n, 0, 0, k] for k in range(4)]))
    for n, row in enumerate(rows):
        state[n : n + 1, :] = row

    which = lax.broadcasted_iota(jnp.int32, (16, LANES), 0)
    rates = jnp.zeros((16, LANES), F32)
    for r in range(15):
        rates = jnp.where(which == r, rates_ref[r], rates)
    coef[...] = jnp.dot(
        coef_in[...], rates, precision=lax.Precision.HIGHEST, preferred_element_type=F32
    )

    lanes8 = lax.broadcasted_iota(jnp.int32, (CX, LANES), 1)
    rows8 = lax.broadcasted_iota(jnp.int32, (CX, LANES), 0)
    cell_x = rows8.astype(F32)
    cell_z = (lanes8 & (NZ - 1)).astype(F32)

    fetched[5].wait()
    slot_rows = lax.broadcasted_iota(jnp.int32, (ROWS, CELLS), 0)

    def fill(row, carry):
        total = None
        for layer in range(2):
            packed = codes[layer, pl.ds(row, 1), :]
            level = (packed & 255).astype(F32)
            hit = jnp.where((packed >> 8) == slot_rows, level, 0.0)
            total = hit if total is None else total + hit
        weights[:, pl.ds(pl.multiple_of(row * CELLS, CELLS), CELLS)] = total.astype(jnp.bfloat16)
        return carry

    lax.fori_loop(0, CX, fill, 0, unroll=8)
    fetched[6].wait()

    def fluid(chunk, carry):
        at = pl.ds(pl.multiple_of(chunk * LANES, LANES), LANES)
        p = [f[i, :, at] for i in range(19)]
        s = {a: p[a] + p[a + 1] for a in range(1, 19, 2)}
        d = {a: p[a] - p[a + 1] for a in range(1, 19, 2)}
        s_xy, a_xy = s[7] + s[9], s[7] - s[9]
        s_xz, a_xz = s[11] + s[13], s[11] - s[13]
        s_yz, a_yz = s[15] + s[17], s[15] - s[17]
        x1, x2 = d[7] + d[9], d[11] + d[13]
        y1, y2 = d[7] - d[9], d[15] + d[17]
        z1, z2 = d[11] - d[13], d[15] - d[17]
        density = (p[0] + s[1]) + (s[3] + s[5]) + (s_xy + s_xz) + s_yz
        jx, jy, jz = d[1] + x1 + x2, d[3] + y1 + y2, d[5] + z1 + z2
        inverse = 1.0 / density
        ux, uy, uz = jx * inverse, jy * inverse, jz * inverse
        code_of = [codes[layer, :, at] for layer in range(2)]
        cover = ((code_of[0] & 255) + (code_of[1] & 255)).astype(F32) * (1.0 / 255.0)

        my = ((lanes8 >> 6) + 2 * chunk).astype(F32)
        mz = cell_z - 32.0
        dx, dy, dz = density * cell_x, density * my, density * mz
        listed = (
            density, dx, dy, dz, dx * cell_x, dy * my, dz * mz, dx * my, dx * mz, dy * mz,
            jx, jy, jz, my * jz - mz * jy, mz * jx - cell_x * jz, cell_x * jy - my * jx,
        )
        for n, value in enumerate(listed):
            parts[chunk, CX * n : CX * (n + 1), :] = value

        keep = 1.0 - cover
        hx, hy, hz = 0.5 * jx * ux, 0.5 * jy * uy, 0.5 * jz * uz
        cxy, cxz, cyz = jx * uy, jx * uz, jy * uz
        base = density * (1.0 / 9.0) - (hx + hy + hz) * (1.0 / 3.0)
        e_x, e_y, e_z = base + hx, base + hy, base + hz
        e_xy, e_xz, e_yz = e_x + hy, e_x + hz, e_y + hz
        even = [s[1] - e_x, s[3] - e_y, s[5] - e_z, s_xy - e_xy, s_xz - e_xz, s_yz - e_yz]
        even = [keep * value for value in even]

        def c(n):
            return jnp.broadcast_to(coef[n : n + 1, :], (CX, LANES))

        sums = []
        for a in range(6):
            total = c(6 * a) * even[0]
            for b in range(1, 6):
                total = total + c(6 * a + b) * even[b]
            sums.append(total)
        third = 1.0 / 3.0
        odd = []
        for axis, (first, second, flow) in enumerate(((x1, x2, jx), (y1, y2, jy), (z1, z2, jz))):
            level = flow * third
            first, second = keep * (first - level), keep * (second - level)
            k = 36 + 4 * axis
            near = c(k) * first + c(k + 1) * second
            far = c(k + 2) * first + c(k + 3) * second
            odd.append((-2.0 * (near + far), near, far))
        n_xy = keep * (a_xy - cxy) * c(48)
        n_xz = keep * (a_xz - cxz) * c(49)
        n_yz = keep * (a_yz - cyz) * c(50)
        half, quarter = 0.5 * cover, 0.25 * cover
        gx, gy, gz = jx * (1.0 / 12.0), jy * (1.0 / 12.0), jz * (1.0 / 12.0)
        pairs = {
            1: (sums[0] + half * e_x, odd[0][0], 2.0 * gx),
            3: (sums[1] + half * e_y, odd[1][0], 2.0 * gy),
            5: (sums[2] + half * e_z, odd[2][0], 2.0 * gz),
            7: (sums[3] + n_xy + quarter * (e_xy + cxy), odd[0][1] + odd[1][1], gx + gy),
            9: (sums[3] - n_xy + quarter * (e_xy - cxy), odd[0][1] - odd[1][1], gx - gy),
            11: (sums[4] + n_xz + quarter * (e_xz + cxz), odd[0][2] + odd[2][1], gx + gz),
            13: (sums[4] - n_xz + quarter * (e_xz - cxz), odd[0][2] - odd[2][1], gx - gz),
            15: (sums[5] + n_yz + quarter * (e_yz + cyz), odd[1][2] + odd[2][2], gy + gz),
            17: (sums[5] - n_yz + quarter * (e_yz - cyz), odd[1][2] - odd[2][2], gy - gz),
        }
        rest = 2.0 * (sums[0] + sums[1] + sums[2]) + 4.0 * (sums[3] + sums[4] + sums[5])
        g = {0: p[0] + rest - 3.0 * cover * base}
        for a, (ev, od, flow) in pairs.items():
            od = od + cover * (d[a] - flow)
            g[a] = p[a] - ev - od
            g[a + 1] = p[a + 1] - ev + od
        for pop in range(19):
            post[pop, :, at] = g[pop]
        post[19, :, at] = density

        common = [density] + [value.astype(F32) for value in code_of]
        for row, names in ((CX - 1, X_UP), (0, X_DOWN)):
            t = NEAR.index((1 if row else -1, 0))
            for n, value in enumerate([g[pop] for pop in names] + common):
                message[pl.ds(FIRST[t] + 8 + 8 * n + chunk, 1), :] = value[row : row + 1, :]
        return carry

    lax.fori_loop(0, CHUNKS, fluid, 0, unroll=8)

    codes_f = {c: [codes[layer, :, c * LANES : (c + 1) * LANES].astype(F32) for layer in range(2)] for c in (0, CHUNKS - 1)}
    for dy, names in ((1, Y_UP), (-1, Y_DOWN)):
        c = CHUNKS - 1 if dy > 0 else 0
        t = NEAR.index((0, dy))
        at = slice(c * LANES, (c + 1) * LANES)
        straight = [post[19, :, at], *codes_f[c], post[names[STRAIGHT], :, at]]
        turned = [pltpu.roll(post[pop, :, at], NZ, 1) for n, pop in enumerate(names) if n != STRAIGHT]
        for n, (one, two) in enumerate(zip(straight, turned)):
            message[rows_of(t, 8 + 8 * n, 16 + 8 * n), :] = jnp.where(
                lanes8 < NZ, *((two, one) if dy > 0 else (one, two))
            )
    for pop, (sx, sy) in CORNERS.items():
        t = NEAR.index((-sx, -sy))
        row = CX - 1 if sx < 0 else 0
        c = CHUNKS - 1 if sy < 0 else 0
        at = slice(c * LANES, (c + 1) * LANES)
        for n, value in enumerate([post[pop, :, at], post[19, :, at]] + codes_f[c]):
            message[rows_of(t, 8 + n, 9 + n), :] = value[row : row + 1, :]

    def halves(chunk, carry):
        for row in range(CX):
            value = parts[chunk, pl.ds(row, MOMENTS, stride=CX), :]
            high = value.astype(jnp.bfloat16).astype(F32)
            both = jnp.concatenate([high, value - high], axis=0)
            at = pl.multiple_of(row * CELLS + chunk * LANES, LANES)
            split[:, pl.ds(at, LANES)] = both.astype(jnp.bfloat16)
        return carry

    lax.fori_loop(0, CHUNKS, halves, 0, unroll=8)
    sums = lax.dot_general(
        split[...], weights[...], (((1,), (1,)), ((), ())), preferred_element_type=F32
    )
    sums = sums[0:MOMENTS] + sums[MOMENTS : 2 * MOMENTS]
    loads[...] = state[...]
    loads[:, 0:ROWS] = sums[0:8]
    loads[:, NZ : NZ + ROWS] = sums[8:16]
    for t in BESIDE:
        message[rows_of(t, 0, 8), :] = loads[...]
    packed = jnp.zeros((1, LANES), F32)
    for n, row in enumerate((place[0], *rows[1:], place[1])):
        packed = jnp.where(lane >> 2 == n, row, packed)
    for t in SENDS:
        if t not in BESIDE:
            message[rows_of(t, 0, 1), :] = packed

    pl.semaphore_wait(barrier, 14)
    for t in SENDS:
        there = 14 - t
        pltpu.make_async_remote_copy(
            src_ref=message.at[rows_of(t, 0, length(t))],
            dst_ref=arrived.at[rows_of(there, 0, length(t))],
            send_sem=near_send.at[0], recv_sem=near_recv.at[0],
            device_id=device(t), device_id_type=MESH,
        ).start()

    pltpu.make_async_copy(arrived.at[0:SENT], arrived.at[0:SENT], near_recv.at[0]).wait()
    group = (lanes8 & 63) >> 2
    full = state[...]
    where = jnp.where(lanes8 < NZ, ROWS, NZ + ROWS) + (lanes8 & 3)
    afar = 4 * jnp.where(jnp.logical_and(lanes8 >= NZ, rows8 == 0), 8, rows8) + (lanes8 & 3)
    for t in SENDS:
        if t in BESIDE:
            tile, at = arrived[rows_of(t, 0, 8), :], where
        else:
            tile, at = jnp.broadcast_to(arrived[rows_of(t, 0, 1), :], (CX, LANES)), afar
        spread = jnp.take_along_axis(tile, at, axis=1, mode="promise_in_bounds")
        full = jnp.where(group == t, spread, full)
    group = group[0:1]
    group_x = (
        (group >= 3).astype(jnp.int32) + (group >= 6).astype(jnp.int32)
        + (group >= 9).astype(jnp.int32) + (group >= 12).astype(jnp.int32)
    )
    moved = jnp.where(lane < NZ, (group_x - 2) * CX, (group - 3 * group_x - 1) * CY)
    centre_x = full[0:1] + moved.astype(F32)
    centre_y = pltpu.roll(centre_x, NZ, 1)
    centre_z = full[1:2]
    spin_x, spin_y, spin_z = full[5:6], full[6:7], full[7:8]
    table[0:1, :] = full[2:3] - (spin_y * centre_z - spin_z * centre_y)
    table[1:2, :] = full[3:4] - (spin_z * centre_x - spin_x * centre_z)
    table[2:3, :] = full[4:5] - (spin_x * centre_y - spin_y * centre_x)
    table[3:6, :] = full[5:8]

    lower = lanes8 < NZ
    halo_x = {}
    for side, names in ((0, X_UP), (1, X_DOWN)):
        t = NEAR.index((-1 if side == 0 else 1, 0))
        got = [arrived[rows_of(t, 8 + 8 * n, 16 + 8 * n), :] for n in range(8)]
        cells = (
            jnp.full((CX, LANES), -1.0 if side == 0 else float(CX), F32),
            (2 * rows8 + (lanes8 >> 6)).astype(F32),
            cell_z,
        )
        terms = sphere_terms(
            got[5], [v.astype(jnp.int32) for v in got[6:8]], table, cells, 12 + (-12 if side == 0 else 12)
        )
        for n, pop in enumerate(names):
            value = got[n] + term_of(terms, pop)
            shift = lane_shift(pop) % LANES
            if shift:
                value = pltpu.roll(value, shift, 1)
            step_y = int(VELOCITIES[pop, 1])
            if step_y:
                crossed = lower if step_y > 0 else jnp.logical_not(lower)
                value = jnp.where(crossed, pltpu.roll(value, step_y % CX, 0), value)
            halo_x[pop] = value
    from_low, from_high = NEAR.index((0, -1)), NEAR.index((0, 1))
    got_low = [arrived[rows_of(from_low, 8 + 8 * n, 16 + 8 * n), :] for n in range(4)]
    got_high = [arrived[rows_of(from_high, 8 + 8 * n, 16 + 8 * n), :] for n in range(4)]
    mixed = [jnp.where(lower, got_high[n], got_low[n]) for n in range(3)]
    cells = (cell_x, jnp.where(lower, float(CY), -1.0), cell_z)
    terms = sphere_terms(
        mixed[0], [v.astype(jnp.int32) for v in mixed[1:]], table, cells, jnp.where(lower, 16, 8)
    )
    halo_y = {}
    for names, got in ((Y_UP, got_low), (Y_DOWN, got_high)):
        for n, pop in enumerate(names):
            if n == STRAIGHT:
                value = pltpu.roll(got[3] + term_of(terms, pop), lane_shift(pop) % LANES, 1)
            else:
                value = got[n - (n > STRAIGHT)] + pltpu.roll(term_of(terms, pop), NZ, 1)
                if VELOCITIES[pop, 2]:
                    value = pltpu.roll(value, int(VELOCITIES[pop, 2]) % LANES, 1)
            step_x = int(VELOCITIES[pop, 0])
            if step_x:
                value = pltpu.roll(value, step_x % CX, 0)
            halo_y[pop] = value
    corner = [jnp.zeros((CX, LANES), F32) for _ in range(4)]
    corner_x = corner_y = jnp.zeros((CX, LANES), F32)
    corner_slot = jnp.zeros((CX, LANES), jnp.int32)
    for row, (pop, (sx, sy)) in enumerate(CORNERS.items()):
        t = NEAR.index((sx, sy))
        here = rows8 == row
        for n in range(4):
            piece = jnp.broadcast_to(arrived[rows_of(t, 8 + n, 9 + n), :], (CX, LANES))
            corner[n] = jnp.where(here, piece, corner[n])
        corner_x = jnp.where(here, -1.0 if sx < 0 else float(CX), corner_x)
        corner_y = jnp.where(here, -1.0 if sy < 0 else float(CY), corner_y)
        corner_slot = jnp.where(here, 12 + 12 * sx + 4 * sy, corner_slot)
    terms = sphere_terms(
        corner[1], [v.astype(jnp.int32) for v in corner[2:4]], table, (corner_x, corner_y, cell_z), corner_slot
    )
    corner_term = jnp.zeros((CX, LANES), F32)
    for row, pop in enumerate(CORNERS):
        corner_term = jnp.where(rows8 == row, term_of(terms, pop), corner_term)
    corner_of = pltpu.roll(corner[0] + corner_term, NZ, 1)

    for n, pop in enumerate((*X_UP, *X_DOWN)):
        halo[0, n] = halo_x[pop]
    for n, pop in enumerate((*Y_UP, *Y_DOWN)):
        halo[1, n] = halo_y[pop]
    corner_out[...] = corner_of

    def covers(chunk, carry):
        at = pl.ds(pl.multiple_of(chunk * LANES, LANES), LANES)
        cell_y = ((lanes8 >> 6) + 2 * chunk).astype(F32)
        terms = sphere_terms(
            post[19, :, at], [codes[layer, :, at] for layer in range(2)], table,
            (cell_x, cell_y, cell_z), 12,
        )
        post[0, :, at] = post[0, :, at] + terms[0][0]
        for pop in range(1, 19):
            post[pop, :, at] = post[pop, :, at] + term_of(terms, pop)
        return carry

    lax.fori_loop(0, CHUNKS, covers, 0, unroll=8)

    named = (lanes8 & 63) >> 2
    moment = jnp.where(named == 4, loads[...], 0.0)
    for t in BESIDE:
        dx, dy = NEAR[t]
        moment = jnp.where(named == (1 - dx) * 3 + 1 - dy, arrived[rows_of(t, 0, 8), :], moment)
    upper = pltpu.roll(moment, NZ, 1)
    m = [half[n : n + 1, :] for half in (moment, upper) for n in range(8)]
    group = lane >> 2
    group_x = (group >= 3).astype(jnp.int32) + (group >= 6).astype(jnp.int32)
    cx = state[0:1, :] + ((group_x - 1) * CX).astype(F32)
    cy = pltpu.roll(state[0:1, :], NZ, 1) + ((group - 3 * group_x - 1) * CY).astype(F32)
    cz = state[1:2, :] - 32.0
    vx, vy, vz, sx, sy, sz = [state[n : n + 1, :] for n in range(2, 8)]
    ex, ey, ez = m[1] - cx * m[0], m[2] - cy * m[0], m[3] - cz * m[0]
    qxx = m[4] - cx * (m[1] + ex)
    qyy = m[5] - cy * (m[2] + ey)
    qzz = m[6] - cz * (m[3] + ez)
    qxy = m[7] - cx * m[2] - cy * ex
    qxz = m[8] - cx * m[3] - cz * ex
    qyz = m[9] - cy * m[3] - cz * ey
    fx = m[10] - vx * m[0] - (sy * ez - sz * ey)
    fy = m[11] - vy * m[0] - (sz * ex - sx * ez)
    fz = m[12] - vz * m[0] - (sx * ey - sy * ex)
    tx = m[13] - (cy * m[12] - cz * m[11]) - (ey * vz - ez * vy) - (sx * (qyy + qzz) - sy * qxy - sz * qxz)
    ty = m[14] - (cz * m[10] - cx * m[12]) - (ez * vx - ex * vz) - (sy * (qxx + qzz) - sx * qxy - sz * qyz)
    tz = m[15] - (cx * m[11] - cy * m[10]) - (ex * vy - ey * vx) - (sz * (qxx + qyy) - sx * qxz - sy * qyz)
    force, torque = 1.0 / (255.0 * RADIUS**2), 1.0 / (255.0 * RADIUS**3)
    listed = (fx * force, fy * force, fz * force, tx * torque, ty * torque, tz * torque)
    tile = jnp.zeros((CX, LANES), F32)
    for n, value in enumerate(listed):
        tile = jnp.where(rows8 == n, jnp.broadcast_to(value, (CX, LANES)), tile)
    tile = jnp.where(lanes8 < 36, tile, 0.0)
    total = tile
    for g in range(1, 9):
        total = total + pltpu.roll(tile, LANES - 4 * g, 1)
    load_ref[...] = total.T[0:4, 0:6]
    pltpu.make_async_copy(message.at[0:SENT], message.at[0:SENT], near_send.at[0]).wait()


def finish(post, halo, corner_of, load, out_hbm, load_hbm, out, out_sem):
    put_load = pltpu.make_async_copy(load, load_hbm, out_sem.at[19])
    put_load.start()
    puts = []
    lanes8 = lax.broadcasted_iota(jnp.int32, (CX, LANES), 1)
    rows8 = lax.broadcasted_iota(jnp.int32, (CX, LANES), 0)
    lower = lanes8 < NZ
    z_of = lax.broadcasted_iota(jnp.int32, (CX, CELLS), 1) & (NZ - 1)
    edge = {1: z_of == 0, -1: z_of == NZ - 1}
    row_of = lax.broadcasted_iota(jnp.int32, (CX, CELLS), 0)
    for pop in range(19):
        step_x, step_y, step_z = (int(v) for v in VELOCITIES[pop])
        value = post[pop]
        shift = lane_shift(pop) % CELLS
        if shift:
            value = pltpu.roll(value, shift, 1)
        if step_x:
            value = pltpu.roll(value, step_x % CX, 0)
            row = 0 if step_x > 0 else CX - 1
            n = (*X_UP, *X_DOWN).index(pop)
            beside_x = jnp.concatenate(
                [jnp.broadcast_to(halo[0, n, c : c + 1, :], (CX, LANES)) for c in range(CHUNKS)], axis=1
            )
            value = jnp.where(row_of == row, beside_x, value)
        if step_y:
            tile = halo[1, (*Y_UP, *Y_DOWN).index(pop)]
            if step_x:
                k = list(CORNERS).index(pop)
                tile = jnp.where(rows8 == row, jnp.broadcast_to(corner_of[k : k + 1, :], (CX, LANES)), tile)
            if step_y > 0:
                value = jnp.concatenate([jnp.where(lower, tile, value[:, :LANES]), value[:, LANES:]], axis=1)
            else:
                value = jnp.concatenate([value[:, :-LANES], jnp.where(lower, value[:, -LANES:], tile)], axis=1)
        if step_z:
            value = jnp.where(edge[step_z], post[OPPOSITE[pop]], value)
        if pop:
            out[pop] = value
        source = out if pop else post
        puts.append(pltpu.make_async_copy(source.at[pop], out_hbm.at[pop], out_sem.at[0]))
        puts[-1].start()
    put_load.wait()
    pltpu.make_async_copy(out, out_hbm, out_sem.at[0]).wait()


def per_device(populations, cover_codes, sphere_cell, sphere_velocity, sphere_spin, relax_rates):
    vmem, anywhere = pl.BlockSpec(memory_space=pltpu.VMEM), pl.BlockSpec(memory_space=pl.ANY)
    dma = pltpu.SemaphoreType.DMA
    post, halo, corner, load = pl.pallas_call(
        kernel,
        out_shape=(
            pltpu.VMEM((20, CX, CELLS), F32),
            pltpu.VMEM((2, 10, CX, LANES), F32),
            pltpu.VMEM((CX, LANES), F32),
            pltpu.VMEM((4, 6), F32),
        ),
        in_specs=[anywhere] * 7,
        out_specs=(vmem,) * 4,
        scratch_shapes=[
            pltpu.SMEM((3, 1, 1, 4), jnp.int32),
            pltpu.SMEM((3, 1, 1, 4), F32),
            pltpu.SMEM((3, 1, 1, 4), F32),
            pltpu.SMEM((15,), F32),
            pltpu.VMEM((64, 16), F32),
            pltpu.VMEM((19, CX, CELLS), F32),
            pltpu.VMEM((2, CX, CELLS), jnp.int32),
            pltpu.VMEM((64, LANES), F32),
            pltpu.VMEM((CHUNKS, MOMENTS * CX, LANES), F32),
            pltpu.VMEM((ROWS, CX * CELLS), jnp.bfloat16),
            pltpu.VMEM((2 * MOMENTS, CX * CELLS), jnp.bfloat16),
            pltpu.VMEM((8, LANES), F32),
            pltpu.VMEM((TOTAL, LANES), F32),
            pltpu.VMEM((TOTAL, LANES), F32),
            pltpu.VMEM((8, LANES), F32),
            pltpu.VMEM((8, LANES), F32),
            dma((7,)),
            dma((1,)),
            dma((1,)),
        ],
        compiler_params=pltpu.CompilerParams(
            collective_id=0, has_side_effects=True, vmem_limit_bytes=60 * 1024 * 1024
        ),
    )(
        populations, cover_codes, sphere_cell, sphere_velocity, sphere_spin, relax_rates,
        jnp.asarray(coefficient_rows()),
    )
    out, load = pl.pallas_call(
        finish,
        out_shape=(jax.ShapeDtypeStruct((19, CX, CELLS), F32), jax.ShapeDtypeStruct((4, 6), F32)),
        in_specs=[vmem] * 4,
        out_specs=(anywhere, anywhere),
        scratch_shapes=[pltpu.VMEM((19, CX, CELLS), F32), dma((20,))],
        compiler_params=pltpu.CompilerParams(vmem_limit_bytes=8 * 1024 * 1024),
    )(*[pltpu.with_memory_space_constraint(v, pltpu.VMEM) for v in (post, halo, corner, load)])
    return out, load.T.reshape(6, 1, 1, 4)


def solution(mesh):
    placed = (
        P(None, "bx", "by"),
        P(None, "bx", "by"),
        P(None, "bx", "by", None),
        P(None, "bx", "by", None),
        P(None, "bx", "by", None),
        P(),
    )
    return jax.shard_map(
        per_device,
        mesh=mesh,
        in_specs=placed,
        out_specs=(P(None, "bx", "by"), P(None, "bx", "by", None)),
        check_vma=False,
    )
```

```python
import jax
import jax.numpy as jnp
import numpy as np
from jax import lax
from jax.experimental import pallas as pl
from jax.experimental.pallas import tpu as pltpu
from jax.sharding import PartitionSpec as P

NZ = 64
RADIUS = 8
CX, CY = 8, 16
CELLS = CY * NZ
LANES = 128
CHUNKS = CELLS // LANES
MESH = pl.DeviceIdType.MESH
F32 = jnp.float32

VELOCITIES = np.array(
    [
        [0, 0, 0],
        [1, 0, 0],
        [-1, 0, 0],
        [0, 1, 0],
        [0, -1, 0],
        [0, 0, 1],
        [0, 0, -1],
        [1, 1, 0],
        [-1, -1, 0],
        [1, -1, 0],
        [-1, 1, 0],
        [1, 0, 1],
        [-1, 0, -1],
        [1, 0, -1],
        [-1, 0, 1],
        [0, 1, 1],
        [0, -1, -1],
        [0, 1, -1],
        [0, -1, 1],
    ]
)
OPPOSITE = [0, 2, 1, 4, 3, 6, 5, 8, 7, 10, 9, 12, 11, 14, 13, 16, 15, 18, 17]
X_UP, X_DOWN = (1, 7, 9, 11, 13), (2, 8, 10, 12, 14)
Y_UP, Y_DOWN = (3, 7, 10, 15, 17), (4, 8, 9, 16, 18)
NEAR = [(dx, dy) for dx in range(-2, 3) for dy in range(-1, 2)]
HERE = NEAR.index((0, 0))
SENDS = [0, 2, 12, 14, 1, 13, 4, 10, 3, 5, 9, 11, 6, 8]
BESIDE = [t for t in SENDS if abs(NEAR[t][0]) < 2]
STRAIGHT = 3
CORNERS = {7: (-1, -1), 8: (1, 1), 9: (-1, 1), 10: (1, -1)}
MOMENTS = 16
ROWS = 48


def moment_rows():
    vel_x, vel_y, vel_z = [VELOCITIES[:, component] * 1.0 for component in range(3)]
    monomials = [
        np.ones(19),
        vel_x,
        vel_y,
        vel_z,
        vel_x * vel_x,
        vel_y * vel_y,
        vel_z * vel_z,
        vel_x * vel_y,
        vel_x * vel_z,
        vel_y * vel_z,
        vel_x * vel_x * vel_y,
        vel_x * vel_x * vel_z,
        vel_y * vel_y * vel_x,
        vel_y * vel_y * vel_z,
        vel_z * vel_z * vel_x,
        vel_z * vel_z * vel_y,
        vel_x * vel_x * vel_y * vel_y,
        vel_x * vel_x * vel_z * vel_z,
        vel_y * vel_y * vel_z * vel_z,
    ]
    orthonormal = []
    for vector in monomials:
        vector = vector.copy()
        for earlier in orthonormal:
            vector = vector - np.dot(earlier, vector) * earlier
        orthonormal.append(vector / np.sqrt(np.dot(vector, vector)))
    return np.stack(orthonormal)


def coefficient_rows():
    rows = moment_rows()[4:]
    even = [1, 3, 5, 7, 11, 15]
    out = []
    for a in even:
        for b in even:
            keep = np.isin(np.arange(15), [0, 1, 2, 12, 13, 14])
            out.append(rows[:, a] * (rows[:, b] - rows[:, 0]) * keep)
    for axis, first, second, rates in ((1, 7, 11, (8, 10)), (3, 7, 15, (6, 11)), (5, 11, 15, (7, 9))):
        for a in (first, second):
            for b in (first, second):
                keep = np.isin(np.arange(15), rates)
                out.append(rows[:, a] * (rows[:, b] - rows[:, axis]) * keep)
    for rate in (3, 4, 5):
        out.append(0.25 * (np.arange(15) == rate))
    table = np.zeros((64, 16), np.float32)
    table[: len(out), :15] = np.stack(out)
    return table


def length(t):
    dx, dy = NEAR[t]
    return 0 if t == HERE else 1 if abs(dx) == 2 else 12 if dx and dy else 72 if dx else 40


FIRST = [0] + [sum(-(-length(t) // 8) * 8 for t in range(n + 1)) for n in range(15)]
TOTAL = FIRST[15]
SENT = sum(length(t) for t in range(15))


def rows_of(t, start, stop):
    return slice(FIRST[t] + start, FIRST[t] + stop)


def lane_shift(pop):
    return int(VELOCITIES[pop, 1]) * NZ + int(VELOCITIES[pop, 2])


def sphere_terms(density, codes, table, cell, first_slot):
    flow, square, cover = None, None, None
    for packed in codes:
        slot = ((packed >> 8) + first_slot) & 63
        weight = (packed & 255).astype(F32) * (1.0 / 255.0) * density
        ax, ay, az, sx, sy, sz = [
            jnp.take_along_axis(
                jnp.broadcast_to(table[n : n + 1, :], (CX, LANES)), slot,
                axis=1, mode="promise_in_bounds",
            )
            for n in range(6)
        ]
        wx = ax + (sy * cell[2] - sz * cell[1])
        wy = ay + (sz * cell[0] - sx * cell[2])
        wz = az + (sx * cell[1] - sy * cell[0])
        bx, by, bz = weight * wx, weight * wy, weight * wz
        one = (bx, by, bz)
        two = (bx * wx, by * wy, bz * wz, bx * wy, bx * wz, by * wz)
        if flow is None:
            flow, square, cover = one, two, weight
        else:
            flow = [a + b for a, b in zip(flow, one)]
            square = [a + b for a, b in zip(square, two)]
            cover = cover + weight
    hx, hy, hz = [value * (1.0 / 12.0) for value in flow]
    qxx, qyy, qzz, qxy, qxz, qyz = square
    base = cover * (1.0 / 18.0) - (qxx + qyy + qzz) * (1.0 / 12.0)
    half = 0.5 * base
    exx, eyy, ezz = 0.125 * qxx, 0.125 * qyy, 0.125 * qzz
    exy, exz, eyz = 0.25 * qxy, 0.25 * qxz, 0.25 * qyz
    b_xy, b_xz, b_yz = half + (exx + eyy), half + (exx + ezz), half + (eyy + ezz)
    return {
        0: (6.0 * base, None),
        1: (base + 2.0 * exx, 2.0 * hx),
        3: (base + 2.0 * eyy, 2.0 * hy),
        5: (base + 2.0 * ezz, 2.0 * hz),
        7: (b_xy + exy, hx + hy),
        9: (b_xy - exy, hx - hy),
        11: (b_xz + exz, hx + hz),
        13: (b_xz - exz, hx - hz),
        15: (b_yz + eyz, hy + hz),
        17: (b_yz - eyz, hy - hz),
    }


def term_of(terms, pop):
    even, odd = terms[pop if pop % 2 else pop - 1]
    return even + odd if pop % 2 else even - odd


def kernel(
    pops_hbm, codes_hbm, cell_hbm, vel_hbm, spin_hbm, rates_hbm, coef_hbm,
    post, halo, corner_out, load_ref,
    cell_ref, vel_ref, spin_ref, rates_ref, coef_in, f, codes, coef, parts, weights, split,
    state, message, arrived, table, loads,
    in_sem, near_send, near_recv,
):
    nx, ny = lax.axis_size("bx"), lax.axis_size("by")
    me_x, me_y = lax.axis_index("bx"), lax.axis_index("by")

    def wrapped(at, size):
        return jnp.where(at < 0, at + size, jnp.where(at >= size, at - size, at))

    x_of = {d: wrapped(me_x + d, nx) for d in range(-2, 3)}
    y_of = {d: wrapped(me_y + d, ny) for d in range(-1, 2)}

    def device(t):
        dx, dy = NEAR[t]
        return (x_of[dx], y_of[dy])

    barrier = pltpu.get_barrier_semaphore()
    for t in SENDS:
        pl.semaphore_signal(barrier, inc=1, device_id=device(t), device_id_type=MESH)
    fetched = []
    for n, (src, dst) in enumerate(
        (
            (cell_hbm, cell_ref), (vel_hbm, vel_ref), (spin_hbm, spin_ref), (rates_hbm, rates_ref),
            (coef_hbm, coef_in), (codes_hbm, codes), (pops_hbm, f),
        )
    ):
        fetched.append(pltpu.make_async_copy(src, dst, in_sem.at[n]))
        fetched[-1].start()

    lane = lax.broadcasted_iota(jnp.int32, (1, LANES), 1)
    sphere = lane & 3

    def along(values):
        return jnp.where(
            sphere < 2,
            jnp.where(sphere == 0, values[0], values[1]),
            jnp.where(sphere == 2, values[2], values[3]),
        )

    for copy in fetched[:5]:
        copy.wait()
    place = [along([cell_ref[n, 0, 0, k].astype(F32) for k in range(4)]) for n in range(3)]
    rows = [jnp.where(lane < NZ, place[0], place[1]), place[2]]
    for source in (vel_ref, spin_ref):
        for n in range(3):
            rows.append(along([source[n, 0, 0, k] for k in range(4)]))
    for n, row in enumerate(rows):
        state[n : n + 1, :] = row

    which = lax.broadcasted_iota(jnp.int32, (16, LANES), 0)
    rates = jnp.zeros((16, LANES), F32)
    for r in range(15):
        rates = jnp.where(which == r, rates_ref[r], rates)
    coef[...] = jnp.dot(
        coef_in[...], rates, precision=lax.Precision.HIGHEST, preferred_element_type=F32
    )

    lanes8 = lax.broadcasted_iota(jnp.int32, (CX, LANES), 1)
    rows8 = lax.broadcasted_iota(jnp.int32, (CX, LANES), 0)
    cell_x = rows8.astype(F32)
    cell_z = (lanes8 & (NZ - 1)).astype(F32)

    fetched[5].wait()
    slot_rows = lax.broadcasted_iota(jnp.int32, (ROWS, CELLS), 0)

    def fill(row, carry):
        total = None
        for layer in range(2):
            packed = codes[layer, pl.ds(row, 1), :]
            level = (packed & 255).astype(F32)
            hit = jnp.where((packed >> 8) == slot_rows, level, 0.0)
            total = hit if total is None else total + hit
        weights[:, pl.ds(pl.multiple_of(row * CELLS, CELLS), CELLS)] = total.astype(jnp.bfloat16)
        return carry

    lax.fori_loop(0, CX, fill, 0, unroll=8)
    fetched[6].wait()

    def fluid(chunk, carry):
        at = pl.ds(pl.multiple_of(chunk * LANES, LANES), LANES)
        p = [f[i, :, at] for i in range(19)]
        s = {a: p[a] + p[a + 1] for a in range(1, 19, 2)}
        d = {a: p[a] - p[a + 1] for a in range(1, 19, 2)}
        s_xy, a_xy = s[7] + s[9], s[7] - s[9]
        s_xz, a_xz = s[11] + s[13], s[11] - s[13]
        s_yz, a_yz = s[15] + s[17], s[15] - s[17]
        x1, x2 = d[7] + d[9], d[11] + d[13]
        y1, y2 = d[7] - d[9], d[15] + d[17]
        z1, z2 = d[11] - d[13], d[15] - d[17]
        density = (p[0] + s[1]) + (s[3] + s[5]) + (s_xy + s_xz) + s_yz
        jx, jy, jz = d[1] + x1 + x2, d[3] + y1 + y2, d[5] + z1 + z2
        inverse = 1.0 / density
        ux, uy, uz = jx * inverse, jy * inverse, jz * inverse
        code_of = [codes[layer, :, at] for layer in range(2)]
        cover = ((code_of[0] & 255) + (code_of[1] & 255)).astype(F32) * (1.0 / 255.0)

        my = ((lanes8 >> 6) + 2 * chunk).astype(F32)
        mz = cell_z - 32.0
        dx, dy, dz = density * cell_x, density * my, density * mz
        listed = (
            density, dx, dy, dz, dx * cell_x, dy * my, dz * mz, dx * my, dx * mz, dy * mz,
            jx, jy, jz, my * jz - mz * jy, mz * jx - cell_x * jz, cell_x * jy - my * jx,
        )
        for n, value in enumerate(listed):
            parts[chunk, CX * n : CX * (n + 1), :] = value

        keep = 1.0 - cover
        hx, hy, hz = 0.5 * jx * ux, 0.5 * jy * uy, 0.5 * jz * uz
        cxy, cxz, cyz = jx * uy, jx * uz, jy * uz
        base = density * (1.0 / 9.0) - (hx + hy + hz) * (1.0 / 3.0)
        e_x, e_y, e_z = base + hx, base + hy, base + hz
        e_xy, e_xz, e_yz = e_x + hy, e_x + hz, e_y + hz
        even = [s[1] - e_x, s[3] - e_y, s[5] - e_z, s_xy - e_xy, s_xz - e_xz, s_yz - e_yz]
        even = [keep * value for value in even]

        def c(n):
            return jnp.broadcast_to(coef[n : n + 1, :], (CX, LANES))

        sums = []
        for a in range(6):
            total = c(6 * a) * even[0]
            for b in range(1, 6):
                total = total + c(6 * a + b) * even[b]
            sums.append(total)
        third = 1.0 / 3.0
        odd = []
        for axis, (first, second, flow) in enumerate(((x1, x2, jx), (y1, y2, jy), (z1, z2, jz))):
            level = flow * third
            first, second = keep * (first - level), keep * (second - level)
            k = 36 + 4 * axis
            near = c(k) * first + c(k + 1) * second
            far = c(k + 2) * first + c(k + 3) * second
            odd.append((-2.0 * (near + far), near, far))
        n_xy = keep * (a_xy - cxy) * c(48)
        n_xz = keep * (a_xz - cxz) * c(49)
        n_yz = keep * (a_yz - cyz) * c(50)
        half, quarter = 0.5 * cover, 0.25 * cover
        gx, gy, gz = jx * (1.0 / 12.0), jy * (1.0 / 12.0), jz * (1.0 / 12.0)
        pairs = {
            1: (sums[0] + half * e_x, odd[0][0], 2.0 * gx),
            3: (sums[1] + half * e_y, odd[1][0], 2.0 * gy),
            5: (sums[2] + half * e_z, odd[2][0], 2.0 * gz),
            7: (sums[3] + n_xy + quarter * (e_xy + cxy), odd[0][1] + odd[1][1], gx + gy),
            9: (sums[3] - n_xy + quarter * (e_xy - cxy), odd[0][1] - odd[1][1], gx - gy),
            11: (sums[4] + n_xz + quarter * (e_xz + cxz), odd[0][2] + odd[2][1], gx + gz),
            13: (sums[4] - n_xz + quarter * (e_xz - cxz), odd[0][2] - odd[2][1], gx - gz),
            15: (sums[5] + n_yz + quarter * (e_yz + cyz), odd[1][2] + odd[2][2], gy + gz),
            17: (sums[5] - n_yz + quarter * (e_yz - cyz), odd[1][2] - odd[2][2], gy - gz),
        }
        rest = 2.0 * (sums[0] + sums[1] + sums[2]) + 4.0 * (sums[3] + sums[4] + sums[5])
        g = {0: p[0] + rest - 3.0 * cover * base}
        for a, (ev, od, flow) in pairs.items():
            od = od + cover * (d[a] - flow)
            g[a] = p[a] - ev - od
            g[a + 1] = p[a + 1] - ev + od
        for pop in range(19):
            post[pop, :, at] = g[pop]
        post[19, :, at] = density

        common = [density] + [value.astype(F32) for value in code_of]
        for row, names in ((CX - 1, X_UP), (0, X_DOWN)):
            t = NEAR.index((1 if row else -1, 0))
            for n, value in enumerate([g[pop] for pop in names] + common):
                message[pl.ds(FIRST[t] + 8 + 8 * n + chunk, 1), :] = value[row : row + 1, :]
        return carry

    lax.fori_loop(0, CHUNKS, fluid, 0, unroll=8)

    codes_f = {c: [codes[layer, :, c * LANES : (c + 1) * LANES].astype(F32) for layer in range(2)] for c in (0, CHUNKS - 1)}
    for dy, names in ((1, Y_UP), (-1, Y_DOWN)):
        c = CHUNKS - 1 if dy > 0 else 0
        t = NEAR.index((0, dy))
        at = slice(c * LANES, (c + 1) * LANES)
        straight = [post[19, :, at], *codes_f[c], post[names[STRAIGHT], :, at]]
        turned = [pltpu.roll(post[pop, :, at], NZ, 1) for n, pop in enumerate(names) if n != STRAIGHT]
        for n, (one, two) in enumerate(zip(straight, turned)):
            message[rows_of(t, 8 + 8 * n, 16 + 8 * n), :] = jnp.where(
                lanes8 < NZ, *((two, one) if dy > 0 else (one, two))
            )
    for pop, (sx, sy) in CORNERS.items():
        t = NEAR.index((-sx, -sy))
        row = CX - 1 if sx < 0 else 0
        c = CHUNKS - 1 if sy < 0 else 0
        at = slice(c * LANES, (c + 1) * LANES)
        for n, value in enumerate([post[pop, :, at], post[19, :, at]] + codes_f[c]):
            message[rows_of(t, 8 + n, 9 + n), :] = value[row : row + 1, :]

    def halves(chunk, carry):
        for row in range(CX):
            value = parts[chunk, pl.ds(row, MOMENTS, stride=CX), :]
            high = value.astype(jnp.bfloat16).astype(F32)
            both = jnp.concatenate([high, value - high], axis=0)
            at = pl.multiple_of(row * CELLS + chunk * LANES, LANES)
            split[:, pl.ds(at, LANES)] = both.astype(jnp.bfloat16)
        return carry

    lax.fori_loop(0, CHUNKS, halves, 0, unroll=8)
    sums = lax.dot_general(
        split[...], weights[...], (((1,), (1,)), ((), ())), preferred_element_type=F32
    )
    sums = sums[0:MOMENTS] + sums[MOMENTS : 2 * MOMENTS]
    loads[...] = state[...]
    loads[:, 0:ROWS] = sums[0:8]
    loads[:, NZ : NZ + ROWS] = sums[8:16]
    for t in BESIDE:
        message[rows_of(t, 0, 8), :] = loads[...]
    packed = jnp.zeros((1, LANES), F32)
    for n, row in enumerate((place[0], *rows[1:], place[1])):
        packed = jnp.where(lane >> 2 == n, row, packed)
    for t in SENDS:
        if t not in BESIDE:
            message[rows_of(t, 0, 1), :] = packed

    pl.semaphore_wait(barrier, 14)
    for t in SENDS:
        there = 14 - t
        pltpu.make_async_remote_copy(
            src_ref=message.at[rows_of(t, 0, length(t))],
            dst_ref=arrived.at[rows_of(there, 0, length(t))],
            send_sem=near_send.at[0], recv_sem=near_recv.at[0],
            device_id=device(t), device_id_type=MESH,
        ).start()

    pltpu.make_async_copy(arrived.at[0:SENT], arrived.at[0:SENT], near_recv.at[0]).wait()
    group = (lanes8 & 63) >> 2
    full = state[...]
    where = jnp.where(lanes8 < NZ, ROWS, NZ + ROWS) + (lanes8 & 3)
    afar = 4 * jnp.where(jnp.logical_and(lanes8 >= NZ, rows8 == 0), 8, rows8) + (lanes8 & 3)
    for t in SENDS:
        if t in BESIDE:
            tile, at = arrived[rows_of(t, 0, 8), :], where
        else:
            tile, at = jnp.broadcast_to(arrived[rows_of(t, 0, 1), :], (CX, LANES)), afar
        spread = jnp.take_along_axis(tile, at, axis=1, mode="promise_in_bounds")
        full = jnp.where(group == t, spread, full)
    group = group[0:1]
    group_x = (
        (group >= 3).astype(jnp.int32) + (group >= 6).astype(jnp.int32)
        + (group >= 9).astype(jnp.int32) + (group >= 12).astype(jnp.int32)
    )
    moved = jnp.where(lane < NZ, (group_x - 2) * CX, (group - 3 * group_x - 1) * CY)
    centre_x = full[0:1] + moved.astype(F32)
    centre_y = pltpu.roll(centre_x, NZ, 1)
    centre_z = full[1:2]
    spin_x, spin_y, spin_z = full[5:6], full[6:7], full[7:8]
    table[0:1, :] = full[2:3] - (spin_y * centre_z - spin_z * centre_y)
    table[1:2, :] = full[3:4] - (spin_z * centre_x - spin_x * centre_z)
    table[2:3, :] = full[4:5] - (spin_x * centre_y - spin_y * centre_x)
    table[3:6, :] = full[5:8]

    lower = lanes8 < NZ
    halo_x = {}
    for side, names in ((0, X_UP), (1, X_DOWN)):
        t = NEAR.index((-1 if side == 0 else 1, 0))
        got = [arrived[rows_of(t, 8 + 8 * n, 16 + 8 * n), :] for n in range(8)]
        cells = (
            jnp.full((CX, LANES), -1.0 if side == 0 else float(CX), F32),
            (2 * rows8 + (lanes8 >> 6)).astype(F32),
            cell_z,
        )
        terms = sphere_terms(
            got[5], [v.astype(jnp.int32) for v in got[6:8]], table, cells, 12 + (-12 if side == 0 else 12)
        )
        for n, pop in enumerate(names):
            value = got[n] + term_of(terms, pop)
            shift = lane_shift(pop) % LANES
            if shift:
                value = pltpu.roll(value, shift, 1)
            step_y = int(VELOCITIES[pop, 1])
            if step_y:
                crossed = lower if step_y > 0 else jnp.logical_not(lower)
                value = jnp.where(crossed, pltpu.roll(value, step_y % CX, 0), value)
            halo_x[pop] = value
    from_low, from_high = NEAR.index((0, -1)), NEAR.index((0, 1))
    got_low = [arrived[rows_of(from_low, 8 + 8 * n, 16 + 8 * n), :] for n in range(4)]
    got_high = [arrived[rows_of(from_high, 8 + 8 * n, 16 + 8 * n), :] for n in range(4)]
    mixed = [jnp.where(lower, got_high[n], got_low[n]) for n in range(3)]
    cells = (cell_x, jnp.where(lower, float(CY), -1.0), cell_z)
    terms = sphere_terms(
        mixed[0], [v.astype(jnp.int32) for v in mixed[1:]], table, cells, jnp.where(lower, 16, 8)
    )
    halo_y = {}
    for names, got in ((Y_UP, got_low), (Y_DOWN, got_high)):
        for n, pop in enumerate(names):
            if n == STRAIGHT:
                value = pltpu.roll(got[3] + term_of(terms, pop), lane_shift(pop) % LANES, 1)
            else:
                value = got[n - (n > STRAIGHT)] + pltpu.roll(term_of(terms, pop), NZ, 1)
                if VELOCITIES[pop, 2]:
                    value = pltpu.roll(value, int(VELOCITIES[pop, 2]) % LANES, 1)
            step_x = int(VELOCITIES[pop, 0])
            if step_x:
                value = pltpu.roll(value, step_x % CX, 0)
            halo_y[pop] = value
    corner = [jnp.zeros((CX, LANES), F32) for _ in range(4)]
    corner_x = corner_y = jnp.zeros((CX, LANES), F32)
    corner_slot = jnp.zeros((CX, LANES), jnp.int32)
    for row, (pop, (sx, sy)) in enumerate(CORNERS.items()):
        t = NEAR.index((sx, sy))
        here = rows8 == row
        for n in range(4):
            piece = jnp.broadcast_to(arrived[rows_of(t, 8 + n, 9 + n), :], (CX, LANES))
            corner[n] = jnp.where(here, piece, corner[n])
        corner_x = jnp.where(here, -1.0 if sx < 0 else float(CX), corner_x)
        corner_y = jnp.where(here, -1.0 if sy < 0 else float(CY), corner_y)
        corner_slot = jnp.where(here, 12 + 12 * sx + 4 * sy, corner_slot)
    terms = sphere_terms(
        corner[1], [v.astype(jnp.int32) for v in corner[2:4]], table, (corner_x, corner_y, cell_z), corner_slot
    )
    corner_term = jnp.zeros((CX, LANES), F32)
    for row, pop in enumerate(CORNERS):
        corner_term = jnp.where(rows8 == row, term_of(terms, pop), corner_term)
    corner_of = pltpu.roll(corner[0] + corner_term, NZ, 1)

    for n, pop in enumerate((*X_UP, *X_DOWN)):
        halo[0, n] = halo_x[pop]
    for n, pop in enumerate((*Y_UP, *Y_DOWN)):
        halo[1, n] = halo_y[pop]
    corner_out[...] = corner_of

    def covers(chunk, carry):
        at = pl.ds(pl.multiple_of(chunk * LANES, LANES), LANES)
        cell_y = ((lanes8 >> 6) + 2 * chunk).astype(F32)
        terms = sphere_terms(
            post[19, :, at], [codes[layer, :, at] for layer in range(2)], table,
            (cell_x, cell_y, cell_z), 12,
        )
        post[0, :, at] = post[0, :, at] + terms[0][0]
        for pop in range(1, 19):
            post[pop, :, at] = post[pop, :, at] + term_of(terms, pop)
        return carry

    lax.fori_loop(0, CHUNKS, covers, 0, unroll=8)

    named = (lanes8 & 63) >> 2
    moment = jnp.where(named == 4, loads[...], 0.0)
    for t in BESIDE:
        dx, dy = NEAR[t]
        moment = jnp.where(named == (1 - dx) * 3 + 1 - dy, arrived[rows_of(t, 0, 8), :], moment)
    upper = pltpu.roll(moment, NZ, 1)
    m = [half[n : n + 1, :] for half in (moment, upper) for n in range(8)]
    group = lane >> 2
    group_x = (group >= 3).astype(jnp.int32) + (group >= 6).astype(jnp.int32)
    cx = state[0:1, :] + ((group_x - 1) * CX).astype(F32)
    cy = pltpu.roll(state[0:1, :], NZ, 1) + ((group - 3 * group_x - 1) * CY).astype(F32)
    cz = state[1:2, :] - 32.0
    vx, vy, vz, sx, sy, sz = [state[n : n + 1, :] for n in range(2, 8)]
    ex, ey, ez = m[1] - cx * m[0], m[2] - cy * m[0], m[3] - cz * m[0]
    qxx = m[4] - cx * (m[1] + ex)
    qyy = m[5] - cy * (m[2] + ey)
    qzz = m[6] - cz * (m[3] + ez)
    qxy = m[7] - cx * m[2] - cy * ex
    qxz = m[8] - cx * m[3] - cz * ex
    qyz = m[9] - cy * m[3] - cz * ey
    fx = m[10] - vx * m[0] - (sy * ez - sz * ey)
    fy = m[11] - vy * m[0] - (sz * ex - sx * ez)
    fz = m[12] - vz * m[0] - (sx * ey - sy * ex)
    tx = m[13] - (cy * m[12] - cz * m[11]) - (ey * vz - ez * vy) - (sx * (qyy + qzz) - sy * qxy - sz * qxz)
    ty = m[14] - (cz * m[10] - cx * m[12]) - (ez * vx - ex * vz) - (sy * (qxx + qzz) - sx * qxy - sz * qyz)
    tz = m[15] - (cx * m[11] - cy * m[10]) - (ex * vy - ey * vx) - (sz * (qxx + qyy) - sx * qxz - sy * qyz)
    force, torque = 1.0 / (255.0 * RADIUS**2), 1.0 / (255.0 * RADIUS**3)
    listed = (fx * force, fy * force, fz * force, tx * torque, ty * torque, tz * torque)
    tile = jnp.zeros((CX, LANES), F32)
    for n, value in enumerate(listed):
        tile = jnp.where(rows8 == n, jnp.broadcast_to(value, (CX, LANES)), tile)
    tile = jnp.where(lanes8 < 36, tile, 0.0)
    total = tile
    for g in range(1, 9):
        total = total + pltpu.roll(tile, LANES - 4 * g, 1)
    load_ref[...] = total.T[0:4, 0:6]
    pltpu.make_async_copy(message.at[0:SENT], message.at[0:SENT], near_send.at[0]).wait()


def finish(post, halo, corner_of, load, out_hbm, load_hbm, out, out_sem):
    put_load = pltpu.make_async_copy(load, load_hbm, out_sem.at[19])
    put_load.start()
    puts = []
    lanes8 = lax.broadcasted_iota(jnp.int32, (CX, LANES), 1)
    rows8 = lax.broadcasted_iota(jnp.int32, (CX, LANES), 0)
    lower = lanes8 < NZ
    z_of = lax.broadcasted_iota(jnp.int32, (CX, CELLS), 1) & (NZ - 1)
    edge = {1: z_of == 0, -1: z_of == NZ - 1}
    row_of = lax.broadcasted_iota(jnp.int32, (CX, CELLS), 0)
    for pop in range(19):
        step_x, step_y, step_z = (int(v) for v in VELOCITIES[pop])
        value = post[pop]
        shift = lane_shift(pop) % CELLS
        if shift:
            value = pltpu.roll(value, shift, 1)
        if step_x:
            value = pltpu.roll(value, step_x % CX, 0)
            row = 0 if step_x > 0 else CX - 1
            n = (*X_UP, *X_DOWN).index(pop)
            beside_x = jnp.concatenate(
                [jnp.broadcast_to(halo[0, n, c : c + 1, :], (CX, LANES)) for c in range(CHUNKS)], axis=1
            )
            value = jnp.where(row_of == row, beside_x, value)
        if step_y:
            tile = halo[1, (*Y_UP, *Y_DOWN).index(pop)]
            if step_x:
                k = list(CORNERS).index(pop)
                tile = jnp.where(rows8 == row, jnp.broadcast_to(corner_of[k : k + 1, :], (CX, LANES)), tile)
            if step_y > 0:
                value = jnp.concatenate([jnp.where(lower, tile, value[:, :LANES]), value[:, LANES:]], axis=1)
            else:
                value = jnp.concatenate([value[:, :-LANES], jnp.where(lower, value[:, -LANES:], tile)], axis=1)
        if step_z:
            value = jnp.where(edge[step_z], post[OPPOSITE[pop]], value)
        if pop:
            out[pop] = value
        source = out if pop else post
        puts.append(pltpu.make_async_copy(source.at[pop], out_hbm.at[pop], out_sem.at[0]))
        puts[-1].start()
    put_load.wait()
    pltpu.make_async_copy(out, out_hbm, out_sem.at[0]).wait()


def per_device(populations, cover_codes, sphere_cell, sphere_velocity, sphere_spin, relax_rates):
    vmem, anywhere = pl.BlockSpec(memory_space=pltpu.VMEM), pl.BlockSpec(memory_space=pl.ANY)
    dma = pltpu.SemaphoreType.DMA
    post, halo, corner, load = pl.pallas_call(
        kernel,
        out_shape=(
            pltpu.VMEM((20, CX, CELLS), F32),
            pltpu.VMEM((2, 10, CX, LANES), F32),
            pltpu.VMEM((CX, LANES), F32),
            pltpu.VMEM((4, 6), F32),
        ),
        in_specs=[anywhere] * 7,
        out_specs=(vmem,) * 4,
        scratch_shapes=[
            pltpu.SMEM((3, 1, 1, 4), jnp.int32),
            pltpu.SMEM((3, 1, 1, 4), F32),
            pltpu.SMEM((3, 1, 1, 4), F32),
            pltpu.SMEM((15,), F32),
            pltpu.VMEM((64, 16), F32),
            pltpu.VMEM((19, CX, CELLS), F32),
            pltpu.VMEM((2, CX, CELLS), jnp.int32),
            pltpu.VMEM((64, LANES), F32),
            pltpu.VMEM((CHUNKS, MOMENTS * CX, LANES), F32),
            pltpu.VMEM((ROWS, CX * CELLS), jnp.bfloat16),
            pltpu.VMEM((2 * MOMENTS, CX * CELLS), jnp.bfloat16),
            pltpu.VMEM((8, LANES), F32),
            pltpu.VMEM((TOTAL, LANES), F32),
            pltpu.VMEM((TOTAL, LANES), F32),
            pltpu.VMEM((8, LANES), F32),
            pltpu.VMEM((8, LANES), F32),
            dma((7,)),
            dma((1,)),
            dma((1,)),
        ],
        compiler_params=pltpu.CompilerParams(
            collective_id=0, has_side_effects=True, vmem_limit_bytes=60 * 1024 * 1024
        ),
    )(
        populations, cover_codes, sphere_cell, sphere_velocity, sphere_spin, relax_rates,
        jnp.asarray(coefficient_rows()),
    )
    out, load = pl.pallas_call(
        finish,
        out_shape=(jax.ShapeDtypeStruct((19, CX, CELLS), F32), jax.ShapeDtypeStruct((4, 6), F32)),
        in_specs=[vmem] * 4,
        out_specs=(anywhere, anywhere),
        scratch_shapes=[pltpu.VMEM((19, CX, CELLS), F32), dma((20,))],
        compiler_params=pltpu.CompilerParams(vmem_limit_bytes=8 * 1024 * 1024),
    )(*[pltpu.with_memory_space_constraint(v, pltpu.VMEM) for v in (post, halo, corner, load)])
    return out, load.T.reshape(6, 1, 1, 4)


def solution(mesh):
    placed = (
        P(None, "bx", "by"),
        P(None, "bx", "by"),
        P(None, "bx", "by", None),
        P(None, "bx", "by", None),
        P(None, "bx", "by", None),
        P(),
    )
    return jax.shard_map(
        per_device,
        mesh=mesh,
        in_specs=placed,
        out_specs=(P(None, "bx", "by"), P(None, "bx", "by", None)),
        check_vma=False,
    )
```
